32 devices in a mesh: grp: 2 (over x), slab: 16 (over z, y, core).
Axes of the slice: x: 2, y: 2, z: 4, core: 2. Of those that a mesh axis runs over, the one named last changes fastest.
Arguments:
- nodes: bfloat16 [2, 4096, 128], P('grp', 'slab'), may hold values from -6 to 6
- leave_list: int32 [2, 1024], P('grp', 'slab'), may hold values from 0 to 255, as said below
- arrive_list: int32 [2, 4096], P('grp', 'slab'), may hold values from 0 to 319, as said below
- send_list: int32 [2, 2048], P('grp', 'slab'), may hold values from 0 to 255
- neighbours: int32 [2, 4096, 32], P('grp', 'slab'), may hold values from 0 to 383
- valid: int32 [2, 4096, 32], P('grp', 'slab'), may hold values 0 or 1
- w_send: bfloat16 [128, 128], replicated, may hold values from -0.5 to 0.5
- w_recv: bfloat16 [128, 128], replicated, may hold values from -0.5 to 0.5
- w_msg: bfloat16 [128, 128], replicated, may hold values from -0.5 to 0.5
- w_self: bfloat16 [128, 128], replicated, may hold values from -0.5 to 0.5
- w_agg: bfloat16 [128, 128], replicated, may hold values from -0.09375 to 0.09375
- w_out: bfloat16 [128, 128], replicated, may hold values from -0.5 to 0.5
- cotangent: bfloat16 [2, 4096, 128], P('grp', 'slab'), may hold values from -6 to 6
Outputs:
- updated: bfloat16 [2, 4096, 128], P('grp', 'slab')
- grad_nodes: bfloat16 [2, 4096, 128], P('grp', 'slab')
- weight_steps: float32 [6, 128, 128], replicated
The draws below stay inside these ranges and needn't reach their ends.
Inputs may be any that keep to these rules, and one draw needn't show every extreme that they name: `leave_list`: each slab's 2 * 32 entries are distinct rows of that slab. `arrive_list`: each slab's 256 entries are distinct; they name every incoming row (entries 256 and above) and every own row not in that slab's leave_list, and nothing else.
All inputs are finite; a program needn't handle non-finite values. No bound on the sum of `valid` on one device may be relied on, other than what follows from the above.
Results may differ from the reference program's by a relative error of at most 0.0065.
Values may be sent and summed in bfloat16 or wider, within the bound.
No kernel may reach another device: no remote copies, remote signals or barrier semaphores. Data moves between devices by JAX's collectives and lax.ppermute only.
A program may use at most 64 MiB of HBM per device.

```python
import jax
import jax.numpy as jnp
from jax import lax

H = 128
K = 32
P_DEV = 256
HALO = 64
MIGR = 32
ROWS = 4096
N_GRP = 2
N_SLAB = 16


def migration_lists(key):
    count = N_GRP * N_SLAB
    keys = jax.random.split(key, count)

    def single(subkey):
        first_key, second_key = jax.random.split(subkey)
        perm = jax.random.permutation(first_key, P_DEV).astype(jnp.int32)
        leaving = perm[:2 * MIGR]
        staying = perm[2 * MIGR:]
        incoming = P_DEV + jnp.arange(2 * MIGR, dtype=jnp.int32)
        arriving = jax.random.permutation(second_key, jnp.concatenate([staying, incoming])).astype(jnp.int32)
        return (leaving, arriving)
    leaving, arriving = jax.vmap(single)(keys)
    return (leaving.reshape(N_GRP, N_SLAB * 2 * MIGR), arriving.reshape(N_GRP, N_SLAB * P_DEV))


def draw_leave_list(key, part):
    leaving, arriving = migration_lists(key)
    return leaving


def draw_arrive_list(key, part):
    leaving, arriving = migration_lists(key)
    return arriving


def touch_ends(result, key, smallest, top_value):
    place = [jax.random.randint(jax.random.fold_in(key, axis), (), 0, length) for axis, length in enumerate(result.shape)]
    longest = result.shape.index(max(result.shape))
    neighbour = place[:longest] + [(place[longest] + 1) % result.shape[longest]] + place[longest + 1:]
    return result.at[tuple(place)].set(smallest).at[tuple(neighbour)].set(top_value)


def block_scale(key, shape, cuts, smallest, largest):
    gain, own = 1.0, jax.random.fold_in(key, 6)
    for position, blocks in cuts:
        draws = jnp.exp(jax.random.uniform(jax.random.fold_in(own, position), (blocks,), jnp.float32, smallest / len(cuts), largest / len(cuts)))
        gain = gain * jnp.repeat(draws, shape[position] // blocks).reshape([-1 if axis == position else 1 for axis in range(len(shape))])
    return gain


def centred(rng, shape, spread, most, shards=(), kind=jnp.bfloat16):
    array = jax.random.normal(rng, shape, jnp.float32) * spread
    if len(shards) > 0:
        array = block_scale(rng, shape, shards, -0.22, 0.18) * array
    return jnp.clip(array, min=-most, max=most).astype(kind)


def setup_inputs(seed: int = 0) -> dict:
    key_list = jax.random.split(jax.random.key(seed), 14)
    nodes = centred(key_list[0], (N_GRP, ROWS, H), 1.0, 6.0, ((0, 2), (1, 16)))
    leave_list = draw_leave_list(jax.random.fold_in(key_list[13], 71), 0)
    arrive_list = draw_arrive_list(jax.random.fold_in(key_list[13], 71), 0)
    send_list = touch_ends(jax.random.randint(key_list[3], (N_GRP, N_SLAB * 2 * HALO), 0, P_DEV), jax.random.fold_in(key_list[3], 1), 0, P_DEV - 1).astype(jnp.int32)
    neighbours = touch_ends(jax.random.randint(key_list[4], (N_GRP, ROWS, K), 0, P_DEV + 2 * HALO), jax.random.fold_in(key_list[4], 1), 0, (P_DEV + 2 * HALO) - 1).astype(jnp.int32)
    valid = touch_ends((jax.random.randint(key_list[5], (N_GRP, ROWS, K), 0, 4) < 3).astype(jnp.int32), jax.random.fold_in(key_list[5], 1), 0, 1)
    w_send = centred(key_list[6], (H, H), H ** -0.5, 0.5)
    w_recv = centred(key_list[7], (H, H), H ** -0.5, 0.5)
    w_msg = centred(key_list[8], (H, H), H ** -0.5, 0.5)
    w_self = centred(key_list[9], (H, H), H ** -0.5, 0.5)
    w_agg = centred(key_list[10], (H, H), (K * H) ** -0.5, 0.09375)
    w_out = centred(key_list[11], (H, H), H ** -0.5, 0.5)
    cotangent = centred(key_list[12], (N_GRP, ROWS, H), 1.0, 6.0, ((0, 2), (1, 16)))
    return dict(nodes=nodes, leave_list=leave_list, arrive_list=arrive_list, send_list=send_list, neighbours=neighbours, valid=valid, w_send=w_send, w_recv=w_recv, w_msg=w_msg, w_self=w_self, w_agg=w_agg, w_out=w_out, cotangent=cotangent)


def dsilu(value):
    sig = jax.nn.sigmoid(value)
    return sig * (1.0 + value * (1.0 - sig))

def inner(left, right):
    return lax.dot_general(left, right, (((0,), (0,)), ((), ())), preferred_element_type=jnp.float32)

def by_transpose(left, right):
    return lax.dot_general(left, right, (((1,), (1,)), ((), ())), preferred_element_type=jnp.float32)

def device_pass(moved, table, nbr, mask, cot, w_send, w_recv, w_msg, w_self, w_agg, w_out):
    rows = moved.shape[0]
    width = moved.shape[1]
    slots = nbr.shape[1]
    centre = jnp.dot(moved, w_send, preferred_element_type=jnp.float32)
    neigh = jnp.dot(table, w_recv, preferred_element_type=jnp.float32).astype(jnp.bfloat16)
    gathered = jnp.take(neigh, nbr.reshape(-1), axis=0).reshape(rows, slots, width)
    pre = centre[:, None, :] + gathered.astype(jnp.float32)
    hid = jax.nn.silu(pre).astype(jnp.bfloat16).reshape(-1, width)
    pre2 = jnp.dot(hid, w_msg, preferred_element_type=jnp.float32).reshape(rows, slots, width)
    maskf = mask.astype(jnp.float32)[:, :, None]
    agg = lax.optimization_barrier(jnp.sum(maskf * jax.nn.silu(pre2), axis=1))
    agg_b = agg.astype(jnp.bfloat16)
    node_pre = jnp.dot(moved, w_self, preferred_element_type=jnp.float32) + jnp.dot(agg_b, w_agg, preferred_element_type=jnp.float32)
    node_hid = jax.nn.silu(node_pre).astype(jnp.bfloat16)
    updated = (moved.astype(jnp.float32) + jnp.dot(node_hid, w_out, preferred_element_type=jnp.float32)).astype(jnp.bfloat16)
    g_out = inner(node_hid, cot)
    d_node_pre = (by_transpose(cot, w_out) * dsilu(node_pre)).astype(jnp.bfloat16)
    g_self = inner(moved, d_node_pre)
    g_agg = inner(agg_b, d_node_pre)
    d_agg = by_transpose(d_node_pre, w_agg)
    d_pre2 = (maskf * d_agg[:, None, :] * dsilu(pre2)).astype(jnp.bfloat16).reshape(-1, width)
    g_msg = inner(hid, d_pre2)
    d_pre = by_transpose(d_pre2, w_msg).reshape(rows, slots, width) * dsilu(pre)
    d_centre = lax.optimization_barrier(jnp.sum(d_pre, axis=1)).astype(jnp.bfloat16)
    d_neigh = jax.ops.segment_sum(d_pre.reshape(-1, width), nbr.reshape(-1), num_segments=table.shape[0]).astype(jnp.bfloat16)
    g_recv = inner(table, d_neigh)
    g_send = inner(moved, d_centre)
    d_table = by_transpose(d_neigh, w_recv)
    d_local = cot.astype(jnp.float32) + by_transpose(d_node_pre, w_self) + by_transpose(d_centre, w_send) + d_table[:rows]
    grads = jnp.stack([g_send, g_recv, g_msg, g_self, g_agg, g_out])
    return (updated, d_local, d_table[rows:], grads)

def reference(nodes, leave_list, arrive_list, send_list, neighbours, valid, w_send, w_recv, w_msg, w_self, w_agg, w_out, cotangent):
    groups = N_GRP
    slabs = N_SLAB
    take = jax.vmap(jax.vmap(lambda rows, index: jnp.take(rows, index, axis=0)))
    plain = nodes.reshape(groups, slabs, P_DEV, H)
    leave = leave_list.reshape(groups, slabs, 2 * MIGR)
    down = take(plain, leave[:, :, :MIGR])
    upward = take(plain, leave[:, :, MIGR:])
    pool = jnp.concatenate([plain, jnp.roll(upward, 1, axis=1), jnp.roll(down, -1, axis=1)], axis=2)
    moved = take(pool, arrive_list.reshape(groups, slabs, P_DEV))
    sends = send_list.reshape(groups, slabs, 2 * HALO)
    lower_rows = take(moved, sends[:, :, :HALO])
    upper_rows = take(moved, sends[:, :, HALO:])
    table = jnp.concatenate([moved, jnp.roll(upper_rows, 1, axis=1), jnp.roll(lower_rows, -1, axis=1)], axis=2)
    count = groups * slabs
    items = (moved.reshape(count, P_DEV, H), table.reshape(count, P_DEV + 2 * HALO, H), neighbours.reshape(count, P_DEV, K), valid.reshape(count, P_DEV, K), cotangent.reshape(count, P_DEV, H))

    def step(total, item):
        updated, d_local, d_halo, grads = device_pass(item[0], item[1], item[2], item[3], item[4], w_send, w_recv, w_msg, w_self, w_agg, w_out)
        return (total + grads, (updated, d_local, d_halo))
    total, outs = lax.scan(step, jnp.zeros((6, H, H), jnp.float32), items)
    updated = outs[0].reshape(groups, slabs * P_DEV, H)
    d_local = outs[1].reshape(groups, slabs, P_DEV, H)
    d_halo = outs[2].reshape(groups, slabs, 2 * HALO, H)
    back_lower = jnp.roll(d_halo[:, :, HALO:], 1, axis=1)
    back_upper = jnp.roll(d_halo[:, :, :HALO], -1, axis=1)
    add_rows = jax.vmap(jax.vmap(lambda field, index, extra: field.at[index].add(extra)))
    d_local = add_rows(d_local, sends[:, :, :HALO], back_lower)
    d_local = add_rows(d_local, sends[:, :, HALO:], back_upper)
    grad_nodes = d_local.reshape(groups, slabs * P_DEV, H).astype(jnp.bfloat16)
    weight_steps = total / jnp.sqrt(lax.optimization_barrier(jnp.mean(total * total, axis=(1, 2), keepdims=True)) + 1e-06)
    return (updated, grad_nodes, weight_steps)
```

```python
import functools

import jax
import jax.numpy as jnp
from jax import lax
from jax.experimental import pallas as pl
from jax.experimental.pallas import tpu as pltpu
from jax.sharding import PartitionSpec as P

F32 = jnp.float32
BF16 = jnp.bfloat16
CODE_ROWS = 16
LANES = 128


def nn(left, right):
    return lax.dot_general(left, right, (((1,), (0,)), ((), ())), preferred_element_type=F32)


def nt(left, right):
    return lax.dot_general(left, right, (((1,), (1,)), ((), ())), preferred_element_type=F32)


def tn(left, right):
    return lax.dot_general(left, right, (((0,), (0,)), ((), ())), preferred_element_type=F32)


def hot_columns(row, count):
    sub = lax.broadcasted_iota(jnp.int32, (count, row.shape[1]), 0)
    return jnp.where(sub == row, 1.0, 0.0).astype(BF16)


def sigmoid(value):
    return 0.5 * jnp.tanh(0.5 * value) + 0.5


def pack_kernel(nodes, leave, arrive, sends, to_up, to_down, far_up, far_down):
    rows = nodes.shape[1]
    migr = leave.shape[1] // 2
    border = sends.shape[1] // 2
    own = nodes[0]
    leaving = tn(hot_columns(leave[...], rows), own).astype(BF16)
    sub = lax.broadcasted_iota(jnp.int32, (rows, 2 * border), 0)
    column = jnp.transpose(
        jnp.broadcast_to(arrive[...].astype(F32), (2 * border, rows)), (1, 0)
    )
    source = jnp.sum(jnp.where(sub == sends[...], column, 0.0), axis=0, keepdims=True)
    source = source.astype(jnp.int32)
    held = tn(hot_columns(source, rows), own).astype(BF16)
    code = jnp.where(source >= rows, source - rows, -1).astype(F32)
    for out, far, part in ((to_down, far_down, 0), (to_up, far_up, 1)):
        out[:border] = held[part * border : (part + 1) * border]
        moving = leaving[part * migr : (part + 1) * migr]
        out[border : border + migr] = moving
        far[...] = moving
        shifted = code if part == 0 else pltpu.roll(code, border, 1)
        out[border + migr :] = jnp.broadcast_to(shifted, (CODE_ROWS, 2 * border)).astype(BF16)


def layer_kernel(
    chunk,
    nodes,
    arrive,
    nbr,
    valid,
    cotangent,
    w_send,
    w_recv,
    w_msg,
    w_self,
    w_agg,
    w_out,
    my_up,
    my_down,
    low,
    high,
    low_far,
    high_far,
    updated,
    d_local,
    back_low,
    back_high,
    grads,
    nbr_s,
    valid_s,
    nbr_t,
    hid_s,
    ds1_s,
    ds2_s,
    agg_s,
    dcen_s,
    dneigh_s,
    gmsg_s,
):
    rows, width = nodes.shape[1:]
    slots = nbr.shape[2]
    migr = low_far.shape[0]
    border = low.shape[0] - migr - CODE_ROWS
    table_rows = rows + 2 * border

    pool = jnp.concatenate(
        [nodes[0], low[border : border + migr], high[border : border + migr]], axis=0
    )
    moved = tn(hot_columns(arrive[...], pool.shape[0]), pool).astype(BF16)

    def halo(message, first, second):
        code = message[border + migr : border + migr + 8].astype(F32)[:1]
        code = code.astype(jnp.int32)
        source = jnp.concatenate([first, second], axis=0)
        extra = tn(hot_columns(code, 2 * migr), source)
        return (message[:border].astype(F32) + extra[:border]).astype(BF16)

    below = halo(low[...], low_far[...], my_down[border : border + migr])
    above = halo(high[...], my_up[border : border + migr], high_far[...])
    table = jnp.concatenate([moved, below, above], axis=0)

    centre = nn(moved, w_send[...])
    neigh = nn(table, w_recv[...]).astype(BF16)
    msg = w_msg[...]
    nbr_s[:, :slots] = nbr[0]
    valid_s[:, :slots] = valid[0].astype(F32)
    nbr_t[...] = jnp.transpose(nbr_s[...], (1, 0))
    agg_s[...] = jnp.zeros_like(agg_s)

    lane = lax.broadcasted_iota(jnp.int32, (rows, table_rows), 1)

    @pl.loop(0, slots // chunk)
    def forward(step):
        first = step * chunk
        shift = lax.rem(LANES - first, LANES)
        near = pltpu.roll(nbr_s[...], shift, 1)
        keep = pltpu.roll(valid_s[...], shift, 1)
        hot = jnp.concatenate(
            [
                jnp.where(lane == near[:, j : j + 1], 1.0, 0.0).astype(BF16)
                for j in range(chunk)
            ],
            axis=0,
        )
        gathered = nn(hot, neigh)
        hids = []
        for j in range(chunk):
            pre = centre + gathered[j * rows : (j + 1) * rows]
            sig = sigmoid(pre)
            hid = pre * sig
            ds1_s[pl.ds((first + j) * rows, rows)] = sig + hid * (1.0 - sig)
            hids.append(hid.astype(BF16))
        hid = jnp.concatenate(hids, axis=0)
        hid_s[pl.ds(first * rows, chunk * rows)] = hid
        pre2s = nn(hid, msg)
        total = agg_s[...]
        for j in range(chunk):
            pre2 = pre2s[j * rows : (j + 1) * rows]
            sig = sigmoid(pre2)
            act = pre2 * sig
            mask = keep[:, j : j + 1]
            total = total + mask * act
            ds2_s[pl.ds((first + j) * rows, rows)] = mask * (sig + act * (1.0 - sig))
        agg_s[...] = total

    agg_b = agg_s[...].astype(BF16)
    node_pre = nn(moved, w_self[...]) + nn(agg_b, w_agg[...])
    sig = sigmoid(node_pre)
    act = node_pre * sig
    node_hid = act.astype(BF16)
    updated[0] = (moved.astype(F32) + nn(node_hid, w_out[...])).astype(BF16)
    cot = cotangent[0]
    d_node = (nt(cot, w_out[...]) * (sig + act * (1.0 - sig))).astype(BF16)
    d_agg = nt(d_node, w_agg[...])

    dcen_s[...] = jnp.zeros_like(dcen_s)
    dneigh_s[...] = jnp.zeros_like(dneigh_s)
    gmsg_s[...] = jnp.zeros_like(gmsg_s)

    @pl.loop(0, slots // chunk)
    def backward(step):
        first = step * chunk
        span = pl.ds(first * rows, chunk * rows)
        d_pre2 = jnp.concatenate(
            [
                (d_agg * ds2_s[pl.ds((first + j) * rows, rows)]).astype(BF16)
                for j in range(chunk)
            ],
            axis=0,
        )
        gmsg_s[...] += tn(hid_s[span], d_pre2)
        d_pre = nt(d_pre2, msg) * ds1_s[span]
        total = dcen_s[...]
        for j in range(chunk):
            total = total + d_pre[j * rows : (j + 1) * rows]
        dcen_s[...] = total
        hot = jnp.concatenate(
            [hot_columns(nbr_t[pl.ds(first + j, 1)], table_rows) for j in range(chunk)], axis=1
        )
        dneigh_s[...] += nn(hot, d_pre.astype(BF16))

    d_centre = dcen_s[...].astype(BF16)
    d_neigh = dneigh_s[...].astype(BF16)
    d_table = nt(d_neigh, w_recv[...])
    d_local[...] = (
        cot.astype(F32) + nt(d_node, w_self[...]) + nt(d_centre, w_send[...]) + d_table[:rows]
    )
    back_low[...] = d_table[rows : rows + border].astype(BF16)
    back_high[...] = d_table[rows + border :].astype(BF16)
    parts = (
        tn(moved, d_centre),
        tn(table, d_neigh),
        gmsg_s[...],
        tn(moved, d_node),
        tn(agg_b, d_node),
        tn(node_hid, cot),
    )
    for m, part in enumerate(parts):
        grads[m * width : (m + 1) * width] = part.astype(BF16)


def finish_kernel(d_local, sends, from_high, from_low, grad_nodes):
    rows = d_local.shape[0]
    returned = jnp.concatenate([from_low[...], from_high[...]], axis=0)
    extra = nn(hot_columns(sends[...], rows), returned)
    grad_nodes[0] = (d_local[...] + extra).astype(BF16)


def sum_kernel(parts, out):
    count = parts.shape[0]
    total = jnp.sum(parts[...].astype(F32), axis=0).astype(BF16)
    out[...] = jnp.broadcast_to(total[None], out.shape)


def norm_kernel(total, steps):
    count, width = steps.shape[0], steps.shape[1]
    for m in range(count):
        part = total[m * width : (m + 1) * width].astype(F32)
        mean = jnp.sum(jnp.sum(part * part, axis=0, keepdims=True), axis=1, keepdims=True)
        mean = mean / (part.shape[0] * part.shape[1])
        steps[m] = part / jnp.sqrt(mean + 1e-06)


def call(kernel, outs, scratch=(), limit=48):
    return pl.pallas_call(
        kernel,
        out_shape=[jax.ShapeDtypeStruct(shape, kind) for shape, kind in outs],
        scratch_shapes=scratch,
        compiler_params=pltpu.CompilerParams(vmem_limit_bytes=limit * 1024 * 1024),
    )


def shards(
    nodes,
    leave_list,
    arrive_list,
    send_list,
    neighbours,
    valid,
    w_send,
    w_recv,
    w_msg,
    w_self,
    w_agg,
    w_out,
    cotangent,
):
    rows, width = nodes.shape[1:]
    slots = neighbours.shape[2]
    migr = leave_list.shape[1] // 2
    border = send_list.shape[1] // 2
    table_rows = rows + 2 * border
    size = lax.axis_size("slab")
    devices = size * lax.axis_size("grp")

    def shift(array, by):
        return lax.ppermute(array, "slab", [(i, (i + by) % size) for i in range(size)])

    message = (border + migr + CODE_ROWS, width)
    to_up, to_down, far_up, far_down = call(
        pack_kernel,
        [(message, BF16), (message, BF16), ((migr, width), BF16), ((migr, width), BF16)],
    )(nodes, leave_list, arrive_list, send_list)
    low, high = shift(to_up, 1), shift(to_down, -1)
    low_far, high_far = shift(far_up, 2), shift(far_down, -2)

    matrices = 6
    edges = rows * slots
    share = -(-matrices * width // (8 * devices)) * 8
    chunk = 4
    updated, d_local, back_low, back_high, grads = call(
        functools.partial(layer_kernel, chunk),
        [
            ((1, rows, width), BF16),
            ((rows, width), F32),
            ((border, width), BF16),
            ((border, width), BF16),
            ((matrices * width, width), BF16),
        ],
        [
            pltpu.VMEM((rows, LANES), jnp.int32),
            pltpu.VMEM((rows, LANES), F32),
            pltpu.VMEM((LANES, rows), jnp.int32),
            pltpu.VMEM((edges, width), BF16),
            pltpu.VMEM((edges, width), F32),
            pltpu.VMEM((edges, width), F32),
            pltpu.VMEM((rows, width), F32),
            pltpu.VMEM((rows, width), F32),
            pltpu.VMEM((table_rows, width), F32),
            pltpu.VMEM((width, width), F32),
        ],
    )(
        nodes,
        arrive_list,
        neighbours,
        valid,
        cotangent,
        w_send,
        w_recv,
        w_msg,
        w_self,
        w_agg,
        w_out,
        to_up,
        to_down,
        low,
        high,
        low_far,
        high_far,
    )
    from_high = shift(back_low, -1)
    from_low = shift(back_high, 1)
    (grad_nodes,) = call(finish_kernel, [((1, rows, width), BF16)])(
        d_local, send_list, from_high, from_low
    )

    if share * devices > matrices * width:
        grads = jnp.pad(grads, ((0, share * devices - matrices * width), (0, 0)))
    axes = ("grp", "slab")
    parts = lax.all_to_all(
        grads.reshape(devices, share, width), axes, split_axis=0, concat_axis=0, tiled=True
    )
    (shared,) = call(sum_kernel, [((devices, share, width), BF16)])(parts)
    total = lax.all_to_all(shared, axes, split_axis=0, concat_axis=0, tiled=True)
    total = total.reshape(devices * share, width)[: matrices * width]
    (weight_steps,) = call(norm_kernel, [((matrices, width, width), F32)])(total)
    return (updated, grad_nodes, weight_steps)


def solution(mesh):
    rows = P("grp", "slab", None)
    lists = P("grp", "slab")
    in_specs = (rows, lists, lists, lists, rows, rows, P(), P(), P(), P(), P(), P(), rows)
    out_specs = (rows, rows, P())
    return jax.shard_map(shards, mesh=mesh, in_specs=in_specs, out_specs=out_specs, check_vma=False)
```

```python
import functools

import jax
import jax.numpy as jnp
from jax import lax
from jax.experimental import pallas as pl
from jax.experimental.pallas import tpu as pltpu
from jax.sharding import PartitionSpec as P

F32 = jnp.float32
BF16 = jnp.bfloat16
CODE_ROWS = 16
LANES = 128
SLAB = ("outer", "inner")


def nn(left, right):
    return lax.dot_general(left, right, (((1,), (0,)), ((), ())), preferred_element_type=F32)


def nt(left, right):
    return lax.dot_general(left, right, (((1,), (1,)), ((), ())), preferred_element_type=F32)


def tn(left, right):
    return lax.dot_general(left, right, (((0,), (0,)), ((), ())), preferred_element_type=F32)


def hot_columns(row, count):
    sub = lax.broadcasted_iota(jnp.int32, (count, row.shape[1]), 0)
    return jnp.where(sub == row, 1.0, 0.0).astype(BF16)


def sigmoid(value):
    return 0.5 * jnp.tanh(0.5 * value) + 0.5


def pack_kernel(
    nodes_h, leave_h, arrive_h, sends_h, to_up, far_up, to_down, far_down,
    nodes, leave, arrive, sends, done,
):
    copies = [
        pltpu.make_async_copy(source, target, done.at[n])
        for n, (source, target) in enumerate(
            ((leave_h, leave), (arrive_h, arrive), (sends_h, sends), (nodes_h, nodes))
        )
    ]
    for copy in copies:
        copy.start()
    for copy in copies:
        copy.wait()
    rows = nodes.shape[1]
    migr = leave.shape[1] // 2
    border = sends.shape[1] // 2
    own = nodes[0]
    leaving = tn(hot_columns(leave[...], rows), own).astype(BF16)
    sub = lax.broadcasted_iota(jnp.int32, (rows, 2 * border), 0)
    column = jnp.transpose(
        jnp.broadcast_to(arrive[...].astype(F32), (2 * border, rows)), (1, 0)
    )
    source = jnp.sum(jnp.where(sub == sends[...], column, 0.0), axis=0, keepdims=True)
    source = source.astype(jnp.int32)
    held = tn(hot_columns(source, rows), own).astype(BF16)
    code = jnp.where(source >= rows, source - rows, -1).astype(F32)
    for out, far, part in ((to_down, far_down, 0), (to_up, far_up, 1)):
        out[:border] = held[part * border : (part + 1) * border]
        moving = leaving[part * migr : (part + 1) * migr]
        out[border : border + migr] = moving
        far[:migr] = moving
        far[migr:] = jnp.zeros_like(far[migr:])
        shifted = code if part == 0 else pltpu.roll(code, border, 1)
        tail = out.shape[0] - border - migr
        out[border + migr :] = jnp.broadcast_to(shifted, (tail, 2 * border)).astype(BF16)


def layer_kernel(
    chunk,
    nodes,
    arrive,
    nbr,
    valid,
    cotangent,
    w_send,
    w_recv,
    w_msg,
    w_self,
    w_agg,
    w_out,
    my_up,
    my_down,
    low,
    low_far,
    high,
    high_far,
    updated,
    d_local,
    back_low,
    back_high,
    grads,
    nbr_s,
    valid_s,
    hid_s,
    ds1_s,
    ds2_s,
    agg_s,
    dcen_s,
    dneigh_s,
    gmsg_s,
):
    rows, width = nodes.shape[1:]
    slots = nbr.shape[1]
    border = back_low.shape[0]
    migr = high.shape[0] - border - CODE_ROWS
    table_rows = rows + 2 * border

    pool = jnp.concatenate(
        [nodes[0], low[border : border + migr], high[border : border + migr]], axis=0
    )
    moved = tn(hot_columns(arrive[...], pool.shape[0]), pool).astype(BF16)

    def halo(message, first, second):
        code = message[border + migr : border + migr + 8].astype(F32)[:1]
        code = code.astype(jnp.int32)
        source = jnp.concatenate([first, second], axis=0)
        extra = tn(hot_columns(code, 2 * migr), source)
        return (message[:border].astype(F32) + extra[:border]).astype(BF16)

    below = halo(low[...], low_far[:migr], my_down[border : border + migr])
    above = halo(high[...], my_up[border : border + migr], high_far[:migr])
    table = jnp.concatenate([moved, below, above], axis=0)

    centre = nn(moved, w_send[...])
    neigh = nn(table, w_recv[...]).astype(BF16)
    msg = w_msg[...]
    fill = jnp.zeros((LANES - slots, rows), jnp.int32)
    nbr_s[...] = jnp.transpose(jnp.concatenate([nbr[0], fill], axis=0), (1, 0))
    valid_s[...] = jnp.transpose(jnp.concatenate([valid[0], fill], axis=0), (1, 0)).astype(F32)
    agg_s[...] = jnp.zeros_like(agg_s)

    lane = lax.broadcasted_iota(jnp.int32, (rows, table_rows), 1)

    @pl.loop(0, slots // chunk)
    def forward(step):
        first = step * chunk
        shift = lax.rem(LANES - first, LANES)
        near = pltpu.roll(nbr_s[...], shift, 1)
        keep = pltpu.roll(valid_s[...], shift, 1)
        hot = jnp.concatenate(
            [
                jnp.where(lane == near[:, j : j + 1], 1.0, 0.0).astype(BF16)
                for j in range(chunk)
            ],
            axis=0,
        )
        gathered = nn(hot, neigh)
        hids = []
        for j in range(chunk):
            pre = centre + gathered[j * rows : (j + 1) * rows]
            sig = sigmoid(pre)
            hid = pre * sig
            ds1_s[pl.ds((first + j) * rows, rows)] = sig + hid * (1.0 - sig)
            hids.append(hid.astype(BF16))
        hid = jnp.concatenate(hids, axis=0)
        hid_s[pl.ds(first * rows, chunk * rows)] = hid
        pre2s = nn(hid, msg)
        total = agg_s[...]
        for j in range(chunk):
            pre2 = pre2s[j * rows : (j + 1) * rows]
            sig = sigmoid(pre2)
            act = pre2 * sig
            mask = keep[:, j : j + 1]
            total = total + mask * act
            ds2_s[pl.ds((first + j) * rows, rows)] = mask * (sig + act * (1.0 - sig))
        agg_s[...] = total

    agg_b = agg_s[...].astype(BF16)
    node_pre = nn(moved, w_self[...]) + nn(agg_b, w_agg[...])
    sig = sigmoid(node_pre)
    act = node_pre * sig
    node_hid = act.astype(BF16)
    updated[0] = (moved.astype(F32) + nn(node_hid, w_out[...])).astype(BF16)
    cot = cotangent[0]
    d_node = (nt(cot, w_out[...]) * (sig + act * (1.0 - sig))).astype(BF16)
    d_agg = nt(d_node, w_agg[...])

    dcen_s[...] = jnp.zeros_like(dcen_s)
    dneigh_s[...] = jnp.zeros_like(dneigh_s)
    gmsg_s[...] = jnp.zeros_like(gmsg_s)

    @pl.loop(0, slots // chunk)
    def backward(step):
        first = step * chunk
        span = pl.ds(first * rows, chunk * rows)
        d_pre2 = jnp.concatenate(
            [
                (d_agg * ds2_s[pl.ds((first + j) * rows, rows)]).astype(BF16)
                for j in range(chunk)
            ],
            axis=0,
        )
        gmsg_s[...] += tn(hid_s[span], d_pre2)
        d_pre = nt(d_pre2, msg) * ds1_s[span]
        total = dcen_s[...]
        for j in range(chunk):
            total = total + d_pre[j * rows : (j + 1) * rows]
        dcen_s[...] = total
        hot = jnp.concatenate(
            [hot_columns(nbr[0, pl.ds(first + j, 1)], table_rows) for j in range(chunk)], axis=1
        )
        dneigh_s[...] += nn(hot, d_pre.astype(BF16))

    d_centre = dcen_s[...].astype(BF16)
    d_neigh = dneigh_s[...].astype(BF16)
    d_table = nt(d_neigh, w_recv[...])
    d_local[...] = (
        cot.astype(F32) + nt(d_node, w_self[...]) + nt(d_centre, w_send[...]) + d_table[:rows]
    )
    back_low[...] = d_table[rows : rows + border].astype(BF16)
    back_high[...] = d_table[rows + border :].astype(BF16)
    parts = (
        tn(moved, d_centre),
        tn(table, d_neigh),
        gmsg_s[...],
        tn(moved, d_node),
        tn(agg_b, d_node),
        tn(node_hid, cot),
    )
    for m, part in enumerate(parts):
        grads[m * width : (m + 1) * width] = part.astype(BF16)


def finish_kernel(d_local, sends, from_high, from_low, grad_nodes):
    rows = d_local.shape[0]
    returned = jnp.concatenate([from_low[...], from_high[...]], axis=0)
    extra = nn(hot_columns(sends[...], rows), returned)
    grad_nodes[0] = (d_local[...] + extra).astype(BF16)


def sum_kernel(parts, out):
    count = parts.shape[0]
    total = jnp.sum(parts[...].astype(F32), axis=0).astype(BF16)
    out[...] = jnp.broadcast_to(total[None], out.shape)


def norm_kernel(total, steps):
    count, width = steps.shape[0], steps.shape[1]
    for m in range(count):
        part = total[m * width : (m + 1) * width].astype(F32)
        mean = jnp.sum(jnp.sum(part * part, axis=0, keepdims=True), axis=1, keepdims=True)
        mean = mean / (part.shape[0] * part.shape[1])
        steps[m] = part / jnp.sqrt(mean + 1e-06)


def call(kernel, outs, scratch=(), limit=48, space=None):
    specs = {} if space is None else {"in_specs": [pl.BlockSpec(memory_space=pl.ANY)] * space}
    return pl.pallas_call(
        kernel,
        **specs,
        out_shape=[jax.ShapeDtypeStruct(shape, kind) for shape, kind in outs],
        scratch_shapes=scratch,
        compiler_params=pltpu.CompilerParams(vmem_limit_bytes=limit * 1024 * 1024),
    )


def shards(
    nodes,
    leave_list,
    arrive_list,
    send_list,
    neighbours,
    valid,
    w_send,
    w_recv,
    w_msg,
    w_self,
    w_agg,
    w_out,
    cotangent,
):
    rows, width = nodes.shape[1:]
    slots = neighbours.shape[2]
    migr = leave_list.shape[1] // 2
    border = send_list.shape[1] // 2
    table_rows = rows + 2 * border
    size = lax.axis_size(SLAB)

    def shift(array, by):
        return lax.ppermute(array, SLAB, [(i, (i + by) % size) for i in range(size)])

    message = (border + migr + CODE_ROWS, width)
    message_up = (border + migr + 2 * CODE_ROWS, width)
    to_up, far_up, to_down, far_down = call(
        pack_kernel,
        [(message_up, BF16)] * 2 + [(message, BF16)] * 2,
        [pltpu.VMEM(a.shape, a.dtype) for a in (nodes, leave_list, arrive_list, send_list)]
        + [pltpu.SemaphoreType.DMA((4,))],
        space=4,
    )(nodes, leave_list, arrive_list, send_list)
    low, low_far = shift(to_up, 1), shift(far_up, 2)
    high, high_far = shift(to_down, -1), shift(far_down, -2)

    matrices = 6
    edges = rows * slots
    chunk = 4
    updated, d_local, back_low, back_high, grads = call(
        functools.partial(layer_kernel, chunk),
        [
            ((1, rows, width), BF16),
            ((rows, width), F32),
            ((border, width), BF16),
            ((border, width), BF16),
            ((matrices * width, width), BF16),
        ],
        [
            pltpu.VMEM((rows, LANES), jnp.int32),
            pltpu.VMEM((rows, LANES), F32),
            pltpu.VMEM((edges, width), BF16),
            pltpu.VMEM((edges, width), F32),
            pltpu.VMEM((edges, width), F32),
            pltpu.VMEM((rows, width), F32),
            pltpu.VMEM((rows, width), F32),
            pltpu.VMEM((table_rows, width), F32),
            pltpu.VMEM((width, width), F32),
        ],
    )(
        nodes,
        arrive_list,
        jnp.swapaxes(neighbours, 1, 2),
        jnp.swapaxes(valid, 1, 2),
        cotangent,
        w_send,
        w_recv,
        w_msg,
        w_self,
        w_agg,
        w_out,
        to_up,
        to_down,
        low,
        low_far,
        high,
        high_far,
    )
    from_high = shift(back_low, -1)
    from_low = shift(back_high, 1)
    (grad_nodes,) = call(finish_kernel, [((1, rows, width), BF16)])(
        d_local, send_list, from_high, from_low
    )

    plane = ("grp", "inner")
    near = lax.axis_size("grp") * lax.axis_size("inner")
    far = lax.axis_size("outer")
    share = matrices * width // near
    parts = lax.all_to_all(
        grads.reshape(near, share, width), plane, split_axis=0, concat_axis=0, tiled=True
    )
    (partial,) = call(sum_kernel, [((far, share, width), BF16)])(parts)
    parts = lax.all_to_all(partial, "outer", split_axis=0, concat_axis=0, tiled=True)
    (shared,) = call(sum_kernel, [((near, share, width), BF16)])(parts)
    total = lax.all_to_all(shared, plane, split_axis=0, concat_axis=0, tiled=True)
    total = total.reshape(matrices * width, width)
    (weight_steps,) = call(norm_kernel, [((matrices, width, width), F32)])(total)
    return (updated, grad_nodes, weight_steps)


def solution(mesh):
    inner = 4
    groups, slabs = mesh.devices.shape
    mesh = jax.sharding.Mesh(
        mesh.devices.reshape(groups, slabs // inner, inner), ("grp", "outer", "inner")
    )
    rows = P("grp", SLAB, None)
    lists = P("grp", SLAB)
    in_specs = (rows, lists, lists, lists, rows, rows, P(), P(), P(), P(), P(), P(), rows)
    out_specs = (rows, rows, P())
    return jax.shard_map(shards, mesh=mesh, in_specs=in_specs, out_specs=out_specs, check_vma=False)
```

```python
import functools

import jax
import jax.numpy as jnp
from jax import lax
from jax.experimental import pallas as pl
from jax.experimental.pallas import tpu as pltpu
from jax.sharding import PartitionSpec as P

F32 = jnp.float32
BF16 = jnp.bfloat16
CODE_ROWS = 16
LANES = 128
FAR = -1e30
PAIRS = 2


def nn(left, right):
    return lax.dot_general(left, right, (((1,), (0,)), ((), ())), preferred_element_type=F32)


def nt(left, right):
    return lax.dot_general(left, right, (((1,), (1,)), ((), ())), preferred_element_type=F32)


def tn(left, right):
    return lax.dot_general(left, right, (((0,), (0,)), ((), ())), preferred_element_type=F32)


def hot_columns(row, count):
    sub = lax.broadcasted_iota(jnp.int32, (count, row.shape[1]), 0)
    return jnp.where(sub == row, 1.0, 0.0).astype(BF16)


def silu_parts(half):
    tan = jnp.tanh(half)
    part = half * tan
    return half + part, (1.0 + tan) * ((1.0 + half) - part)


def first_kernel(out):
    out[...] = jnp.zeros_like(out)


def pack_kernel(_, nodes, leave, arrive, sends, to_up, far_up, to_down, far_down):
    rows = nodes.shape[1]
    migr = leave.shape[1] // 2
    border = sends.shape[1] // 2
    own = nodes[0]
    leaving = tn(hot_columns(leave[...], rows), own).astype(BF16)
    sub = lax.broadcasted_iota(jnp.int32, (rows, 2 * border), 0)
    column = jnp.transpose(
        jnp.broadcast_to(arrive[...].astype(F32), (2 * border, rows)), (1, 0)
    )
    source = jnp.sum(jnp.where(sub == sends[...], column, 0.0), axis=0, keepdims=True)
    source = source.astype(jnp.int32)
    rest = tn(hot_columns(source, rows), own).astype(BF16)
    code = jnp.where(source >= rows, source - rows, -1).astype(F32)
    for out, far, part in ((to_down, far_down, 0), (to_up, far_up, 1)):
        out[:border] = rest[part * border : (part + 1) * border]
        moving = leaving[part * migr : (part + 1) * migr]
        out[border : border + migr] = moving
        far[:migr] = moving
        far[migr:] = jnp.zeros_like(far[migr:])
        shifted = code if part == 0 else pltpu.roll(code, border, 1)
        tail = out.shape[0] - border - migr
        out[border + migr :] = jnp.broadcast_to(shifted, (tail, 2 * border)).astype(BF16)


def layer_kernel(
    nodes,
    arrive,
    my_up,
    my_down,
    low,
    low_far,
    high,
    high_far,
    nbr,
    valid,
    w_send,
    w_recv,
    w_msg,
    w_self,
    w_agg,
    w_out,
    cotangent,
    updated,
    back_low,
    back_high,
    grads,
    d_node_o,
    d_centre_o,
    d_neigh_o,
    nbr_s,
    neigh_s,
    wide_s,
    hid_s,
    ds1_s,
    ds2_s,
    agg_s,
    dcen_s,
    dneigh_s,
    gmsg_s,
):
    rows, width = nodes.shape[1:]
    slots = nbr.shape[1]
    border = back_low.shape[0]
    migr = high.shape[0] - border - CODE_ROWS
    table_rows = rows + 2 * border
    chunk = 2 * PAIRS
    steps = slots // chunk

    pool = jnp.concatenate(
        [nodes[0], low[border : border + migr], high[border : border + migr]], axis=0
    )
    moved = tn(hot_columns(arrive[...], pool.shape[0]), pool).astype(BF16)

    def halo(message, first, second):
        code = message[border + migr : border + migr + 8].astype(F32)[:1]
        code = code.astype(jnp.int32)
        source = jnp.concatenate([first, second], axis=0)
        extra = tn(hot_columns(code, 2 * migr), source)
        return (message[:border].astype(F32) + extra[:border]).astype(BF16)

    below = halo(low[...], low_far[:migr], my_down[border : border + migr])
    above = halo(high[...], my_up[border : border + migr], high_far[:migr])
    table = jnp.concatenate([moved, below, above], axis=0)

    half_centre = 0.5 * nn(moved, w_send[...])
    half_neigh = (0.5 * nn(table, w_recv[...]).astype(BF16).astype(F32)).astype(BF16)
    none = jnp.zeros((table_rows, width), BF16)
    neigh_s[...] = jnp.concatenate(
        [
            jnp.concatenate([half_neigh, none], axis=1),
            jnp.concatenate([none, half_neigh], axis=1),
        ],
        axis=0,
    )
    half_msg = 0.5 * w_msg[...].astype(F32)
    none = jnp.zeros((width, width), F32)
    for part, block in enumerate((half_msg, jnp.transpose(half_msg, (1, 0)))):
        wide_s[part] = jnp.concatenate(
            [
                jnp.concatenate([block, none], axis=1),
                jnp.concatenate([none, block], axis=1),
            ],
            axis=0,
        ).astype(BF16)
    index = jnp.where(valid[0] == 1, nbr[0], -1)
    fill = jnp.zeros((LANES - slots, rows), jnp.int32)
    nbr_s[...] = jnp.transpose(jnp.concatenate([index, fill], axis=0), (1, 0))
    agg_s[...] = jnp.zeros_like(agg_s)

    lane = lax.broadcasted_iota(jnp.int32, (rows, table_rows), 1).astype(jnp.int16)
    one = jnp.ones((rows, table_rows), BF16)
    zero = jnp.zeros((rows, table_rows), BF16)

    @pl.loop(0, steps)
    def forward(step):
        near = pltpu.roll(nbr_s[...], lax.rem(LANES - step * chunk, LANES), 1)
        ids = [jnp.broadcast_to(near[:, j : j + 1], (rows, LANES)) for j in range(chunk)]
        hots = []
        for j in range(chunk):
            short = ids[j].astype(jnp.int16)
            short = jnp.concatenate([short] * (table_rows // LANES), axis=1)
            hots.append(jnp.where(short == lane, one, zero))
        hot = jnp.concatenate(
            [
                jnp.concatenate([hots[2 * p], hots[2 * p + 1]], axis=1)
                for p in range(PAIRS)
            ],
            axis=0,
        )
        gathered = nn(hot, neigh_s[...])
        base = step * (PAIRS * rows)
        for p in range(PAIRS):
            for side in range(2):
                cols = slice(side * width, (side + 1) * width)
                half = half_centre + gathered[p * rows : (p + 1) * rows, cols]
                half = jnp.where(ids[2 * p + side] < 0, FAR, half)
                act, slope = silu_parts(half)
                span = pl.ds(base + p * rows, rows)
                ds1_s[span, cols] = slope
                hid_s[span, cols] = act.astype(BF16)
        halves = nn(hid_s[pl.ds(base, PAIRS * rows)], wide_s[0])
        total = agg_s[...]
        for p in range(PAIRS):
            for side in range(2):
                cols = slice(side * width, (side + 1) * width)
                act, slope = silu_parts(halves[p * rows : (p + 1) * rows, cols])
                total = total + act
                ds2_s[pl.ds(base + p * rows, rows), cols] = slope
        agg_s[...] = total

    agg_b = agg_s[...].astype(BF16)
    node_pre = nn(moved, w_self[...]) + nn(agg_b, w_agg[...])
    act, slope = silu_parts(0.5 * node_pre)
    node_hid = act.astype(BF16)
    updated[0] = (moved.astype(F32) + nn(node_hid, w_out[...])).astype(BF16)
    cot = cotangent[0]
    d_node = (nt(cot, w_out[...]) * (0.5 * slope)).astype(BF16)
    half_d_agg = 0.5 * nt(d_node, w_agg[...])

    dcen_s[...] = jnp.zeros_like(dcen_s)
    dneigh_s[...] = jnp.zeros_like(dneigh_s)
    gmsg_s[...] = jnp.zeros_like(gmsg_s)
    sub = lax.broadcasted_iota(jnp.int32, (table_rows, rows), 0).astype(jnp.int16)
    one_t = jnp.ones((table_rows, rows), BF16)
    zero_t = jnp.zeros((table_rows, rows), BF16)

    def stack(wide):
        return jnp.concatenate(
            [
                wide[p * rows : (p + 1) * rows, side * width : (side + 1) * width]
                for p in range(PAIRS)
                for side in range(2)
            ],
            axis=0,
        )

    @pl.loop(0, steps)
    def backward(step):
        span = pl.ds(step * (PAIRS * rows), PAIRS * rows)
        d_agg = jnp.concatenate([half_d_agg, half_d_agg], axis=1)
        d_agg = jnp.concatenate([d_agg] * PAIRS, axis=0)
        d_pre2 = (d_agg * ds2_s[span]).astype(BF16)
        d_pre = nn(d_pre2, wide_s[1]) * ds1_s[span]
        gmsg_s[...] += tn(stack(hid_s[span]), stack(d_pre2))
        d_pre = stack(d_pre)
        total = dcen_s[...]
        for j in range(chunk):
            total = total + d_pre[j * rows : (j + 1) * rows]
        dcen_s[...] = total
        hots = []
        for j in range(chunk):
            row = jnp.broadcast_to(nbr[0, pl.ds(step * chunk + j, 1)], (16, rows))
            short = jnp.concatenate([row.astype(jnp.int16)] * (table_rows // 16), axis=0)
            hots.append(jnp.where(short == sub, one_t, zero_t))
        dneigh_s[...] += nn(jnp.concatenate(hots, axis=1), d_pre.astype(BF16))

    d_centre = dcen_s[...].astype(BF16)
    d_neigh = dneigh_s[...].astype(BF16)
    d_borrowed = nt(d_neigh[rows:], w_recv[...]).astype(BF16)
    back_low[...] = d_borrowed[:border]
    back_high[...] = d_borrowed[border:]
    d_node_o[...] = d_node
    d_centre_o[...] = d_centre
    d_neigh_o[...] = d_neigh[:rows]
    parts = (
        tn(moved, d_centre),
        tn(table, d_neigh),
        gmsg_s[...],
        tn(moved, d_node),
        tn(agg_b, d_node),
        tn(node_hid, cot),
    )
    for m, part in enumerate(parts):
        grads[m * width : (m + 1) * width] = part.astype(BF16)
    used = len(parts) * width
    if grads.shape[0] > used:
        grads[used:] = jnp.zeros_like(grads[used:])


def finish_kernel(
    cotangent, d_node, d_centre, d_neigh, w_self, w_send, w_recv, sends, from_low, from_high, out
):
    rows = d_node.shape[0]
    returned = jnp.concatenate([from_low[...], from_high[...]], axis=0)
    out[0] = (
        cotangent[0].astype(F32)
        + nt(d_node[...], w_self[...])
        + nt(d_centre[...], w_send[...])
        + nt(d_neigh[...], w_recv[...])
        + nn(hot_columns(sends[...], rows), returned)
    ).astype(BF16)


def sum_kernel(parts, out):
    total = jnp.sum(parts[...].astype(F32), axis=0).astype(BF16)
    out[...] = jnp.broadcast_to(total[None], out.shape)


def norm_kernel(total, steps):
    count, width = steps.shape[0], steps.shape[1]
    for m in range(count):
        part = total[m * width : (m + 1) * width].astype(F32)
        mean = jnp.sum(jnp.sum(part * part, axis=0, keepdims=True), axis=1, keepdims=True)
        mean = mean / (part.shape[0] * part.shape[1])
        steps[m] = part / jnp.sqrt(mean + 1e-06)


def call(kernel, outs, scratch=()):
    return pl.pallas_call(
        kernel,
        out_shape=[jax.ShapeDtypeStruct(shape, kind) for shape, kind in outs],
        scratch_shapes=scratch,
        compiler_params=pltpu.CompilerParams(vmem_limit_bytes=40 * 1024 * 1024),
        cost_estimate=pl.CostEstimate(flops=2 * 10**9, bytes_accessed=1024, transcendentals=0),
    )


def shards(
    nodes,
    leave_list,
    arrive_list,
    send_list,
    neighbours,
    valid,
    w_send,
    w_recv,
    w_msg,
    w_self,
    w_agg,
    w_out,
    cotangent,
):
    rows, width = nodes.shape[1:]
    slots = neighbours.shape[2]
    migr = leave_list.shape[1] // 2
    border = send_list.shape[1] // 2
    table_rows = rows + 2 * border
    size = lax.axis_size("slab")
    devices = size * lax.axis_size("grp")
    axes = ("grp", "slab")

    def shift(array, by):
        return lax.ppermute(array, "slab", [(i, (i + by) % size) for i in range(size)])

    message = (border + migr + CODE_ROWS, width)
    message_up = (message[0] + CODE_ROWS, width)
    (token,) = call(first_kernel, [((8, LANES), F32)])()
    to_up, far_up, to_down, far_down = call(
        pack_kernel,
        [(message_up, BF16)] * 2 + [(message, BF16)] * 2,
    )(token, nodes, leave_list, arrive_list, send_list)
    low, low_far = shift(to_up, 1), shift(far_up, 2)
    high, high_far = shift(to_down, -1), shift(far_down, -2)

    matrices = 6
    pair_rows = rows * slots // 2
    share = -(-matrices * width // (8 * devices)) * 8
    sources = (
        nodes,
        arrive_list,
        to_up,
        to_down,
        low,
        low_far,
        high,
        high_far,
        jnp.swapaxes(neighbours, 1, 2),
        jnp.swapaxes(valid, 1, 2),
        w_send,
        w_recv,
        w_msg,
        w_self,
        w_agg,
        w_out,
        cotangent,
    )
    updated, back_low, back_high, grads, d_node, d_centre, d_neigh = call(
        layer_kernel,
        [
            ((1, rows, width), BF16),
            ((border, width), BF16),
            ((border, width), BF16),
            ((devices * share, width), BF16),
            ((rows, width), BF16),
            ((rows, width), BF16),
            ((rows, width), BF16),
        ],
        [
            pltpu.VMEM((rows, LANES), jnp.int32),
            pltpu.VMEM((2 * table_rows, 2 * width), BF16),
            pltpu.VMEM((2, 2 * width, 2 * width), BF16),
            pltpu.VMEM((pair_rows, 2 * width), BF16),
            pltpu.VMEM((pair_rows, 2 * width), F32),
            pltpu.VMEM((pair_rows, 2 * width), F32),
            pltpu.VMEM((rows, width), F32),
            pltpu.VMEM((rows, width), F32),
            pltpu.VMEM((table_rows, width), F32),
            pltpu.VMEM((width, width), F32),
        ],
    )(*sources)
    from_low = shift(back_high, 1)
    from_high = shift(back_low, -1)
    parts = lax.all_to_all(
        grads.reshape(devices, share, width), axes, split_axis=0, concat_axis=0, tiled=True
    )
    sources = (
        cotangent,
        d_node,
        d_centre,
        d_neigh,
        w_self,
        w_send,
        w_recv,
        send_list,
        from_low,
        from_high,
    )
    (grad_nodes,) = call(
        finish_kernel,
        [((1, rows, width), BF16)],
    )(*sources)
    (shared,) = call(sum_kernel, [((devices, share, width), BF16)])(parts)
    total = lax.all_to_all(shared, axes, split_axis=0, concat_axis=0, tiled=True)
    total = total.reshape(devices * share, width)[: matrices * width]
    (weight_steps,) = call(norm_kernel, [((matrices, width, width), F32)])(total)
    return (updated, grad_nodes, weight_steps)


def solution(mesh):
    rows = P("grp", "slab", None)
    lists = P("grp", "slab")
    in_specs = (rows, lists, lists, lists, rows, rows, P(), P(), P(), P(), P(), P(), rows)
    out_specs = (rows, rows, P())
    return jax.shard_map(shards, mesh=mesh, in_specs=in_specs, out_specs=out_specs, check_vma=False)
```

```python
import functools

import jax
import jax.numpy as jnp
from jax import lax
from jax.experimental import pallas as pl
from jax.experimental.pallas import tpu as pltpu
from jax.sharding import PartitionSpec as P

F32 = jnp.float32
BF16 = jnp.bfloat16
CODE_ROWS = 16
LANES = 128
FAR = -1e30
PAIRS = 4


def nn(left, right):
    return lax.dot_general(left, right, (((1,), (0,)), ((), ())), preferred_element_type=F32)


def nt(left, right):
    return lax.dot_general(left, right, (((1,), (1,)), ((), ())), preferred_element_type=F32)


def tn(left, right):
    return lax.dot_general(left, right, (((0,), (0,)), ((), ())), preferred_element_type=F32)


def hot_columns(row, count):
    sub = lax.broadcasted_iota(jnp.int32, (count, row.shape[1]), 0)
    return jnp.where(sub == row, 1.0, 0.0).astype(BF16)


def silu_parts(half):
    tan = jnp.tanh(half)
    part = half * tan
    return half + part, (1.0 + tan) * ((1.0 + half) - part)


def first_kernel(out):
    out[...] = jnp.zeros_like(out)


def pack_kernel(_, nodes, leave, arrive, sends, to_up, far_up, to_down, far_down):
    rows = nodes.shape[1]
    migr = leave.shape[1] // 2
    border = sends.shape[1] // 2
    own = nodes[0]
    leaving = tn(hot_columns(leave[...], rows), own).astype(BF16)
    sub = lax.broadcasted_iota(jnp.int32, (rows, 2 * border), 0)
    column = jnp.transpose(
        jnp.broadcast_to(arrive[...].astype(F32), (2 * border, rows)), (1, 0)
    )
    source = jnp.sum(jnp.where(sub == sends[...], column, 0.0), axis=0, keepdims=True)
    source = source.astype(jnp.int32)
    rest = tn(hot_columns(source, rows), own).astype(BF16)
    code = jnp.where(source >= rows, source - rows, -1).astype(F32)
    for out, far, part in ((to_down, far_down, 0), (to_up, far_up, 1)):
        out[:border] = rest[part * border : (part + 1) * border]
        moving = leaving[part * migr : (part + 1) * migr]
        out[border : border + migr] = moving
        far[:migr] = moving
        far[migr:] = jnp.zeros_like(far[migr:])
        shifted = code if part == 0 else pltpu.roll(code, border, 1)
        tail = out.shape[0] - border - migr
        out[border + migr :] = jnp.broadcast_to(shifted, (tail, 2 * border)).astype(BF16)


def layer_kernel(
    nodes,
    arrive,
    my_up,
    my_down,
    low,
    low_far,
    high,
    high_far,
    nbr,
    valid,
    w_send,
    w_recv,
    w_msg,
    w_self,
    w_agg,
    w_out,
    cotangent,
    updated,
    back_low,
    back_high,
    grads,
    d_node_o,
    d_centre_o,
    d_neigh_o,
    nbr_s,
    neigh_s,
    wide_s,
    hid_s,
    ds1_s,
    ds2_s,
    agg_s,
    dcen_s,
    dneigh_s,
    gmsg_s,
):
    rows, width = nodes.shape[1:]
    slots = nbr.shape[1]
    border = back_low.shape[0]
    migr = high.shape[0] - border - CODE_ROWS
    table_rows = rows + 2 * border
    chunk = 2 * PAIRS
    steps = slots // chunk

    pool = jnp.concatenate(
        [nodes[0], low[border : border + migr], high[border : border + migr]], axis=0
    )
    moved = tn(hot_columns(arrive[...], pool.shape[0]), pool).astype(BF16)

    def halo(message, first, second):
        code = message[border + migr : border + migr + 8].astype(F32)[:1]
        code = code.astype(jnp.int32)
        source = jnp.concatenate([first, second], axis=0)
        extra = tn(hot_columns(code, 2 * migr), source)
        return (message[:border].astype(F32) + extra[:border]).astype(BF16)

    below = halo(low[...], low_far[:migr], my_down[border : border + migr])
    above = halo(high[...], my_up[border : border + migr], high_far[:migr])
    table = jnp.concatenate([moved, below, above], axis=0)

    half_centre = 0.5 * nn(moved, w_send[...])
    half_neigh = (0.5 * nn(table, w_recv[...]).astype(BF16).astype(F32)).astype(BF16)
    none = jnp.zeros((table_rows, width), BF16)
    neigh_s[...] = jnp.concatenate(
        [
            jnp.concatenate([half_neigh, none], axis=1),
            jnp.concatenate([none, half_neigh], axis=1),
        ],
        axis=0,
    )
    half_msg = 0.5 * w_msg[...].astype(F32)
    none = jnp.zeros((width, width), F32)
    for part, block in enumerate((half_msg, jnp.transpose(half_msg, (1, 0)))):
        wide_s[part] = jnp.concatenate(
            [
                jnp.concatenate([block, none], axis=1),
                jnp.concatenate([none, block], axis=1),
            ],
            axis=0,
        ).astype(BF16)
    index = jnp.where(valid[0] == 1, nbr[0], -1)
    fill = jnp.zeros((LANES - slots, rows), jnp.int32)
    nbr_s[...] = jnp.transpose(jnp.concatenate([index, fill], axis=0), (1, 0))
    agg_s[...] = jnp.zeros_like(agg_s)

    lane = lax.broadcasted_iota(jnp.int32, (rows, table_rows), 1).astype(jnp.int16)
    one = jnp.ones((rows, table_rows), BF16)
    zero = jnp.zeros((rows, table_rows), BF16)

    @pl.loop(0, steps)
    def forward(step):
        near = pltpu.roll(nbr_s[...], lax.rem(LANES - step * chunk, LANES), 1)
        ids = [jnp.broadcast_to(near[:, j : j + 1], (rows, LANES)) for j in range(chunk)]
        hots = []
        for j in range(chunk):
            short = ids[j].astype(jnp.int16)
            short = jnp.concatenate([short] * (table_rows // LANES), axis=1)
            hots.append(jnp.where(short == lane, one, zero))
        hot = jnp.concatenate(
            [
                jnp.concatenate([hots[2 * p], hots[2 * p + 1]], axis=1)
                for p in range(PAIRS)
            ],
            axis=0,
        )
        gathered = nn(hot, neigh_s[...])
        base = step * (PAIRS * rows)
        for p in range(PAIRS):
            for side in range(2):
                cols = slice(side * width, (side + 1) * width)
                half = half_centre + gathered[p * rows : (p + 1) * rows, cols]
                half = jnp.where(ids[2 * p + side] < 0, FAR, half)
                act, slope = silu_parts(half)
                span = pl.ds(base + p * rows, rows)
                ds1_s[span, cols] = slope
                hid_s[span, cols] = act.astype(BF16)
        halves = nn(hid_s[pl.ds(base, PAIRS * rows)], wide_s[0])
        total = agg_s[...]
        for p in range(PAIRS):
            for side in range(2):
                cols = slice(side * width, (side + 1) * width)
                act, slope = silu_parts(halves[p * rows : (p + 1) * rows, cols])
                total = total + act
                ds2_s[pl.ds(base + p * rows, rows), cols] = slope
        agg_s[...] = total

    agg_b = agg_s[...].astype(BF16)
    node_pre = nn(moved, w_self[...]) + nn(agg_b, w_agg[...])
    act, slope = silu_parts(0.5 * node_pre)
    node_hid = act.astype(BF16)
    updated[0] = (moved.astype(F32) + nn(node_hid, w_out[...])).astype(BF16)
    cot = cotangent[0]
    d_node = (nt(cot, w_out[...]) * (0.5 * slope)).astype(BF16)
    half_d_agg = 0.5 * nt(d_node, w_agg[...])

    dcen_s[...] = jnp.zeros_like(dcen_s)
    dneigh_s[...] = jnp.zeros_like(dneigh_s)
    gmsg_s[...] = jnp.zeros_like(gmsg_s)
    sub = lax.broadcasted_iota(jnp.int32, (table_rows, rows), 0).astype(jnp.int16)
    one_t = jnp.ones((table_rows, rows), BF16)
    zero_t = jnp.zeros((table_rows, rows), BF16)

    def stack(wide):
        return jnp.concatenate(
            [
                wide[p * rows : (p + 1) * rows, side * width : (side + 1) * width]
                for p in range(PAIRS)
                for side in range(2)
            ],
            axis=0,
        )

    @pl.loop(0, steps)
    def backward(step):
        span = pl.ds(step * (PAIRS * rows), PAIRS * rows)
        d_agg = jnp.concatenate([half_d_agg, half_d_agg], axis=1)
        d_agg = jnp.concatenate([d_agg] * PAIRS, axis=0)
        d_pre2 = (d_agg * ds2_s[span]).astype(BF16)
        d_pre = nn(d_pre2, wide_s[1]) * ds1_s[span]
        gmsg_s[...] += tn(stack(hid_s[span]), stack(d_pre2))
        d_pre = stack(d_pre)
        total = dcen_s[...]
        for j in range(chunk):
            total = total + d_pre[j * rows : (j + 1) * rows]
        dcen_s[...] = total
        hots = []
        for j in range(chunk):
            row = jnp.broadcast_to(nbr[0, pl.ds(step * chunk + j, 1)], (16, rows))
            short = jnp.concatenate([row.astype(jnp.int16)] * (table_rows // 16), axis=0)
            hots.append(jnp.where(short == sub, one_t, zero_t))
        dneigh_s[...] += nn(jnp.concatenate(hots, axis=1), d_pre.astype(BF16))

    d_centre = dcen_s[...].astype(BF16)
    d_neigh = dneigh_s[...].astype(BF16)
    d_borrowed = nt(d_neigh[rows:], w_recv[...]).astype(BF16)
    back_low[...] = d_borrowed[:border]
    back_high[...] = d_borrowed[border:]
    d_node_o[...] = d_node
    d_centre_o[...] = d_centre
    d_neigh_o[...] = d_neigh[:rows]
    parts = (
        tn(moved, d_centre),
        tn(table, d_neigh),
        gmsg_s[...],
        tn(moved, d_node),
        tn(agg_b, d_node),
        tn(node_hid, cot),
    )
    for m, part in enumerate(parts):
        grads[m * width : (m + 1) * width] = part.astype(BF16)
    used = len(parts) * width
    if grads.shape[0] > used:
        grads[used:] = jnp.zeros_like(grads[used:])


def finish_kernel(
    cotangent, d_node, d_centre, d_neigh, w_self, w_send, w_recv, sends, from_low, from_high, out
):
    rows = d_node.shape[0]
    returned = jnp.concatenate([from_low[...], from_high[...]], axis=0)
    out[0] = (
        cotangent[0].astype(F32)
        + nt(d_node[...], w_self[...])
        + nt(d_centre[...], w_send[...])
        + nt(d_neigh[...], w_recv[...])
        + nn(hot_columns(sends[...], rows), returned)
    ).astype(BF16)


def sum_kernel(parts, out):
    total = jnp.sum(parts[...].astype(F32), axis=0).astype(BF16)
    out[...] = jnp.broadcast_to(total[None], out.shape)


def norm_kernel(total, steps):
    count, width = steps.shape[0], steps.shape[1]
    for m in range(count):
        part = total[m * width : (m + 1) * width].astype(F32)
        mean = jnp.sum(jnp.sum(part * part, axis=0, keepdims=True), axis=1, keepdims=True)
        mean = mean / (part.shape[0] * part.shape[1])
        steps[m] = part / jnp.sqrt(mean + 1e-06)


def call(kernel, outs, scratch=()):
    return pl.pallas_call(
        kernel,
        out_shape=[jax.ShapeDtypeStruct(shape, kind) for shape, kind in outs],
        scratch_shapes=scratch,
        compiler_params=pltpu.CompilerParams(vmem_limit_bytes=40 * 1024 * 1024),
        cost_estimate=pl.CostEstimate(flops=2 * 10**9, bytes_accessed=1024, transcendentals=0),
    )


def shards(
    nodes,
    leave_list,
    arrive_list,
    send_list,
    neighbours,
    valid,
    w_send,
    w_recv,
    w_msg,
    w_self,
    w_agg,
    w_out,
    cotangent,
):
    rows, width = nodes.shape[1:]
    slots = neighbours.shape[2]
    migr = leave_list.shape[1] // 2
    border = send_list.shape[1] // 2
    table_rows = rows + 2 * border
    size = lax.axis_size("slab")
    devices = size * lax.axis_size("grp")
    axes = ("grp", "slab")

    def shift(array, by):
        return lax.ppermute(array, "slab", [(i, (i + by) % size) for i in range(size)])

    message = (border + migr + CODE_ROWS, width)
    message_up = (message[0] + CODE_ROWS, width)
    (token,) = call(first_kernel, [((8, LANES), F32)])()
    to_up, far_up, to_down, far_down = call(
        pack_kernel,
        [(message_up, BF16)] * 2 + [(message, BF16)] * 2,
    )(token, nodes, leave_list, arrive_list, send_list)
    low, low_far = shift(to_up, 1), shift(far_up, 2)
    high, high_far = shift(to_down, -1), shift(far_down, -2)

    matrices = 6
    pair_rows = rows * slots // 2
    share = -(-matrices * width // (8 * devices)) * 8
    sources = (
        nodes,
        arrive_list,
        to_up,
        to_down,
        low,
        low_far,
        high,
        high_far,
        jnp.swapaxes(neighbours, 1, 2),
        jnp.swapaxes(valid, 1, 2),
        w_send,
        w_recv,
        w_msg,
        w_self,
        w_agg,
        w_out,
        cotangent,
    )
    updated, back_low, back_high, grads, d_node, d_centre, d_neigh = call(
        layer_kernel,
        [
            ((1, rows, width), BF16),
            ((border, width), BF16),
            ((border, width), BF16),
            ((devices * share, width), BF16),
            ((rows, width), BF16),
            ((rows, width), BF16),
            ((rows, width), BF16),
        ],
        [
            pltpu.VMEM((rows, LANES), jnp.int32),
            pltpu.VMEM((2 * table_rows, 2 * width), BF16),
            pltpu.VMEM((2, 2 * width, 2 * width), BF16),
            pltpu.VMEM((pair_rows, 2 * width), BF16),
            pltpu.VMEM((pair_rows, 2 * width), F32),
            pltpu.VMEM((pair_rows, 2 * width), F32),
            pltpu.VMEM((rows, width), F32),
            pltpu.VMEM((rows, width), F32),
            pltpu.VMEM((table_rows, width), F32),
            pltpu.VMEM((width, width), F32),
        ],
    )(*sources)
    from_low = shift(back_high, 1)
    from_high = shift(back_low, -1)
    parts = lax.all_to_all(
        grads.reshape(devices, share, width), axes, split_axis=0, concat_axis=0, tiled=True
    )
    sources = (
        cotangent,
        d_node,
        d_centre,
        d_neigh,
        w_self,
        w_send,
        w_recv,
        send_list,
        from_low,
        from_high,
    )
    (grad_nodes,) = call(
        finish_kernel,
        [((1, rows, width), BF16)],
    )(*sources)
    (shared,) = call(sum_kernel, [((devices, share, width), BF16)])(parts)
    total = lax.all_to_all(shared, axes, split_axis=0, concat_axis=0, tiled=True)
    total = total.reshape(devices * share, width)[: matrices * width]
    (weight_steps,) = call(norm_kernel, [((matrices, width, width), F32)])(total)
    return (updated, grad_nodes, weight_steps)


def solution(mesh):
    rows = P("grp", "slab", None)
    lists = P("grp", "slab")
    in_specs = (rows, lists, lists, lists, rows, rows, P(), P(), P(), P(), P(), P(), rows)
    out_specs = (rows, rows, P())
    return jax.shard_map(shards, mesh=mesh, in_specs=in_specs, out_specs=out_specs, check_vma=False)
```

```python
import functools

import jax
import jax.numpy as jnp
from jax import lax
from jax.experimental import pallas as pl
from jax.experimental.pallas import tpu as pltpu
from jax.sharding import PartitionSpec as P

F32 = jnp.float32
BF16 = jnp.bfloat16
CODE_ROWS = 16
LANES = 128
FAR = -1e30
PAIRS = 8


def nn(left, right):
    return lax.dot_general(left, right, (((1,), (0,)), ((), ())), preferred_element_type=F32)


def nt(left, right):
    return lax.dot_general(left, right, (((1,), (1,)), ((), ())), preferred_element_type=F32)


def tn(left, right):
    return lax.dot_general(left, right, (((0,), (0,)), ((), ())), preferred_element_type=F32)


def hot_columns(row, count):
    sub = lax.broadcasted_iota(jnp.int32, (count, row.shape[1]), 0)
    return jnp.where(sub == row, 1.0, 0.0).astype(BF16)


def silu_parts(half):
    tan = jnp.tanh(half)
    part = half * tan
    return half + part, (1.0 + tan) * ((1.0 + half) - part)


def first_kernel(out):
    out[...] = jnp.zeros_like(out)


def pack_kernel(_, nodes, leave, arrive, sends, to_up, far_up, to_down, far_down):
    rows = nodes.shape[1]
    migr = leave.shape[1] // 2
    border = sends.shape[1] // 2
    own = nodes[0]
    leaving = tn(hot_columns(leave[...], rows), own).astype(BF16)
    sub = lax.broadcasted_iota(jnp.int32, (rows, 2 * border), 0)
    column = jnp.transpose(
        jnp.broadcast_to(arrive[...].astype(F32), (2 * border, rows)), (1, 0)
    )
    source = jnp.sum(jnp.where(sub == sends[...], column, 0.0), axis=0, keepdims=True)
    source = source.astype(jnp.int32)
    rest = tn(hot_columns(source, rows), own).astype(BF16)
    code = jnp.where(source >= rows, source - rows, -1).astype(F32)
    for out, far, part in ((to_down, far_down, 0), (to_up, far_up, 1)):
        out[:border] = rest[part * border : (part + 1) * border]
        moving = leaving[part * migr : (part + 1) * migr]
        out[border : border + migr] = moving
        far[:migr] = moving
        far[migr:] = jnp.zeros_like(far[migr:])
        shifted = code if part == 0 else pltpu.roll(code, border, 1)
        tail = out.shape[0] - border - migr
        out[border + migr :] = jnp.broadcast_to(shifted, (tail, 2 * border)).astype(BF16)


def layer_kernel(
    nodes,
    arrive,
    my_up,
    my_down,
    low,
    low_far,
    high,
    high_far,
    nbr,
    valid,
    w_send,
    w_recv,
    w_msg,
    w_self,
    w_agg,
    w_out,
    cotangent,
    updated,
    back_low,
    back_high,
    grads,
    d_node_o,
    d_centre_o,
    d_neigh_o,
    nbr_s,
    neigh_s,
    wide_s,
    hid_s,
    ds1_s,
    ds2_s,
    agg_s,
    dcen_s,
    dneigh_s,
    gmsg_s,
):
    rows, width = nodes.shape[1:]
    slots = nbr.shape[1]
    border = back_low.shape[0]
    migr = high.shape[0] - border - CODE_ROWS
    table_rows = rows + 2 * border
    chunk = 2 * PAIRS
    steps = slots // chunk

    pool = jnp.concatenate(
        [nodes[0], low[border : border + migr], high[border : border + migr]], axis=0
    )
    moved = tn(hot_columns(arrive[...], pool.shape[0]), pool).astype(BF16)

    def halo(message, first, second):
        code = message[border + migr : border + migr + 8].astype(F32)[:1]
        code = code.astype(jnp.int32)
        source = jnp.concatenate([first, second], axis=0)
        extra = tn(hot_columns(code, 2 * migr), source)
        return (message[:border].astype(F32) + extra[:border]).astype(BF16)

    below = halo(low[...], low_far[:migr], my_down[border : border + migr])
    above = halo(high[...], my_up[border : border + migr], high_far[:migr])
    table = jnp.concatenate([moved, below, above], axis=0)

    half_centre = 0.5 * nn(moved, w_send[...])
    half_neigh = (0.5 * nn(table, w_recv[...]).astype(BF16).astype(F32)).astype(BF16)
    none = jnp.zeros((table_rows, width), BF16)
    neigh_s[...] = jnp.concatenate(
        [
            jnp.concatenate([half_neigh, none], axis=1),
            jnp.concatenate([none, half_neigh], axis=1),
        ],
        axis=0,
    )
    half_msg = 0.5 * w_msg[...].astype(F32)
    none = jnp.zeros((width, width), F32)
    for part, block in enumerate((half_msg, jnp.transpose(half_msg, (1, 0)))):
        wide_s[part] = jnp.concatenate(
            [
                jnp.concatenate([block, none], axis=1),
                jnp.concatenate([none, block], axis=1),
            ],
            axis=0,
        ).astype(BF16)
    index = jnp.where(valid[0] == 1, nbr[0], -1)
    fill = jnp.zeros((LANES - slots, rows), jnp.int32)
    nbr_s[...] = jnp.transpose(jnp.concatenate([index, fill], axis=0), (1, 0))
    agg_s[...] = jnp.zeros_like(agg_s)

    lane = lax.broadcasted_iota(jnp.int32, (rows, table_rows), 1).astype(jnp.int16)
    one = jnp.ones((rows, table_rows), BF16)
    zero = jnp.zeros((rows, table_rows), BF16)

    @pl.loop(0, steps)
    def forward(step):
        near = pltpu.roll(nbr_s[...], lax.rem(LANES - step * chunk, LANES), 1)
        ids = [jnp.broadcast_to(near[:, j : j + 1], (rows, LANES)) for j in range(chunk)]
        hots = []
        for j in range(chunk):
            short = ids[j].astype(jnp.int16)
            short = jnp.concatenate([short] * (table_rows // LANES), axis=1)
            hots.append(jnp.where(short == lane, one, zero))
        hot = jnp.concatenate(
            [
                jnp.concatenate([hots[2 * p], hots[2 * p + 1]], axis=1)
                for p in range(PAIRS)
            ],
            axis=0,
        )
        gathered = nn(hot, neigh_s[...])
        base = step * (PAIRS * rows)
        for p in range(PAIRS):
            for side in range(2):
                cols = slice(side * width, (side + 1) * width)
                half = half_centre + gathered[p * rows : (p + 1) * rows, cols]
                half = jnp.where(ids[2 * p + side] < 0, FAR, half)
                act, slope = silu_parts(half)
                span = pl.ds(base + p * rows, rows)
                ds1_s[span, cols] = slope
                hid_s[span, cols] = act.astype(BF16)
        halves = nn(hid_s[pl.ds(base, PAIRS * rows)], wide_s[0])
        total = agg_s[...]
        for p in range(PAIRS):
            for side in range(2):
                cols = slice(side * width, (side + 1) * width)
                act, slope = silu_parts(halves[p * rows : (p + 1) * rows, cols])
                total = total + act
                ds2_s[pl.ds(base + p * rows, rows), cols] = slope
        agg_s[...] = total

    agg_b = agg_s[...].astype(BF16)
    node_pre = nn(moved, w_self[...]) + nn(agg_b, w_agg[...])
    act, slope = silu_parts(0.5 * node_pre)
    node_hid = act.astype(BF16)
    updated[0] = (moved.astype(F32) + nn(node_hid, w_out[...])).astype(BF16)
    cot = cotangent[0]
    d_node = (nt(cot, w_out[...]) * (0.5 * slope)).astype(BF16)
    half_d_agg = 0.5 * nt(d_node, w_agg[...])

    dcen_s[...] = jnp.zeros_like(dcen_s)
    dneigh_s[...] = jnp.zeros_like(dneigh_s)
    gmsg_s[...] = jnp.zeros_like(gmsg_s)
    sub = lax.broadcasted_iota(jnp.int32, (table_rows, rows), 0).astype(jnp.int16)
    one_t = jnp.ones((table_rows, rows), BF16)
    zero_t = jnp.zeros((table_rows, rows), BF16)

    def stack(wide):
        return jnp.concatenate(
            [
                wide[p * rows : (p + 1) * rows, side * width : (side + 1) * width]
                for p in range(PAIRS)
                for side in range(2)
            ],
            axis=0,
        )

    @pl.loop(0, steps)
    def backward(step):
        span = pl.ds(step * (PAIRS * rows), PAIRS * rows)
        d_agg = jnp.concatenate([half_d_agg, half_d_agg], axis=1)
        d_agg = jnp.concatenate([d_agg] * PAIRS, axis=0)
        d_pre2 = (d_agg * ds2_s[span]).astype(BF16)
        d_pre = nn(d_pre2, wide_s[1]) * ds1_s[span]
        gmsg_s[...] += tn(stack(hid_s[span]), stack(d_pre2))
        d_pre = stack(d_pre)
        total = dcen_s[...]
        for j in range(chunk):
            total = total + d_pre[j * rows : (j + 1) * rows]
        dcen_s[...] = total
        hots = []
        for j in range(chunk):
            row = jnp.broadcast_to(nbr[0, pl.ds(step * chunk + j, 1)], (16, rows))
            short = jnp.concatenate([row.astype(jnp.int16)] * (table_rows // 16), axis=0)
            hots.append(jnp.where(short == sub, one_t, zero_t))
        dneigh_s[...] += nn(jnp.concatenate(hots, axis=1), d_pre.astype(BF16))

    d_centre = dcen_s[...].astype(BF16)
    d_neigh = dneigh_s[...].astype(BF16)
    d_borrowed = nt(d_neigh[rows:], w_recv[...]).astype(BF16)
    back_low[...] = d_borrowed[:border]
    back_high[...] = d_borrowed[border:]
    d_node_o[...] = d_node
    d_centre_o[...] = d_centre
    d_neigh_o[...] = d_neigh[:rows]
    parts = (
        tn(moved, d_centre),
        tn(table, d_neigh),
        gmsg_s[...],
        tn(moved, d_node),
        tn(agg_b, d_node),
        tn(node_hid, cot),
    )
    for m, part in enumerate(parts):
        grads[m * width : (m + 1) * width] = part.astype(BF16)
    used = len(parts) * width
    if grads.shape[0] > used:
        grads[used:] = jnp.zeros_like(grads[used:])


def finish_kernel(
    cotangent, d_node, d_centre, d_neigh, w_self, w_send, w_recv, sends, from_low, from_high, out
):
    rows = d_node.shape[0]
    returned = jnp.concatenate([from_low[...], from_high[...]], axis=0)
    out[0] = (
        cotangent[0].astype(F32)
        + nt(d_node[...], w_self[...])
        + nt(d_centre[...], w_send[...])
        + nt(d_neigh[...], w_recv[...])
        + nn(hot_columns(sends[...], rows), returned)
    ).astype(BF16)


def sum_kernel(parts, out):
    total = jnp.sum(parts[...].astype(F32), axis=0).astype(BF16)
    out[...] = jnp.broadcast_to(total[None], out.shape)


def norm_kernel(total, steps):
    count, width = steps.shape[0], steps.shape[1]
    for m in range(count):
        part = total[m * width : (m + 1) * width].astype(F32)
        mean = jnp.sum(jnp.sum(part * part, axis=0, keepdims=True), axis=1, keepdims=True)
        mean = mean / (part.shape[0] * part.shape[1])
        steps[m] = part / jnp.sqrt(mean + 1e-06)


def call(kernel, outs, scratch=()):
    return pl.pallas_call(
        kernel,
        out_shape=[jax.ShapeDtypeStruct(shape, kind) for shape, kind in outs],
        scratch_shapes=scratch,
        compiler_params=pltpu.CompilerParams(vmem_limit_bytes=40 * 1024 * 1024),
        cost_estimate=pl.CostEstimate(flops=2 * 10**9, bytes_accessed=1024, transcendentals=0),
    )


def shards(
    nodes,
    leave_list,
    arrive_list,
    send_list,
    neighbours,
    valid,
    w_send,
    w_recv,
    w_msg,
    w_self,
    w_agg,
    w_out,
    cotangent,
):
    rows, width = nodes.shape[1:]
    slots = neighbours.shape[2]
    migr = leave_list.shape[1] // 2
    border = send_list.shape[1] // 2
    table_rows = rows + 2 * border
    size = lax.axis_size("slab")
    devices = size * lax.axis_size("grp")
    axes = ("grp", "slab")

    def shift(array, by):
        return lax.ppermute(array, "slab", [(i, (i + by) % size) for i in range(size)])

    message = (border + migr + CODE_ROWS, width)
    message_up = (message[0] + CODE_ROWS, width)
    (token,) = call(first_kernel, [((8, LANES), F32)])()
    to_up, far_up, to_down, far_down = call(
        pack_kernel,
        [(message_up, BF16)] * 2 + [(message, BF16)] * 2,
    )(token, nodes, leave_list, arrive_list, send_list)
    low, low_far = shift(to_up, 1), shift(far_up, 2)
    high, high_far = shift(to_down, -1), shift(far_down, -2)

    matrices = 6
    pair_rows = rows * slots // 2
    share = -(-matrices * width // (8 * devices)) * 8
    sources = (
        nodes,
        arrive_list,
        to_up,
        to_down,
        low,
        low_far,
        high,
        high_far,
        jnp.swapaxes(neighbours, 1, 2),
        jnp.swapaxes(valid, 1, 2),
        w_send,
        w_recv,
        w_msg,
        w_self,
        w_agg,
        w_out,
        cotangent,
    )
    updated, back_low, back_high, grads, d_node, d_centre, d_neigh = call(
        layer_kernel,
        [
            ((1, rows, width), BF16),
            ((border, width), BF16),
            ((border, width), BF16),
            ((devices * share, width), BF16),
            ((rows, width), BF16),
            ((rows, width), BF16),
            ((rows, width), BF16),
        ],
        [
            pltpu.VMEM((rows, LANES), jnp.int32),
            pltpu.VMEM((2 * table_rows, 2 * width), BF16),
            pltpu.VMEM((2, 2 * width, 2 * width), BF16),
            pltpu.VMEM((pair_rows, 2 * width), BF16),
            pltpu.VMEM((pair_rows, 2 * width), F32),
            pltpu.VMEM((pair_rows, 2 * width), F32),
            pltpu.VMEM((rows, width), F32),
            pltpu.VMEM((rows, width), F32),
            pltpu.VMEM((table_rows, width), F32),
            pltpu.VMEM((width, width), F32),
        ],
    )(*sources)
    from_low = shift(back_high, 1)
    from_high = shift(back_low, -1)
    parts = lax.all_to_all(
        grads.reshape(devices, share, width), axes, split_axis=0, concat_axis=0, tiled=True
    )
    sources = (
        cotangent,
        d_node,
        d_centre,
        d_neigh,
        w_self,
        w_send,
        w_recv,
        send_list,
        from_low,
        from_high,
    )
    (grad_nodes,) = call(
        finish_kernel,
        [((1, rows, width), BF16)],
    )(*sources)
    (shared,) = call(sum_kernel, [((devices, share, width), BF16)])(parts)
    total = lax.all_to_all(shared, axes, split_axis=0, concat_axis=0, tiled=True)
    total = total.reshape(devices * share, width)[: matrices * width]
    (weight_steps,) = call(norm_kernel, [((matrices, width, width), F32)])(total)
    return (updated, grad_nodes, weight_steps)


def solution(mesh):
    rows = P("grp", "slab", None)
    lists = P("grp", "slab")
    in_specs = (rows, lists, lists, lists, rows, rows, P(), P(), P(), P(), P(), P(), rows)
    out_specs = (rows, rows, P())
    return jax.shard_map(shards, mesh=mesh, in_specs=in_specs, out_specs=out_specs, check_vma=False)
```

```python
import functools

import jax
import jax.numpy as jnp
from jax import lax
from jax.experimental import pallas as pl
from jax.experimental.pallas import tpu as pltpu
from jax.sharding import PartitionSpec as P

F32 = jnp.float32
BF16 = jnp.bfloat16
CODE_ROWS = 16
LANES = 128
FAR = -1e30
PAIRS = 8


def nn(left, right):
    return lax.dot_general(left, right, (((1,), (0,)), ((), ())), preferred_element_type=F32)


def nt(left, right):
    return lax.dot_general(left, right, (((1,), (1,)), ((), ())), preferred_element_type=F32)


def tn(left, right):
    return lax.dot_general(left, right, (((0,), (0,)), ((), ())), preferred_element_type=F32)


def hot_columns(row, count):
    sub = lax.broadcasted_iota(jnp.int32, (count, row.shape[1]), 0)
    return jnp.where(sub == row, 1.0, 0.0).astype(BF16)


def silu_parts(half):
    tan = jnp.tanh(half)
    part = half * tan
    return half + part, (1.0 + tan) * ((1.0 + half) - part)


def first_kernel(out):
    out[...] = jnp.zeros_like(out)


def pack_kernel(_, nodes, leave, arrive, sends, to_up, far_up, to_down, far_down):
    rows = nodes.shape[1]
    migr = leave.shape[1] // 2
    border = sends.shape[1] // 2
    own = nodes[0]
    leaving = tn(hot_columns(leave[...], rows), own).astype(BF16)
    sub = lax.broadcasted_iota(jnp.int32, (rows, 2 * border), 0)
    column = jnp.transpose(
        jnp.broadcast_to(arrive[...].astype(F32), (2 * border, rows)), (1, 0)
    )
    source = jnp.sum(jnp.where(sub == sends[...], column, 0.0), axis=0, keepdims=True)
    source = source.astype(jnp.int32)
    rest = tn(hot_columns(source, rows), own).astype(BF16)
    code = jnp.where(source >= rows, source - rows, -1).astype(F32)
    for out, far, part in ((to_down, far_down, 0), (to_up, far_up, 1)):
        out[:border] = rest[part * border : (part + 1) * border]
        moving = leaving[part * migr : (part + 1) * migr]
        out[border : border + migr] = moving
        far[:migr] = moving
        far[migr:] = jnp.zeros_like(far[migr:])
        shifted = code if part == 0 else pltpu.roll(code, border, 1)
        tail = out.shape[0] - border - migr
        out[border + migr :] = jnp.broadcast_to(shifted, (tail, 2 * border)).astype(BF16)


def layer_kernel(
    nodes,
    arrive,
    my_up,
    my_down,
    low,
    low_far,
    high,
    high_far,
    nbr,
    valid,
    w_send,
    w_recv,
    w_msg,
    w_self,
    w_agg,
    w_out,
    cotangent,
    updated,
    back_low,
    back_high,
    grads,
    d_node_o,
    d_centre_o,
    d_neigh_o,
    nbr_s,
    row_s,
    neigh_s,
    wide_s,
    hid_s,
    ds1_s,
    ds2_s,
    agg_s,
    dcen_s,
    dneigh_s,
    gmsg_s,
):
    rows, width = nodes.shape[1:]
    slots = nbr.shape[1]
    border = back_low.shape[0]
    migr = high.shape[0] - border - CODE_ROWS
    table_rows = rows + 2 * border
    chunk = 2 * PAIRS
    steps = slots // chunk

    pool = jnp.concatenate(
        [nodes[0], low[border : border + migr], high[border : border + migr]], axis=0
    )
    moved = tn(hot_columns(arrive[...], pool.shape[0]), pool).astype(BF16)

    def halo(message, first, second):
        code = message[border + migr : border + migr + 8].astype(F32)[:1]
        code = code.astype(jnp.int32)
        source = jnp.concatenate([first, second], axis=0)
        extra = tn(hot_columns(code, 2 * migr), source)
        return (message[:border].astype(F32) + extra[:border]).astype(BF16)

    below = halo(low[...], low_far[:migr], my_down[border : border + migr])
    above = halo(high[...], my_up[border : border + migr], high_far[:migr])
    table = jnp.concatenate([moved, below, above], axis=0)

    half_rows = table_rows // 2
    hot_rows = -(-(half_rows + 1) // LANES) * LANES
    half_centre = 0.5 * nn(moved, w_send[...])
    half_neigh = (0.5 * nn(table, w_recv[...]).astype(BF16).astype(F32)).astype(BF16)
    neigh_s[:half_rows] = jnp.concatenate([half_neigh[:half_rows], half_neigh[half_rows:]], axis=1)
    neigh_s[half_rows:] = jnp.full((hot_rows - half_rows, 2 * width), FAR, BF16)
    half_msg = 0.5 * w_msg[...].astype(F32)
    none = jnp.zeros((width, width), F32)
    for part, block in enumerate((half_msg, jnp.transpose(half_msg, (1, 0)))):
        wide_s[part] = jnp.concatenate(
            [
                jnp.concatenate([block, none], axis=1),
                jnp.concatenate([none, block], axis=1),
            ],
            axis=0,
        ).astype(BF16)
    upper = nbr[0] >= half_rows
    low_row = jnp.where(upper, nbr[0] - half_rows, nbr[0])
    row_s[...] = low_row
    index = jnp.where(valid[0] == 1, low_row, half_rows) + jnp.where(upper, hot_rows, 0)
    fill = jnp.zeros((LANES - slots, rows), jnp.int32)
    nbr_s[...] = jnp.transpose(jnp.concatenate([index, fill], axis=0), (1, 0))
    agg_s[...] = jnp.zeros_like(agg_s)

    lane = lax.broadcasted_iota(jnp.int32, (rows, hot_rows), 1).astype(jnp.int16)
    one = jnp.ones((rows, hot_rows), BF16)
    zero = jnp.zeros((rows, hot_rows), BF16)

    def slot_ids(step):
        near = pltpu.roll(nbr_s[...], lax.rem(LANES - step * chunk, LANES), 1)
        return [jnp.broadcast_to(near[:, j : j + 1], (rows, LANES)) for j in range(chunk)]

    @pl.loop(0, steps)
    def forward(step):
        ids = slot_ids(step)
        hots = []
        for j in range(chunk):
            short = (ids[j] & (hot_rows - 1)).astype(jnp.int16)
            short = jnp.concatenate([short] * (hot_rows // LANES), axis=1)
            hots.append(jnp.where(short == lane, one, zero))
        gathered = nn(jnp.concatenate(hots, axis=0), neigh_s[...])
        base = step * (PAIRS * rows)
        for p in range(PAIRS):
            for side in range(2):
                cols = slice(side * width, (side + 1) * width)
                j = 2 * p + side
                pick = gathered[j * rows : (j + 1) * rows]
                pick = jnp.where(ids[j] >= hot_rows, pick[:, width:], pick[:, :width])
                act, slope = silu_parts(half_centre + pick)
                span = pl.ds(base + p * rows, rows)
                ds1_s[span, cols] = slope
                hid_s[span, cols] = act.astype(BF16)
        halves = nn(hid_s[pl.ds(base, PAIRS * rows)], wide_s[0])
        total = agg_s[...]
        for p in range(PAIRS):
            for side in range(2):
                cols = slice(side * width, (side + 1) * width)
                act, slope = silu_parts(halves[p * rows : (p + 1) * rows, cols])
                total = total + act
                ds2_s[pl.ds(base + p * rows, rows), cols] = slope
        agg_s[...] = total

    agg_b = agg_s[...].astype(BF16)
    node_pre = nn(moved, w_self[...]) + nn(agg_b, w_agg[...])
    act, slope = silu_parts(0.5 * node_pre)
    node_hid = act.astype(BF16)
    updated[0] = (moved.astype(F32) + nn(node_hid, w_out[...])).astype(BF16)
    cot = cotangent[0]
    d_node = (nt(cot, w_out[...]) * (0.5 * slope)).astype(BF16)
    half_d_agg = 0.5 * nt(d_node, w_agg[...])

    dcen_s[...] = jnp.zeros_like(dcen_s)
    dneigh_s[...] = jnp.zeros_like(dneigh_s)
    gmsg_s[...] = jnp.zeros_like(gmsg_s)
    sub = lax.broadcasted_iota(jnp.int32, (half_rows, rows), 0).astype(jnp.int16)
    one_t = jnp.ones((half_rows, rows), BF16)
    zero_t = jnp.zeros((half_rows, rows), BF16)
    none = jnp.zeros((rows, width), BF16)
    border_id = jnp.full((rows, width), hot_rows, jnp.int16)

    @pl.loop(0, steps)
    def backward(step):
        ids = slot_ids(step)
        span = pl.ds(step * (PAIRS * rows), PAIRS * rows)
        d_agg = jnp.concatenate([half_d_agg, half_d_agg], axis=1)
        d_agg = jnp.concatenate([d_agg] * PAIRS, axis=0)
        d_pre2 = (d_agg * ds2_s[span]).astype(BF16)
        d_pre = nn(d_pre2, wide_s[1]) * ds1_s[span]
        gmsg_s[...] += tn(hid_s[span], d_pre2)
        total = dcen_s[...]
        hots, wides = [], []
        for j in range(chunk):
            p, side = divmod(j, 2)
            part = d_pre[p * rows : (p + 1) * rows, side * width : (side + 1) * width]
            total = total + part
            part = part.astype(BF16)
            is_up = ids[j].astype(jnp.int16) >= border_id
            wides.append(
                jnp.concatenate(
                    [jnp.where(is_up, none, part), jnp.where(is_up, part, none)], axis=1
                )
            )
            row = jnp.broadcast_to(row_s[pl.ds(step * chunk + j, 1)], (16, rows))
            short = jnp.concatenate([row.astype(jnp.int16)] * (half_rows // 16), axis=0)
            hots.append(jnp.where(short == sub, one_t, zero_t))
        dcen_s[...] = total
        dneigh_s[...] += nn(jnp.concatenate(hots, axis=1), jnp.concatenate(wides, axis=0))

    d_centre = dcen_s[...].astype(BF16)
    d_neigh = dneigh_s[...].astype(BF16)
    d_neigh = jnp.concatenate([d_neigh[:, :width], d_neigh[:, width:]], axis=0)
    d_borrowed = nt(d_neigh[rows:], w_recv[...]).astype(BF16)
    back_low[...] = d_borrowed[:border]
    back_high[...] = d_borrowed[border:]
    d_node_o[...] = d_node
    d_centre_o[...] = d_centre
    d_neigh_o[...] = d_neigh[:rows]
    parts = (
        tn(moved, d_centre),
        tn(table, d_neigh),
        gmsg_s[:width, :width] + gmsg_s[width:, width:],
        tn(moved, d_node),
        tn(agg_b, d_node),
        tn(node_hid, cot),
    )
    for m, part in enumerate(parts):
        grads[m * width : (m + 1) * width] = part.astype(BF16)
    used = len(parts) * width
    if grads.shape[0] > used:
        grads[used:] = jnp.zeros_like(grads[used:])


def finish_kernel(
    cotangent, d_node, d_centre, d_neigh, w_self, w_send, w_recv, sends, from_low, from_high, out
):
    rows = d_node.shape[0]
    returned = jnp.concatenate([from_low[...], from_high[...]], axis=0)
    out[0] = (
        cotangent[0].astype(F32)
        + nt(d_node[...], w_self[...])
        + nt(d_centre[...], w_send[...])
        + nt(d_neigh[...], w_recv[...])
        + nn(hot_columns(sends[...], rows), returned)
    ).astype(BF16)


def sum_kernel(parts, out):
    total = jnp.sum(parts[...].astype(F32), axis=0).astype(BF16)
    out[...] = jnp.broadcast_to(total[None], out.shape)


def norm_kernel(total, steps):
    count, width = steps.shape[0], steps.shape[1]
    for m in range(count):
        part = total[m * width : (m + 1) * width].astype(F32)
        mean = jnp.sum(jnp.sum(part * part, axis=0, keepdims=True), axis=1, keepdims=True)
        mean = mean / (part.shape[0] * part.shape[1])
        steps[m] = part / jnp.sqrt(mean + 1e-06)


def call(kernel, outs, scratch=()):
    return pl.pallas_call(
        kernel,
        out_shape=[jax.ShapeDtypeStruct(shape, kind) for shape, kind in outs],
        scratch_shapes=scratch,
        compiler_params=pltpu.CompilerParams(vmem_limit_bytes=40 * 1024 * 1024),
        cost_estimate=pl.CostEstimate(flops=2 * 10**9, bytes_accessed=1024, transcendentals=0),
    )


def shards(
    nodes,
    leave_list,
    arrive_list,
    send_list,
    neighbours,
    valid,
    w_send,
    w_recv,
    w_msg,
    w_self,
    w_agg,
    w_out,
    cotangent,
):
    rows, width = nodes.shape[1:]
    slots = neighbours.shape[2]
    migr = leave_list.shape[1] // 2
    border = send_list.shape[1] // 2
    table_rows = rows + 2 * border
    size = lax.axis_size("slab")
    devices = size * lax.axis_size("grp")
    axes = ("grp", "slab")

    def shift(array, by):
        return lax.ppermute(array, "slab", [(i, (i + by) % size) for i in range(size)])

    message = (border + migr + CODE_ROWS, width)
    message_up = (message[0] + CODE_ROWS, width)
    (token,) = call(first_kernel, [((8, LANES), F32)])()
    to_up, far_up, to_down, far_down = call(
        pack_kernel,
        [(message_up, BF16)] * 2 + [(message, BF16)] * 2,
    )(token, nodes, leave_list, arrive_list, send_list)
    low, low_far = shift(to_up, 1), shift(far_up, 2)
    high, high_far = shift(to_down, -1), shift(far_down, -2)

    matrices = 6
    pair_rows = rows * slots // 2
    half_rows = table_rows // 2
    hot_rows = -(-(half_rows + 1) // LANES) * LANES
    share = -(-matrices * width // (8 * devices)) * 8
    sources = (
        nodes,
        arrive_list,
        to_up,
        to_down,
        low,
        low_far,
        high,
        high_far,
        jnp.swapaxes(neighbours, 1, 2),
        jnp.swapaxes(valid, 1, 2),
        w_send,
        w_recv,
        w_msg,
        w_self,
        w_agg,
        w_out,
        cotangent,
    )
    updated, back_low, back_high, grads, d_node, d_centre, d_neigh = call(
        layer_kernel,
        [
            ((1, rows, width), BF16),
            ((border, width), BF16),
            ((border, width), BF16),
            ((devices * share, width), BF16),
            ((rows, width), BF16),
            ((rows, width), BF16),
            ((rows, width), BF16),
        ],
        [
            pltpu.VMEM((rows, LANES), jnp.int32),
            pltpu.VMEM((slots, rows), jnp.int32),
            pltpu.VMEM((hot_rows, 2 * width), BF16),
            pltpu.VMEM((2, 2 * width, 2 * width), BF16),
            pltpu.VMEM((pair_rows, 2 * width), BF16),
            pltpu.VMEM((pair_rows, 2 * width), F32),
            pltpu.VMEM((pair_rows, 2 * width), F32),
            pltpu.VMEM((rows, width), F32),
            pltpu.VMEM((rows, width), F32),
            pltpu.VMEM((half_rows, 2 * width), F32),
            pltpu.VMEM((2 * width, 2 * width), F32),
        ],
    )(*sources)
    from_low = shift(back_high, 1)
    from_high = shift(back_low, -1)
    parts = lax.all_to_all(
        grads.reshape(devices, share, width), axes, split_axis=0, concat_axis=0, tiled=True
    )
    sources = (
        cotangent,
        d_node,
        d_centre,
        d_neigh,
        w_self,
        w_send,
        w_recv,
        send_list,
        from_low,
        from_high,
    )
    (grad_nodes,) = call(
        finish_kernel,
        [((1, rows, width), BF16)],
    )(*sources)
    (shared,) = call(sum_kernel, [((devices, share, width), BF16)])(parts)
    total = lax.all_to_all(shared, axes, split_axis=0, concat_axis=0, tiled=True)
    total = total.reshape(devices * share, width)[: matrices * width]
    (weight_steps,) = call(norm_kernel, [((matrices, width, width), F32)])(total)
    return (updated, grad_nodes, weight_steps)


def solution(mesh):
    rows = P("grp", "slab", None)
    lists = P("grp", "slab")
    in_specs = (rows, lists, lists, lists, rows, rows, P(), P(), P(), P(), P(), P(), rows)
    out_specs = (rows, rows, P())
    return jax.shard_map(shards, mesh=mesh, in_specs=in_specs, out_specs=out_specs, check_vma=False)
```

```python
import functools

import jax
import jax.numpy as jnp
from jax import lax
from jax.experimental import pallas as pl
from jax.experimental.pallas import tpu as pltpu
from jax.sharding import PartitionSpec as P

F32 = jnp.float32
BF16 = jnp.bfloat16
CODE_ROWS = 16
LANES = 128
FAR = -1e30
PAIRS = 8


def nn(left, right):
    return lax.dot_general(left, right, (((1,), (0,)), ((), ())), preferred_element_type=F32)


def nt(left, right):
    return lax.dot_general(left, right, (((1,), (1,)), ((), ())), preferred_element_type=F32)


def tn(left, right):
    return lax.dot_general(left, right, (((0,), (0,)), ((), ())), preferred_element_type=F32)


def hot_columns(row, count):
    sub = lax.broadcasted_iota(jnp.int32, (count, row.shape[1]), 0)
    return jnp.where(sub == row, 1.0, 0.0).astype(BF16)


def silu_parts(half):
    tan = jnp.tanh(half)
    part = half * tan
    return half + part, (1.0 + tan) * ((1.0 + half) - part)


def first_kernel(out):
    out[...] = jnp.zeros_like(out)


def pack_kernel(_, nodes, leave, arrive, sends, to_up, far_up, to_down, far_down):
    rows = nodes.shape[1]
    migr = leave.shape[1] // 2
    border = sends.shape[1] // 2
    own = nodes[0]
    leaving = tn(hot_columns(leave[...], rows), own).astype(BF16)
    sub = lax.broadcasted_iota(jnp.int32, (rows, 2 * border), 0)
    column = jnp.transpose(
        jnp.broadcast_to(arrive[...].astype(F32), (2 * border, rows)), (1, 0)
    )
    source = jnp.sum(jnp.where(sub == sends[...], column, 0.0), axis=0, keepdims=True)
    source = source.astype(jnp.int32)
    rest = tn(hot_columns(source, rows), own).astype(BF16)
    code = jnp.where(source >= rows, source - rows, -1).astype(F32)
    for out, far, part in ((to_down, far_down, 0), (to_up, far_up, 1)):
        out[:border] = rest[part * border : (part + 1) * border]
        moving = leaving[part * migr : (part + 1) * migr]
        out[border : border + migr] = moving
        far[:migr] = moving
        if far.shape[0] > migr:
            far[migr:] = jnp.zeros_like(far[migr:])
        shifted = code if part == 0 else pltpu.roll(code, border, 1)
        tail = out.shape[0] - border - migr
        out[border + migr :] = jnp.broadcast_to(shifted, (tail, 2 * border)).astype(BF16)


def layer_kernel(
    nodes,
    arrive,
    my_up,
    my_down,
    low,
    low_far,
    high,
    high_far,
    nbr,
    valid,
    w_send,
    w_recv,
    w_msg,
    w_self,
    w_agg,
    w_out,
    cotangent,
    updated,
    back_low,
    back_high,
    grads,
    d_node_o,
    d_centre_o,
    d_neigh_o,
    nbr_s,
    row_s,
    neigh_s,
    wide_s,
    hid_s,
    ds1_s,
    ds2_s,
    agg_s,
    dcen_s,
    dneigh_s,
    gmsg_s,
):
    rows, width = nodes.shape[1:]
    slots = nbr.shape[1]
    border = back_low.shape[0]
    migr = high.shape[0] - border - CODE_ROWS
    table_rows = rows + 2 * border
    chunk = 2 * PAIRS
    steps = slots // chunk

    pool = jnp.concatenate(
        [nodes[0], low[border : border + migr], high[border : border + migr]], axis=0
    )
    moved = tn(hot_columns(arrive[...], pool.shape[0]), pool).astype(BF16)

    def halo(message, first, second):
        code = message[border + migr : border + migr + 8].astype(F32)[:1]
        code = code.astype(jnp.int32)
        source = jnp.concatenate([first, second], axis=0)
        extra = tn(hot_columns(code, 2 * migr), source)
        return (message[:border].astype(F32) + extra[:border]).astype(BF16)

    below = halo(low[...], low_far[:migr], my_down[border : border + migr])
    above = halo(high[...], my_up[border : border + migr], high_far[:migr])
    table = jnp.concatenate([moved, below, above], axis=0)

    half_rows = table_rows // 2
    hot_rows = -(-(half_rows + 1) // LANES) * LANES
    half_centre = 0.5 * nn(moved, w_send[...])
    half_neigh = (0.5 * nn(table, w_recv[...]).astype(BF16).astype(F32)).astype(BF16)
    neigh_s[:half_rows] = jnp.concatenate([half_neigh[:half_rows], half_neigh[half_rows:]], axis=1)
    neigh_s[half_rows:] = jnp.full((hot_rows - half_rows, 2 * width), FAR, BF16)
    half_msg = 0.5 * w_msg[...].astype(F32)
    none = jnp.zeros((width, width), F32)
    for part, block in enumerate((half_msg, jnp.transpose(half_msg, (1, 0)))):
        wide_s[part] = jnp.concatenate(
            [
                jnp.concatenate([block, none], axis=1),
                jnp.concatenate([none, block], axis=1),
            ],
            axis=0,
        ).astype(BF16)
    upper = nbr[0] >= half_rows
    low_row = jnp.where(upper, nbr[0] - half_rows, nbr[0])
    row_s[...] = low_row
    index = jnp.where(valid[0] == 1, low_row, half_rows) + jnp.where(upper, hot_rows, 0)
    fill = jnp.zeros((LANES - slots, rows), jnp.int32)
    nbr_s[...] = jnp.transpose(jnp.concatenate([index, fill], axis=0), (1, 0))
    agg_s[...] = jnp.zeros_like(agg_s)

    lane = lax.broadcasted_iota(jnp.int32, (rows, hot_rows), 1).astype(jnp.int16)
    one = jnp.ones((rows, hot_rows), BF16)
    zero = jnp.zeros((rows, hot_rows), BF16)

    def slot_ids(step):
        near = pltpu.roll(nbr_s[...], lax.rem(LANES - step * chunk, LANES), 1)
        return [jnp.broadcast_to(near[:, j : j + 1], (rows, LANES)) for j in range(chunk)]

    @pl.loop(0, steps)
    def forward(step):
        ids = slot_ids(step)
        hots = []
        for j in range(chunk):
            short = (ids[j] & (hot_rows - 1)).astype(jnp.int16)
            short = jnp.concatenate([short] * (hot_rows // LANES), axis=1)
            hots.append(jnp.where(short == lane, one, zero))
        gathered = nn(jnp.concatenate(hots, axis=0), neigh_s[...])
        base = step * (PAIRS * rows)
        for p in range(PAIRS):
            for side in range(2):
                cols = slice(side * width, (side + 1) * width)
                j = 2 * p + side
                pick = gathered[j * rows : (j + 1) * rows]
                pick = jnp.where(ids[j] >= hot_rows, pick[:, width:], pick[:, :width])
                act, slope = silu_parts(half_centre + pick)
                span = pl.ds(base + p * rows, rows)
                ds1_s[span, cols] = slope
                hid_s[span, cols] = act.astype(BF16)
        halves = nn(hid_s[pl.ds(base, PAIRS * rows)], wide_s[0])
        total = agg_s[...]
        for p in range(PAIRS):
            for side in range(2):
                cols = slice(side * width, (side + 1) * width)
                act, slope = silu_parts(halves[p * rows : (p + 1) * rows, cols])
                total = total + act
                ds2_s[pl.ds(base + p * rows, rows), cols] = slope
        agg_s[...] = total

    agg_b = agg_s[...].astype(BF16)
    node_pre = nn(moved, w_self[...]) + nn(agg_b, w_agg[...])
    act, slope = silu_parts(0.5 * node_pre)
    node_hid = act.astype(BF16)
    updated[0] = (moved.astype(F32) + nn(node_hid, w_out[...])).astype(BF16)
    cot = cotangent[0]
    d_node = (nt(cot, w_out[...]) * (0.5 * slope)).astype(BF16)
    half_d_agg = 0.5 * nt(d_node, w_agg[...])

    dcen_s[...] = jnp.zeros_like(dcen_s)
    dneigh_s[...] = jnp.zeros_like(dneigh_s)
    gmsg_s[...] = jnp.zeros_like(gmsg_s)
    sub = lax.broadcasted_iota(jnp.int32, (half_rows, rows), 0).astype(jnp.int16)
    one_t = jnp.ones((half_rows, rows), BF16)
    zero_t = jnp.zeros((half_rows, rows), BF16)
    none = jnp.zeros((rows, width), BF16)
    border_id = jnp.full((rows, width), hot_rows, jnp.int16)

    @pl.loop(0, steps)
    def backward(step):
        ids = slot_ids(step)
        span = pl.ds(step * (PAIRS * rows), PAIRS * rows)
        d_agg = jnp.concatenate([half_d_agg, half_d_agg], axis=1)
        d_agg = jnp.concatenate([d_agg] * PAIRS, axis=0)
        d_pre2 = (d_agg * ds2_s[span]).astype(BF16)
        d_pre = nn(d_pre2, wide_s[1]) * ds1_s[span]
        gmsg_s[...] += tn(hid_s[span], d_pre2)
        total = dcen_s[...]
        hots, wides = [], []
        for j in range(chunk):
            p, side = divmod(j, 2)
            part = d_pre[p * rows : (p + 1) * rows, side * width : (side + 1) * width]
            total = total + part
            part = part.astype(BF16)
            is_up = ids[j].astype(jnp.int16) >= border_id
            wides.append(
                jnp.concatenate(
                    [jnp.where(is_up, none, part), jnp.where(is_up, part, none)], axis=1
                )
            )
            row = jnp.broadcast_to(row_s[pl.ds(step * chunk + j, 1)], (16, rows))
            short = jnp.concatenate([row.astype(jnp.int16)] * (half_rows // 16), axis=0)
            hots.append(jnp.where(short == sub, one_t, zero_t))
        dcen_s[...] = total
        dneigh_s[...] += nn(jnp.concatenate(hots, axis=1), jnp.concatenate(wides, axis=0))

    d_centre = dcen_s[...].astype(BF16)
    d_neigh = dneigh_s[...].astype(BF16)
    d_neigh = jnp.concatenate([d_neigh[:, :width], d_neigh[:, width:]], axis=0)
    d_borrowed = nt(d_neigh[rows:], w_recv[...]).astype(BF16)
    back_low[...] = d_borrowed[:border]
    back_high[...] = d_borrowed[border:]
    d_node_o[...] = d_node
    d_centre_o[...] = d_centre
    d_neigh_o[...] = d_neigh[:rows]
    parts = (
        tn(moved, d_centre),
        tn(table, d_neigh),
        gmsg_s[:width, :width] + gmsg_s[width:, width:],
        tn(moved, d_node),
        tn(agg_b, d_node),
        tn(node_hid, cot),
    )
    for m, part in enumerate(parts):
        grads[m * width : (m + 1) * width] = part.astype(BF16)
    used = len(parts) * width
    if grads.shape[0] > used:
        grads[used:] = jnp.zeros_like(grads[used:])


def finish_kernel(
    cotangent, d_node, d_centre, d_neigh, w_self, w_send, w_recv, sends, from_low, from_high, out
):
    rows = d_node.shape[0]
    returned = jnp.concatenate([from_low[...], from_high[...]], axis=0)
    out[0] = (
        cotangent[0].astype(F32)
        + nt(d_node[...], w_self[...])
        + nt(d_centre[...], w_send[...])
        + nt(d_neigh[...], w_recv[...])
        + nn(hot_columns(sends[...], rows), returned)
    ).astype(BF16)


def sum_kernel(parts, _, __, out):
    total = jnp.sum(parts[...].astype(F32), axis=0).astype(BF16)
    out[...] = jnp.broadcast_to(total[None], out.shape)


def norm_kernel(total, steps):
    count, width = steps.shape[0], steps.shape[1]
    for m in range(count):
        part = total[m * width : (m + 1) * width].astype(F32)
        mean = jnp.sum(jnp.sum(part * part, axis=0, keepdims=True), axis=1, keepdims=True)
        mean = mean / (part.shape[0] * part.shape[1])
        steps[m] = part / jnp.sqrt(mean + 1e-06)


def call(kernel, outs, scratch=()):
    return pl.pallas_call(
        kernel,
        out_shape=[jax.ShapeDtypeStruct(shape, kind) for shape, kind in outs],
        scratch_shapes=scratch,
        compiler_params=pltpu.CompilerParams(vmem_limit_bytes=40 * 1024 * 1024),
        cost_estimate=pl.CostEstimate(flops=2 * 10**9, bytes_accessed=1024, transcendentals=0),
    )


def shards(
    nodes,
    leave_list,
    arrive_list,
    send_list,
    neighbours,
    valid,
    w_send,
    w_recv,
    w_msg,
    w_self,
    w_agg,
    w_out,
    cotangent,
):
    rows, width = nodes.shape[1:]
    slots = neighbours.shape[2]
    migr = leave_list.shape[1] // 2
    border = send_list.shape[1] // 2
    table_rows = rows + 2 * border
    size = lax.axis_size("slab")
    devices = size * lax.axis_size("grp")
    axes = ("grp", "slab")

    def shift(array, by):
        return lax.ppermute(array, "slab", [(i, (i + by) % size) for i in range(size)])

    down_rows = border + migr + CODE_ROWS
    lengths = (down_rows + 2 * CODE_ROWS, down_rows + CODE_ROWS, down_rows, migr)
    (token,) = call(first_kernel, [((8, LANES), F32)])()
    to_up, far_up, to_down, far_down = call(
        pack_kernel,
        [((length, width), BF16) for length in lengths],
    )(token, nodes, leave_list, arrive_list, send_list)
    low, low_far = shift(to_up, 1), shift(far_up, 2)
    high, high_far = shift(to_down, -1), shift(far_down, -2)

    matrices = 6
    pair_rows = rows * slots // 2
    half_rows = table_rows // 2
    hot_rows = -(-(half_rows + 1) // LANES) * LANES
    share = -(-matrices * width // (8 * devices)) * 8
    sources = (
        nodes,
        arrive_list,
        to_up,
        to_down,
        low,
        low_far,
        high,
        high_far,
        jnp.swapaxes(neighbours, 1, 2),
        jnp.swapaxes(valid, 1, 2),
        w_send,
        w_recv,
        w_msg,
        w_self,
        w_agg,
        w_out,
        cotangent,
    )
    updated, back_low, back_high, grads, d_node, d_centre, d_neigh = call(
        layer_kernel,
        [
            ((1, rows, width), BF16),
            ((border, width), BF16),
            ((border, width), BF16),
            ((devices * share, width), BF16),
            ((rows, width), BF16),
            ((rows, width), BF16),
            ((rows, width), BF16),
        ],
        [
            pltpu.VMEM((rows, LANES), jnp.int32),
            pltpu.VMEM((slots, rows), jnp.int32),
            pltpu.VMEM((hot_rows, 2 * width), BF16),
            pltpu.VMEM((2, 2 * width, 2 * width), BF16),
            pltpu.VMEM((pair_rows, 2 * width), BF16),
            pltpu.VMEM((pair_rows, 2 * width), F32),
            pltpu.VMEM((pair_rows, 2 * width), F32),
            pltpu.VMEM((rows, width), F32),
            pltpu.VMEM((rows, width), F32),
            pltpu.VMEM((half_rows, 2 * width), F32),
            pltpu.VMEM((2 * width, 2 * width), F32),
        ],
    )(*sources)
    from_low = shift(back_high, 1)
    from_high = shift(back_low, -1)
    parts = lax.all_to_all(
        grads.reshape(devices, share, width), axes, split_axis=0, concat_axis=0, tiled=True
    )
    sources = (
        cotangent,
        d_node,
        d_centre,
        d_neigh,
        w_self,
        w_send,
        w_recv,
        send_list,
        from_low,
        from_high,
    )
    (grad_nodes,) = call(
        finish_kernel,
        [((1, rows, width), BF16)],
    )(*sources)
    (shared,) = call(sum_kernel, [((devices, share, width), BF16)])(parts, from_low, from_high)
    total = lax.all_to_all(shared, axes, split_axis=0, concat_axis=0, tiled=True)
    total = total.reshape(devices * share, width)[: matrices * width]
    (weight_steps,) = call(norm_kernel, [((matrices, width, width), F32)])(total)
    return (updated, grad_nodes, weight_steps)


def solution(mesh):
    rows = P("grp", "slab", None)
    lists = P("grp", "slab")
    in_specs = (rows, lists, lists, lists, rows, rows, P(), P(), P(), P(), P(), P(), rows)
    out_specs = (rows, rows, P())
    return jax.shard_map(shards, mesh=mesh, in_specs=in_specs, out_specs=out_specs, check_vma=False)
```

```python
import functools

import jax
import jax.numpy as jnp
from jax import lax
from jax.experimental import pallas as pl
from jax.experimental.pallas import tpu as pltpu
from jax.sharding import PartitionSpec as P

F32 = jnp.float32
BF16 = jnp.bfloat16
CODE_ROWS = 16
LANES = 128
FAR = -1e30
PAIRS = 8


def nn(left, right):
    return lax.dot_general(left, right, (((1,), (0,)), ((), ())), preferred_element_type=F32)


def nt(left, right):
    return lax.dot_general(left, right, (((1,), (1,)), ((), ())), preferred_element_type=F32)


def tn(left, right):
    return lax.dot_general(left, right, (((0,), (0,)), ((), ())), preferred_element_type=F32)


def hot_columns(row, count):
    sub = lax.broadcasted_iota(jnp.int32, (count, row.shape[1]), 0)
    return jnp.where(sub == row, 1.0, 0.0).astype(BF16)


def silu_parts(half):
    tan = jnp.tanh(half)
    part = half * tan
    return half + part, (1.0 + tan) * ((1.0 + half) - part)


def first_kernel(out):
    out[...] = jnp.zeros_like(out)


def pack_kernel(_, nodes, leave, arrive, sends, to_up, far_up, to_down, far_down):
    rows = nodes.shape[1]
    migr = leave.shape[1] // 2
    border = sends.shape[1] // 2
    own = nodes[0]
    leaving = tn(hot_columns(leave[...], rows), own).astype(BF16)
    sub = lax.broadcasted_iota(jnp.int32, (rows, 2 * border), 0)
    column = jnp.transpose(
        jnp.broadcast_to(arrive[...].astype(F32), (2 * border, rows)), (1, 0)
    )
    source = jnp.sum(jnp.where(sub == sends[...], column, 0.0), axis=0, keepdims=True)
    source = source.astype(jnp.int32)
    rest = tn(hot_columns(source, rows), own).astype(BF16)
    code = jnp.where(source >= rows, source - rows, -1).astype(F32)
    for out, far, part in ((to_down, far_down, 0), (to_up, far_up, 1)):
        out[:border] = rest[part * border : (part + 1) * border]
        moving = leaving[part * migr : (part + 1) * migr]
        out[border : border + migr] = moving
        far[:migr] = moving
        far[migr:] = jnp.zeros_like(far[migr:])
        shifted = code if part == 0 else pltpu.roll(code, border, 1)
        tail = out.shape[0] - border - migr
        out[border + migr :] = jnp.broadcast_to(shifted, (tail, 2 * border)).astype(BF16)


def prep_kernel(nbr, valid, w_msg, w_out, cotangent, hot_o, hot_t_o, wide_o, ids_o, d_hid_o):
    slots, rows = nbr.shape[1:]
    width = w_msg.shape[0]
    half_rows, hot_rows = hot_t_o.shape[0], hot_o.shape[1]
    chunk = 4
    half_msg = 0.5 * w_msg[...].astype(F32)
    none = jnp.zeros((width, width), F32)
    for part, block in enumerate((half_msg, jnp.transpose(half_msg, (1, 0)))):
        wide_o[part] = jnp.concatenate(
            [
                jnp.concatenate([block, none], axis=1),
                jnp.concatenate([none, block], axis=1),
            ],
            axis=0,
        ).astype(BF16)
    d_hid_o[...] = nt(cotangent[0], w_out[...])
    upper = nbr[0] >= half_rows
    low_row = jnp.where(upper, nbr[0] - half_rows, nbr[0])
    index = jnp.where(valid[0] == 1, low_row, half_rows) + jnp.where(upper, hot_rows, 0)
    fill = jnp.zeros((LANES - slots, rows), jnp.int32)
    ids_o[...] = jnp.transpose(jnp.concatenate([index, fill], axis=0), (1, 0))

    lane = lax.broadcasted_iota(jnp.int32, (rows, hot_rows), 1).astype(jnp.int16)
    one = jnp.ones((rows, hot_rows), BF16)
    zero = jnp.zeros((rows, hot_rows), BF16)
    sub = lax.broadcasted_iota(jnp.int32, (half_rows, rows), 0).astype(jnp.int16)
    one_t = jnp.ones((half_rows, rows), BF16)
    zero_t = jnp.zeros((half_rows, rows), BF16)

    @pl.loop(0, slots // chunk)
    def build(step):
        for j, short in enumerate(slot_ids(ids_o, step, chunk)):
            slot = step * chunk + j
            short = (short & (hot_rows - 1)).astype(jnp.int16)
            short = jnp.concatenate([short] * (hot_rows // LANES), axis=1)
            hot_o[pl.ds(slot * rows, rows)] = jnp.where(short == lane, one, zero)
            row = nbr[0, pl.ds(slot, 1)]
            row = jnp.where(row >= half_rows, row - half_rows, row)
            short = jnp.broadcast_to(row, (16, rows)).astype(jnp.int16)
            short = jnp.concatenate([short] * (half_rows // 16), axis=0)
            hot_t_o[:, pl.ds(pl.multiple_of(slot * rows, LANES), rows)] = jnp.where(
                short == sub, one_t, zero_t
            )


def slot_ids(ids, step, chunk):
    near = pltpu.roll(ids[...], lax.rem(LANES - step * chunk, LANES), 1)
    shape = (ids.shape[0], LANES)
    return [jnp.broadcast_to(near[:, j : j + 1], shape) for j in range(chunk)]


def layer_kernel(
    nodes,
    arrive,
    my_up,
    my_down,
    low,
    low_far,
    high,
    high_far,
    hot,
    hot_t,
    wide,
    nbr_ids,
    d_hid,
    w_send,
    w_recv,
    w_self,
    w_agg,
    w_out,
    cotangent,
    updated,
    back_low,
    back_high,
    grads,
    d_node_o,
    d_centre_o,
    d_neigh_o,
    neigh_s,
    hid_s,
    ds1_s,
    ds2_s,
    agg_s,
    dcen_s,
    dneigh_s,
    gmsg_s,
):
    rows, width = nodes.shape[1:]
    slots = hot.shape[0] // rows
    border = back_low.shape[0]
    migr = low.shape[0] - border - CODE_ROWS
    table_rows = rows + 2 * border
    chunk = 2 * PAIRS
    steps = slots // chunk

    pool = jnp.concatenate(
        [nodes[0], low[border : border + migr], high[border : border + migr]], axis=0
    )
    moved = tn(hot_columns(arrive[...], pool.shape[0]), pool).astype(BF16)

    def halo(message, first, second):
        code = message[border + migr : border + migr + 8].astype(F32)[:1]
        code = code.astype(jnp.int32)
        source = jnp.concatenate([first, second], axis=0)
        extra = tn(hot_columns(code, 2 * migr), source)
        return (message[:border].astype(F32) + extra[:border]).astype(BF16)

    below = halo(low[...], low_far[:migr], my_down[border : border + migr])
    above = halo(high[...], my_up[border : border + migr], high_far[:migr])
    table = jnp.concatenate([moved, below, above], axis=0)

    half_rows, hot_rows = hot_t.shape[0], hot.shape[1]
    half_centre = 0.5 * nn(moved, w_send[...])
    half_neigh = (0.5 * nn(table, w_recv[...]).astype(BF16).astype(F32)).astype(BF16)
    neigh_s[:half_rows] = jnp.concatenate([half_neigh[:half_rows], half_neigh[half_rows:]], axis=1)
    neigh_s[half_rows:] = jnp.full((hot_rows - half_rows, 2 * width), FAR, BF16)
    agg_s[...] = jnp.zeros_like(agg_s)

    @pl.loop(0, steps)
    def forward(step):
        ids = slot_ids(nbr_ids, step, chunk)
        gathered = nn(hot[pl.ds(step * (chunk * rows), chunk * rows)], neigh_s[...])
        base = step * (PAIRS * rows)
        for p in range(PAIRS):
            for side in range(2):
                cols = slice(side * width, (side + 1) * width)
                j = 2 * p + side
                pick = gathered[j * rows : (j + 1) * rows]
                pick = jnp.where(ids[j] >= hot_rows, pick[:, width:], pick[:, :width])
                act, slope = silu_parts(half_centre + pick)
                span = pl.ds(base + p * rows, rows)
                ds1_s[span, cols] = slope
                hid_s[span, cols] = act.astype(BF16)
        halves = nn(hid_s[pl.ds(base, PAIRS * rows)], wide[0])
        total = agg_s[...]
        for p in range(PAIRS):
            for side in range(2):
                cols = slice(side * width, (side + 1) * width)
                act, slope = silu_parts(halves[p * rows : (p + 1) * rows, cols])
                total = total + act
                ds2_s[pl.ds(base + p * rows, rows), cols] = slope
        agg_s[...] = total

    agg_b = agg_s[...].astype(BF16)
    node_pre = nn(moved, w_self[...]) + nn(agg_b, w_agg[...])
    act, slope = silu_parts(0.5 * node_pre)
    node_hid = act.astype(BF16)
    updated[0] = (moved.astype(F32) + nn(node_hid, w_out[...])).astype(BF16)
    cot = cotangent[0]
    d_node = (d_hid[...] * (0.5 * slope)).astype(BF16)
    half_d_agg = 0.5 * nt(d_node, w_agg[...])

    dcen_s[...] = jnp.zeros_like(dcen_s)
    dneigh_s[...] = jnp.zeros_like(dneigh_s)
    gmsg_s[...] = jnp.zeros_like(gmsg_s)
    none = jnp.zeros((rows, width), BF16)
    border_id = jnp.full((rows, width), hot_rows, jnp.int16)

    @pl.loop(0, steps)
    def backward(step):
        ids = slot_ids(nbr_ids, step, chunk)
        span = pl.ds(step * (PAIRS * rows), PAIRS * rows)
        d_agg = jnp.concatenate([half_d_agg, half_d_agg], axis=1)
        d_agg = jnp.concatenate([d_agg] * PAIRS, axis=0)
        d_pre2 = (d_agg * ds2_s[span]).astype(BF16)
        d_pre = nn(d_pre2, wide[1]) * ds1_s[span]
        gmsg_s[...] += tn(hid_s[span], d_pre2)
        total = dcen_s[...]
        wides = []
        for j in range(chunk):
            p, side = divmod(j, 2)
            part = d_pre[p * rows : (p + 1) * rows, side * width : (side + 1) * width]
            total = total + part
            part = part.astype(BF16)
            is_up = ids[j].astype(jnp.int16) >= border_id
            wides.append(
                jnp.concatenate(
                    [jnp.where(is_up, none, part), jnp.where(is_up, part, none)], axis=1
                )
            )
        dcen_s[...] = total
        edges = pl.ds(pl.multiple_of(step * (chunk * rows), LANES), chunk * rows)
        dneigh_s[...] += nn(hot_t[:, edges], jnp.concatenate(wides, axis=0))

    d_centre = dcen_s[...].astype(BF16)
    d_neigh = dneigh_s[...].astype(BF16)
    d_neigh = jnp.concatenate([d_neigh[:, :width], d_neigh[:, width:]], axis=0)
    d_borrowed = nt(d_neigh[rows:], w_recv[...]).astype(BF16)
    back_low[...] = d_borrowed[:border]
    back_high[...] = d_borrowed[border:]
    d_node_o[...] = d_node
    d_centre_o[...] = d_centre
    d_neigh_o[...] = d_neigh[:rows]
    parts = (
        tn(moved, d_centre),
        tn(table, d_neigh),
        gmsg_s[:width, :width] + gmsg_s[width:, width:],
        tn(moved, d_node),
        tn(agg_b, d_node),
        tn(node_hid, cot),
    )
    for m, part in enumerate(parts):
        grads[m * width : (m + 1) * width] = part.astype(BF16)
    used = len(parts) * width
    if grads.shape[0] > used:
        grads[used:] = jnp.zeros_like(grads[used:])


def finish_kernel(
    cotangent, d_node, d_centre, d_neigh, w_self, w_send, w_recv, sends, from_low, from_high, out
):
    rows = d_node.shape[0]
    returned = jnp.concatenate([from_low[...], from_high[...]], axis=0)
    out[0] = (
        cotangent[0].astype(F32)
        + nt(d_node[...], w_self[...])
        + nt(d_centre[...], w_send[...])
        + nt(d_neigh[...], w_recv[...])
        + nn(hot_columns(sends[...], rows), returned)
    ).astype(BF16)


def sum_kernel(parts, out):
    total = jnp.sum(parts[...].astype(F32), axis=0).astype(BF16)
    out[...] = jnp.broadcast_to(total[None], out.shape)


def norm_kernel(total, steps):
    count, width = steps.shape[0], steps.shape[1]
    for m in range(count):
        part = total[m * width : (m + 1) * width].astype(F32)
        mean = jnp.sum(jnp.sum(part * part, axis=0, keepdims=True), axis=1, keepdims=True)
        mean = mean / (part.shape[0] * part.shape[1])
        steps[m] = part / jnp.sqrt(mean + 1e-06)


def call(kernel, outs, scratch=()):
    return pl.pallas_call(
        kernel,
        out_shape=[jax.ShapeDtypeStruct(shape, kind) for shape, kind in outs],
        scratch_shapes=scratch,
        compiler_params=pltpu.CompilerParams(vmem_limit_bytes=40 * 1024 * 1024),
        cost_estimate=pl.CostEstimate(flops=2 * 10**9, bytes_accessed=1024, transcendentals=0),
    )


def shards(
    nodes,
    leave_list,
    arrive_list,
    send_list,
    neighbours,
    valid,
    w_send,
    w_recv,
    w_msg,
    w_self,
    w_agg,
    w_out,
    cotangent,
):
    rows, width = nodes.shape[1:]
    slots = neighbours.shape[2]
    migr = leave_list.shape[1] // 2
    border = send_list.shape[1] // 2
    table_rows = rows + 2 * border
    size = lax.axis_size("slab")
    devices = size * lax.axis_size("grp")
    axes = ("grp", "slab")

    def shift(array, by):
        return lax.ppermute(array, "slab", [(i, (i + by) % size) for i in range(size)])

    message = (border + migr + CODE_ROWS, width)
    message_down = (message[0] + CODE_ROWS, width)
    (token,) = call(first_kernel, [((8, LANES), F32)])()
    to_up, far_up, to_down, far_down = call(
        pack_kernel,
        [(message, BF16)] * 2 + [(message_down, BF16)] * 2,
    )(token, nodes, leave_list, arrive_list, send_list)
    low, low_far = shift(to_up, 1), shift(far_up, 2)
    high, high_far = shift(to_down, -1), shift(far_down, -2)

    matrices = 6
    pair_rows = rows * slots // 2
    half_rows = table_rows // 2
    hot_rows = -(-(half_rows + 1) // LANES) * LANES
    share = -(-matrices * width // (8 * devices)) * 8
    edges = rows * slots
    hot, hot_t, wide, ids, d_hid = call(
        prep_kernel,
        [
            ((edges, hot_rows), BF16),
            ((half_rows, edges), BF16),
            ((2, 2 * width, 2 * width), BF16),
            ((rows, LANES), jnp.int32),
            ((rows, width), F32),
        ],
    )(jnp.swapaxes(neighbours, 1, 2), jnp.swapaxes(valid, 1, 2), w_msg, w_out, cotangent)
    sources = (
        nodes,
        arrive_list,
        to_up,
        to_down,
        low,
        low_far,
        high,
        high_far,
        hot,
        hot_t,
        wide,
        ids,
        d_hid,
        w_send,
        w_recv,
        w_self,
        w_agg,
        w_out,
        cotangent,
    )
    updated, back_low, back_high, grads, d_node, d_centre, d_neigh = call(
        layer_kernel,
        [
            ((1, rows, width), BF16),
            ((border, width), BF16),
            ((border, width), BF16),
            ((devices * share, width), BF16),
            ((rows, width), BF16),
            ((rows, width), BF16),
            ((rows, width), BF16),
        ],
        [
            pltpu.VMEM((hot_rows, 2 * width), BF16),
            pltpu.VMEM((pair_rows, 2 * width), BF16),
            pltpu.VMEM((pair_rows, 2 * width), F32),
            pltpu.VMEM((pair_rows, 2 * width), F32),
            pltpu.VMEM((rows, width), F32),
            pltpu.VMEM((rows, width), F32),
            pltpu.VMEM((half_rows, 2 * width), F32),
            pltpu.VMEM((2 * width, 2 * width), F32),
        ],
    )(*sources)
    from_low = shift(back_high, 1)
    from_high = shift(back_low, -1)
    parts = lax.all_to_all(
        grads.reshape(devices, share, width), axes, split_axis=0, concat_axis=0, tiled=True
    )
    sources = (
        cotangent,
        d_node,
        d_centre,
        d_neigh,
        w_self,
        w_send,
        w_recv,
        send_list,
        from_low,
        from_high,
    )
    (grad_nodes,) = call(
        finish_kernel,
        [((1, rows, width), BF16)],
    )(*sources)
    (shared,) = call(sum_kernel, [((devices, share, width), BF16)])(parts)
    total = lax.all_to_all(shared, axes, split_axis=0, concat_axis=0, tiled=True)
    total = total.reshape(devices * share, width)[: matrices * width]
    (weight_steps,) = call(norm_kernel, [((matrices, width, width), F32)])(total)
    return (updated, grad_nodes, weight_steps)


def solution(mesh):
    rows = P("grp", "slab", None)
    lists = P("grp", "slab")
    in_specs = (rows, lists, lists, lists, rows, rows, P(), P(), P(), P(), P(), P(), rows)
    out_specs = (rows, rows, P())
    return jax.shard_map(shards, mesh=mesh, in_specs=in_specs, out_specs=out_specs, check_vma=False)
```

```python
import functools

import jax
import jax.numpy as jnp
from jax import lax
from jax.experimental import pallas as pl
from jax.experimental.pallas import tpu as pltpu
from jax.sharding import PartitionSpec as P

F32 = jnp.float32
BF16 = jnp.bfloat16
CODE_ROWS = 16
LANES = 128
FAR = -1e30
PAIRS = 16


def nn(left, right):
    return lax.dot_general(left, right, (((1,), (0,)), ((), ())), preferred_element_type=F32)


def nt(left, right):
    return lax.dot_general(left, right, (((1,), (1,)), ((), ())), preferred_element_type=F32)


def tn(left, right):
    return lax.dot_general(left, right, (((0,), (0,)), ((), ())), preferred_element_type=F32)


def hot_columns(row, count):
    sub = lax.broadcasted_iota(jnp.int32, (count, row.shape[1]), 0)
    return jnp.where(sub == row, 1.0, 0.0).astype(BF16)


def silu_parts(half):
    tan = jnp.tanh(half)
    part = half * tan
    return half + part, (1.0 + tan) * ((1.0 + half) - part)


def first_kernel(out):
    out[...] = jnp.zeros_like(out)


def pack_kernel(_, nodes, leave, arrive, sends, to_up, far_up, to_down, far_down):
    rows = nodes.shape[1]
    migr = leave.shape[1] // 2
    border = sends.shape[1] // 2
    own = nodes[0]
    leaving = tn(hot_columns(leave[...], rows), own).astype(BF16)
    sub = lax.broadcasted_iota(jnp.int32, (rows, 2 * border), 0)
    column = jnp.transpose(
        jnp.broadcast_to(arrive[...].astype(F32), (2 * border, rows)), (1, 0)
    )
    source = jnp.sum(jnp.where(sub == sends[...], column, 0.0), axis=0, keepdims=True)
    source = source.astype(jnp.int32)
    rest = tn(hot_columns(source, rows), own).astype(BF16)
    code = jnp.where(source >= rows, source - rows, -1).astype(F32)
    for out, far, part in ((to_down, far_down, 0), (to_up, far_up, 1)):
        out[:border] = rest[part * border : (part + 1) * border]
        moving = leaving[part * migr : (part + 1) * migr]
        out[border : border + migr] = moving
        far[:migr] = moving
        far[migr:] = jnp.zeros_like(far[migr:])
        shifted = code if part == 0 else pltpu.roll(code, border, 1)
        tail = out.shape[0] - border - migr
        out[border + migr :] = jnp.broadcast_to(shifted, (tail, 2 * border)).astype(BF16)


def prep_kernel(nbr, valid, w_msg, w_out, cotangent, hot_o, hot_t_o, wide_o, ids_o, d_hid_o):
    slots, rows = nbr.shape[1:]
    width = w_msg.shape[0]
    half_rows, hot_rows = hot_t_o.shape[0], hot_o.shape[1]
    chunk = 4
    half_msg = 0.5 * w_msg[...].astype(F32)
    none = jnp.zeros((width, width), F32)
    for part, block in enumerate((half_msg, jnp.transpose(half_msg, (1, 0)))):
        wide_o[part] = jnp.concatenate(
            [
                jnp.concatenate([block, none], axis=1),
                jnp.concatenate([none, block], axis=1),
            ],
            axis=0,
        ).astype(BF16)
    d_hid_o[...] = nt(cotangent[0], w_out[...])
    upper = nbr[0] >= half_rows
    low_row = jnp.where(upper, nbr[0] - half_rows, nbr[0])
    index = jnp.where(valid[0] == 1, low_row, half_rows) + jnp.where(upper, hot_rows, 0)
    fill = jnp.zeros((LANES - slots, rows), jnp.int32)
    ids_o[...] = jnp.transpose(jnp.concatenate([index, fill], axis=0), (1, 0))

    lane = lax.broadcasted_iota(jnp.int32, (rows, hot_rows), 1).astype(jnp.int16)
    one = jnp.ones((rows, hot_rows), BF16)
    zero = jnp.zeros((rows, hot_rows), BF16)
    sub = lax.broadcasted_iota(jnp.int32, (half_rows, rows), 0).astype(jnp.int16)
    one_t = jnp.ones((half_rows, rows), BF16)
    zero_t = jnp.zeros((half_rows, rows), BF16)

    @pl.loop(0, slots // chunk)
    def build(step):
        for j, short in enumerate(slot_ids(ids_o, step, chunk)):
            slot = step * chunk + j
            short = (short & (hot_rows - 1)).astype(jnp.int16)
            short = jnp.concatenate([short] * (hot_rows // LANES), axis=1)
            hot_o[pl.ds(slot * rows, rows)] = jnp.where(short == lane, one, zero)
            row = nbr[0, pl.ds(slot, 1)]
            row = jnp.where(row >= half_rows, row - half_rows, row)
            short = jnp.broadcast_to(row, (16, rows)).astype(jnp.int16)
            short = jnp.concatenate([short] * (half_rows // 16), axis=0)
            hot_t_o[:, pl.ds(pl.multiple_of(slot * rows, LANES), rows)] = jnp.where(
                short == sub, one_t, zero_t
            )


def slot_ids(ids, step, chunk):
    near = pltpu.roll(ids[...], lax.rem(LANES - step * chunk, LANES), 1)
    shape = (ids.shape[0], LANES)
    return [jnp.broadcast_to(near[:, j : j + 1], shape) for j in range(chunk)]


def layer_kernel(
    nodes,
    arrive,
    my_up,
    my_down,
    low,
    low_far,
    high,
    high_far,
    hot,
    hot_t,
    wide,
    nbr_ids,
    d_hid,
    w_send,
    w_recv,
    w_self,
    w_agg,
    w_out,
    cotangent,
    updated,
    back_low,
    back_high,
    grads,
    d_node_o,
    d_centre_o,
    d_neigh_o,
    neigh_s,
    hid_s,
    ds1_s,
    ds2_s,
    agg_s,
    dcen_s,
    dneigh_s,
    gmsg_s,
):
    rows, width = nodes.shape[1:]
    slots = hot.shape[0] // rows
    border = back_low.shape[0]
    migr = low.shape[0] - border - CODE_ROWS
    table_rows = rows + 2 * border
    chunk = 2 * PAIRS
    steps = slots // chunk

    pool = jnp.concatenate(
        [nodes[0], low[border : border + migr], high[border : border + migr]], axis=0
    )
    moved = tn(hot_columns(arrive[...], pool.shape[0]), pool).astype(BF16)

    def halo(message, first, second):
        code = message[border + migr : border + migr + 8].astype(F32)[:1]
        code = code.astype(jnp.int32)
        source = jnp.concatenate([first, second], axis=0)
        extra = tn(hot_columns(code, 2 * migr), source)
        return (message[:border].astype(F32) + extra[:border]).astype(BF16)

    below = halo(low[...], low_far[:migr], my_down[border : border + migr])
    above = halo(high[...], my_up[border : border + migr], high_far[:migr])
    table = jnp.concatenate([moved, below, above], axis=0)

    half_rows, hot_rows = hot_t.shape[0], hot.shape[1]
    half_centre = 0.5 * nn(moved, w_send[...])
    half_neigh = (0.5 * nn(table, w_recv[...]).astype(BF16).astype(F32)).astype(BF16)
    neigh_s[:half_rows] = jnp.concatenate([half_neigh[:half_rows], half_neigh[half_rows:]], axis=1)
    neigh_s[half_rows:] = jnp.full((hot_rows - half_rows, 2 * width), FAR, BF16)
    agg_s[...] = jnp.zeros_like(agg_s)

    @pl.loop(0, steps)
    def forward(step):
        ids = slot_ids(nbr_ids, step, chunk)
        gathered = nn(hot[pl.ds(step * (chunk * rows), chunk * rows)], neigh_s[...])
        base = step * (PAIRS * rows)
        for p in range(PAIRS):
            for side in range(2):
                cols = slice(side * width, (side + 1) * width)
                j = 2 * p + side
                pick = gathered[j * rows : (j + 1) * rows]
                pick = jnp.where(ids[j] >= hot_rows, pick[:, width:], pick[:, :width])
                act, slope = silu_parts(half_centre + pick)
                span = pl.ds(base + p * rows, rows)
                ds1_s[span, cols] = slope
                hid_s[span, cols] = act.astype(BF16)
        halves = nn(hid_s[pl.ds(base, PAIRS * rows)], wide[0])
        total = agg_s[...]
        for p in range(PAIRS):
            for side in range(2):
                cols = slice(side * width, (side + 1) * width)
                act, slope = silu_parts(halves[p * rows : (p + 1) * rows, cols])
                total = total + act
                ds2_s[pl.ds(base + p * rows, rows), cols] = slope
        agg_s[...] = total

    agg_b = agg_s[...].astype(BF16)
    node_pre = nn(moved, w_self[...]) + nn(agg_b, w_agg[...])
    act, slope = silu_parts(0.5 * node_pre)
    node_hid = act.astype(BF16)
    updated[0] = (moved.astype(F32) + nn(node_hid, w_out[...])).astype(BF16)
    cot = cotangent[0]
    d_node = (d_hid[...] * (0.5 * slope)).astype(BF16)
    half_d_agg = 0.5 * nt(d_node, w_agg[...])

    dcen_s[...] = jnp.zeros_like(dcen_s)
    dneigh_s[...] = jnp.zeros_like(dneigh_s)
    gmsg_s[...] = jnp.zeros_like(gmsg_s)
    none = jnp.zeros((rows, width), BF16)
    border_id = jnp.full((rows, width), hot_rows, jnp.int16)

    @pl.loop(0, steps)
    def backward(step):
        ids = slot_ids(nbr_ids, step, chunk)
        span = pl.ds(step * (PAIRS * rows), PAIRS * rows)
        d_agg = jnp.concatenate([half_d_agg, half_d_agg], axis=1)
        d_agg = jnp.concatenate([d_agg] * PAIRS, axis=0)
        d_pre2 = (d_agg * ds2_s[span]).astype(BF16)
        d_pre = nn(d_pre2, wide[1]) * ds1_s[span]
        gmsg_s[...] += tn(hid_s[span], d_pre2)
        total = dcen_s[...]
        wides = []
        for j in range(chunk):
            p, side = divmod(j, 2)
            part = d_pre[p * rows : (p + 1) * rows, side * width : (side + 1) * width]
            total = total + part
            part = part.astype(BF16)
            is_up = ids[j].astype(jnp.int16) >= border_id
            wides.append(
                jnp.concatenate(
                    [jnp.where(is_up, none, part), jnp.where(is_up, part, none)], axis=1
                )
            )
        dcen_s[...] = total
        edges = pl.ds(pl.multiple_of(step * (chunk * rows), LANES), chunk * rows)
        dneigh_s[...] += nn(hot_t[:, edges], jnp.concatenate(wides, axis=0))

    d_centre = dcen_s[...].astype(BF16)
    d_neigh = dneigh_s[...].astype(BF16)
    d_neigh = jnp.concatenate([d_neigh[:, :width], d_neigh[:, width:]], axis=0)
    d_borrowed = nt(d_neigh[rows:], w_recv[...]).astype(BF16)
    back_low[...] = d_borrowed[:border]
    back_high[...] = d_borrowed[border:]
    d_node_o[...] = d_node
    d_centre_o[...] = d_centre
    d_neigh_o[...] = d_neigh[:rows]
    parts = (
        tn(moved, d_centre),
        tn(table, d_neigh),
        gmsg_s[:width, :width] + gmsg_s[width:, width:],
        tn(moved, d_node),
        tn(agg_b, d_node),
        tn(node_hid, cot),
    )
    for m, part in enumerate(parts):
        grads[m * width : (m + 1) * width] = part.astype(BF16)
    used = len(parts) * width
    if grads.shape[0] > used:
        grads[used:] = jnp.zeros_like(grads[used:])


def finish_kernel(
    cotangent, d_node, d_centre, d_neigh, w_self, w_send, w_recv, sends, from_low, from_high, out
):
    rows = d_node.shape[0]
    returned = jnp.concatenate([from_low[...], from_high[...]], axis=0)
    out[0] = (
        cotangent[0].astype(F32)
        + nt(d_node[...], w_self[...])
        + nt(d_centre[...], w_send[...])
        + nt(d_neigh[...], w_recv[...])
        + nn(hot_columns(sends[...], rows), returned)
    ).astype(BF16)


def sum_kernel(parts, out):
    total = jnp.sum(parts[...].astype(F32), axis=0).astype(BF16)
    out[...] = jnp.broadcast_to(total[None], out.shape)


def norm_kernel(total, steps):
    count, width = steps.shape[0], steps.shape[1]
    for m in range(count):
        part = total[m * width : (m + 1) * width].astype(F32)
        mean = jnp.sum(jnp.sum(part * part, axis=0, keepdims=True), axis=1, keepdims=True)
        mean = mean / (part.shape[0] * part.shape[1])
        steps[m] = part / jnp.sqrt(mean + 1e-06)


def call(kernel, outs, scratch=()):
    return pl.pallas_call(
        kernel,
        out_shape=[jax.ShapeDtypeStruct(shape, kind) for shape, kind in outs],
        scratch_shapes=scratch,
        compiler_params=pltpu.CompilerParams(vmem_limit_bytes=40 * 1024 * 1024),
        cost_estimate=pl.CostEstimate(flops=2 * 10**9, bytes_accessed=1024, transcendentals=0),
    )


def shards(
    nodes,
    leave_list,
    arrive_list,
    send_list,
    neighbours,
    valid,
    w_send,
    w_recv,
    w_msg,
    w_self,
    w_agg,
    w_out,
    cotangent,
):
    rows, width = nodes.shape[1:]
    slots = neighbours.shape[2]
    migr = leave_list.shape[1] // 2
    border = send_list.shape[1] // 2
    table_rows = rows + 2 * border
    size = lax.axis_size("slab")
    devices = size * lax.axis_size("grp")
    axes = ("grp", "slab")

    def shift(array, by):
        return lax.ppermute(array, "slab", [(i, (i + by) % size) for i in range(size)])

    message = (border + migr + CODE_ROWS, width)
    message_down = (message[0] + CODE_ROWS, width)
    (token,) = call(first_kernel, [((8, LANES), F32)])()
    to_up, far_up, to_down, far_down = call(
        pack_kernel,
        [(message, BF16)] * 2 + [(message_down, BF16)] * 2,
    )(token, nodes, leave_list, arrive_list, send_list)
    low, low_far = shift(to_up, 1), shift(far_up, 2)
    high, high_far = shift(to_down, -1), shift(far_down, -2)

    matrices = 6
    pair_rows = rows * slots // 2
    half_rows = table_rows // 2
    hot_rows = -(-(half_rows + 1) // LANES) * LANES
    share = -(-matrices * width // (8 * devices)) * 8
    edges = rows * slots
    hot, hot_t, wide, ids, d_hid = call(
        prep_kernel,
        [
            ((edges, hot_rows), BF16),
            ((half_rows, edges), BF16),
            ((2, 2 * width, 2 * width), BF16),
            ((rows, LANES), jnp.int32),
            ((rows, width), F32),
        ],
    )(jnp.swapaxes(neighbours, 1, 2), jnp.swapaxes(valid, 1, 2), w_msg, w_out, cotangent)
    sources = (
        nodes,
        arrive_list,
        to_up,
        to_down,
        low,
        low_far,
        high,
        high_far,
        hot,
        hot_t,
        wide,
        ids,
        d_hid,
        w_send,
        w_recv,
        w_self,
        w_agg,
        w_out,
        cotangent,
    )
    updated, back_low, back_high, grads, d_node, d_centre, d_neigh = call(
        layer_kernel,
        [
            ((1, rows, width), BF16),
            ((border, width), BF16),
            ((border, width), BF16),
            ((devices * share, width), BF16),
            ((rows, width), BF16),
            ((rows, width), BF16),
            ((rows, width), BF16),
        ],
        [
            pltpu.VMEM((hot_rows, 2 * width), BF16),
            pltpu.VMEM((pair_rows, 2 * width), BF16),
            pltpu.VMEM((pair_rows, 2 * width), F32),
            pltpu.VMEM((pair_rows, 2 * width), F32),
            pltpu.VMEM((rows, width), F32),
            pltpu.VMEM((rows, width), F32),
            pltpu.VMEM((half_rows, 2 * width), F32),
            pltpu.VMEM((2 * width, 2 * width), F32),
        ],
    )(*sources)
    from_low = shift(back_high, 1)
    from_high = shift(back_low, -1)
    parts = lax.all_to_all(
        grads.reshape(devices, share, width), axes, split_axis=0, concat_axis=0, tiled=True
    )
    sources = (
        cotangent,
        d_node,
        d_centre,
        d_neigh,
        w_self,
        w_send,
        w_recv,
        send_list,
        from_low,
        from_high,
    )
    (grad_nodes,) = call(
        finish_kernel,
        [((1, rows, width), BF16)],
    )(*sources)
    (shared,) = call(sum_kernel, [((devices, share, width), BF16)])(parts)
    total = lax.all_to_all(shared, axes, split_axis=0, concat_axis=0, tiled=True)
    total = total.reshape(devices * share, width)[: matrices * width]
    (weight_steps,) = call(norm_kernel, [((matrices, width, width), F32)])(total)
    return (updated, grad_nodes, weight_steps)


def solution(mesh):
    rows = P("grp", "slab", None)
    lists = P("grp", "slab")
    in_specs = (rows, lists, lists, lists, rows, rows, P(), P(), P(), P(), P(), P(), rows)
    out_specs = (rows, rows, P())
    return jax.shard_map(shards, mesh=mesh, in_specs=in_specs, out_specs=out_specs, check_vma=False)
```

```python
import functools

import jax
import jax.numpy as jnp
from jax import lax
from jax.experimental import pallas as pl
from jax.experimental.pallas import tpu as pltpu
from jax.sharding import PartitionSpec as P

F32 = jnp.float32
BF16 = jnp.bfloat16
CODE_ROWS = 16
LANES = 128
FAR = -1e30
GROUP = 4
BLOCK = 64


def nn(left, right):
    return lax.dot_general(left, right, (((1,), (0,)), ((), ())), preferred_element_type=F32)


def nt(left, right):
    return lax.dot_general(left, right, (((1,), (1,)), ((), ())), preferred_element_type=F32)


def tn(left, right):
    return lax.dot_general(left, right, (((0,), (0,)), ((), ())), preferred_element_type=F32)


def hot_columns(row, count):
    sub = lax.broadcasted_iota(jnp.int32, (count, row.shape[1]), 0)
    return jnp.where(sub == row, 1.0, 0.0).astype(BF16)


def silu_parts(half):
    tan = jnp.tanh(half)
    part = half * tan
    return half + part, (1.0 + tan) * ((1.0 + half) - part)


def first_kernel(out):
    out[...] = jnp.zeros_like(out)


def pack_kernel(_, nodes, leave, arrive, sends, to_up, far_up, to_down, far_down):
    rows = nodes.shape[1]
    migr = leave.shape[1] // 2
    border = sends.shape[1] // 2
    own = nodes[0]
    leaving = tn(hot_columns(leave[...], rows), own).astype(BF16)
    sub = lax.broadcasted_iota(jnp.int32, (rows, 2 * border), 0)
    column = jnp.transpose(
        jnp.broadcast_to(arrive[...].astype(F32), (2 * border, rows)), (1, 0)
    )
    source = jnp.sum(jnp.where(sub == sends[...], column, 0.0), axis=0, keepdims=True)
    source = source.astype(jnp.int32)
    rest = tn(hot_columns(source, rows), own).astype(BF16)
    code = jnp.where(source >= rows, source - rows, -1).astype(F32)
    for out, far, part in ((to_down, far_down, 0), (to_up, far_up, 1)):
        out[:border] = rest[part * border : (part + 1) * border]
        moving = leaving[part * migr : (part + 1) * migr]
        out[border : border + migr] = moving
        far[:migr] = moving
        far[migr:] = jnp.zeros_like(far[migr:])
        shifted = code if part == 0 else pltpu.roll(code, border, 1)
        tail = out.shape[0] - border - migr
        out[border + migr :] = jnp.broadcast_to(shifted, (tail, 2 * border)).astype(BF16)


def prep_kernel(nbr, valid, w_msg, w_out, cotangent, hot_o, hot_t_o, wide_o, ids_o, d_hid_o):
    slots, rows = nbr.shape[1:]
    width = w_msg.shape[0]
    half_rows, hot_rows = hot_t_o.shape[0], hot_o.shape[1]
    chunk = 4
    half_msg = 0.5 * w_msg[...].astype(F32)
    none = jnp.zeros((width, width), F32)
    for part, block in enumerate((half_msg, jnp.transpose(half_msg, (1, 0)))):
        wide_o[part] = jnp.concatenate(
            [
                jnp.concatenate([block, none], axis=1),
                jnp.concatenate([none, block], axis=1),
            ],
            axis=0,
        ).astype(BF16)
    d_hid_o[...] = nt(cotangent[0], w_out[...])
    upper = nbr[0] >= half_rows
    low_row = jnp.where(upper, nbr[0] - half_rows, nbr[0])
    index = jnp.where(valid[0] == 1, low_row, half_rows) + jnp.where(upper, hot_rows, 0)
    fill = jnp.zeros((LANES - slots, rows), jnp.int32)
    ids_o[...] = jnp.transpose(jnp.concatenate([index, fill], axis=0), (1, 0))

    lane = lax.broadcasted_iota(jnp.int32, (rows, hot_rows), 1).astype(jnp.int16)
    one = jnp.ones((rows, hot_rows), BF16)
    zero = jnp.zeros((rows, hot_rows), BF16)
    sub = lax.broadcasted_iota(jnp.int32, (half_rows, rows), 0).astype(jnp.int16)
    one_t = jnp.ones((half_rows, rows), BF16)
    zero_t = jnp.zeros((half_rows, rows), BF16)

    @pl.loop(0, slots // chunk)
    def build(step):
        for j, short in enumerate(slot_ids(ids_o, step, chunk)):
            slot = step * chunk + j
            short = (short & (hot_rows - 1)).astype(jnp.int16)
            short = jnp.concatenate([short] * (hot_rows // LANES), axis=1)
            hot_o[pl.ds(slot * rows, rows)] = jnp.where(short == lane, one, zero)
            row = nbr[0, pl.ds(slot, 1)]
            row = jnp.where(row >= half_rows, row - half_rows, row)
            short = jnp.broadcast_to(row, (16, rows)).astype(jnp.int16)
            short = jnp.concatenate([short] * (half_rows // 16), axis=0)
            hot_t_o[:, pl.ds(pl.multiple_of(slot * rows, LANES), rows)] = jnp.where(
                short == sub, one_t, zero_t
            )


def slot_ids(ids, step, chunk):
    near = pltpu.roll(ids[...], lax.rem(LANES - step * chunk, LANES), 1)
    shape = (ids.shape[0], LANES)
    return [jnp.broadcast_to(near[:, j : j + 1], shape) for j in range(chunk)]


def layer_kernel(
    nodes,
    arrive,
    my_up,
    my_down,
    low,
    low_far,
    high,
    high_far,
    hot,
    hot_t,
    wide,
    nbr_ids,
    d_hid,
    w_send,
    w_recv,
    w_self,
    w_agg,
    w_out,
    cotangent,
    updated,
    back_low,
    back_high,
    grads,
    d_node_o,
    d_centre_o,
    d_neigh_o,
    neigh_s,
    hid_s,
    ds1_s,
    ds2_s,
    agg_s,
    dcen_s,
    dpre2_s,
    dpre_s,
):
    rows, width = nodes.shape[1:]
    slots = hot.shape[0] // rows
    border = back_low.shape[0]
    migr = low.shape[0] - border - CODE_ROWS
    table_rows = rows + 2 * border

    pool = jnp.concatenate(
        [nodes[0], low[border : border + migr], high[border : border + migr]], axis=0
    )
    moved = tn(hot_columns(arrive[...], pool.shape[0]), pool).astype(BF16)

    def halo(message, first, second):
        code = message[border + migr : border + migr + 8].astype(F32)[:1]
        code = code.astype(jnp.int32)
        source = jnp.concatenate([first, second], axis=0)
        extra = tn(hot_columns(code, 2 * migr), source)
        return (message[:border].astype(F32) + extra[:border]).astype(BF16)

    below = halo(low[...], low_far[:migr], my_down[border : border + migr])
    above = halo(high[...], my_up[border : border + migr], high_far[:migr])
    table = jnp.concatenate([moved, below, above], axis=0)

    half_rows, hot_rows = hot_t.shape[0], hot.shape[1]
    half_centre = 0.5 * nn(moved, w_send[...])
    half_neigh = (0.5 * nn(table, w_recv[...]).astype(BF16).astype(F32)).astype(BF16)
    neigh_s[:half_rows] = jnp.concatenate([half_neigh[:half_rows], half_neigh[half_rows:]], axis=1)
    neigh_s[half_rows:] = jnp.full((hot_rows - half_rows, 2 * width), FAR, BF16)
    ids = slot_ids(nbr_ids, 0, slots)
    blocks = [slice(start, start + BLOCK) for start in range(0, rows, BLOCK)]
    sides = (slice(0, width), slice(width, 2 * width))

    for first in range(0, slots, GROUP):
        gathered = nn(hot[first * rows : (first + GROUP) * rows], neigh_s[...])
        for j in range(GROUP):
            pair, side = divmod(first + j, 2)
            for block in blocks:
                pick = gathered[j * rows + block.start : j * rows + block.stop]
                pick = jnp.where(
                    ids[first + j][block] >= hot_rows, pick[:, sides[1]], pick[:, sides[0]]
                )
                act, slope = silu_parts(half_centre[block] + pick)
                at = slice(pair * rows + block.start, pair * rows + block.stop)
                ds1_s[at, sides[side]] = slope
                hid_s[at, sides[side]] = act.astype(BF16)
        base = first // 2 * rows
        halves = nn(hid_s[base : base + GROUP // 2 * rows], wide[0])
        for block in blocks:
            total = jnp.zeros((BLOCK, width), F32) if first == 0 else agg_s[block]
            for j in range(GROUP):
                pair, side = divmod(j, 2)
                at = slice(pair * rows + block.start, pair * rows + block.stop)
                act, slope = silu_parts(halves[at, sides[side]])
                total = total + act
                ds2_s[base + at.start : base + at.stop, sides[side]] = slope
            agg_s[block] = total

    agg_b = agg_s[...].astype(BF16)
    node_pre = nn(moved, w_self[...]) + nn(agg_b, w_agg[...])
    act, slope = silu_parts(0.5 * node_pre)
    node_hid = act.astype(BF16)
    updated[0] = (moved.astype(F32) + nn(node_hid, w_out[...])).astype(BF16)
    cot = cotangent[0]
    d_node = (d_hid[...] * (0.5 * slope)).astype(BF16)
    half_d_agg = 0.5 * nt(d_node, w_agg[...])

    none = jnp.zeros((BLOCK, width), BF16)
    border_id = jnp.full((BLOCK, width), hot_rows, jnp.int16)
    for first in range(0, slots, GROUP):
        base = first // 2 * rows
        span = slice(base, base + GROUP // 2 * rows)
        for pair in range(GROUP // 2):
            for block in blocks:
                at = slice(base + pair * rows + block.start, base + pair * rows + block.stop)
                for side in sides:
                    dpre2_s[at, side] = (half_d_agg[block] * ds2_s[at, side]).astype(BF16)
        d_hids = nn(dpre2_s[span], wide[1])
        for block in blocks:
            total = jnp.zeros((BLOCK, width), F32) if first == 0 else dcen_s[block]
            for j in range(GROUP):
                pair, side = divmod(j, 2)
                at = slice(pair * rows + block.start, pair * rows + block.stop)
                part = d_hids[at, sides[side]] * ds1_s[base + at.start : base + at.stop, sides[side]]
                total = total + part
                part = part.astype(BF16)
                is_up = ids[first + j][block].astype(jnp.int16) >= border_id
                at = slice((first + j) * rows + block.start, (first + j) * rows + block.stop)
                dpre_s[at, sides[0]] = jnp.where(is_up, none, part)
                dpre_s[at, sides[1]] = jnp.where(is_up, part, none)
            dcen_s[block] = total
    gmsg = tn(hid_s[...], dpre2_s[...])
    d_neigh = nn(hot_t[...], dpre_s[...]).astype(BF16)

    d_centre = dcen_s[...].astype(BF16)
    d_neigh = jnp.concatenate([d_neigh[:, :width], d_neigh[:, width:]], axis=0)
    d_borrowed = nt(d_neigh[rows:], w_recv[...]).astype(BF16)
    back_low[...] = d_borrowed[:border]
    back_high[...] = d_borrowed[border:]
    d_node_o[...] = d_node
    d_centre_o[...] = d_centre
    d_neigh_o[...] = d_neigh[:rows]
    parts = (
        tn(moved, d_centre),
        tn(table, d_neigh),
        gmsg[:width, :width] + gmsg[width:, width:],
        tn(moved, d_node),
        tn(agg_b, d_node),
        tn(node_hid, cot),
    )
    for m, part in enumerate(parts):
        grads[m * width : (m + 1) * width] = part.astype(BF16)
    used = len(parts) * width
    if grads.shape[0] > used:
        grads[used:] = jnp.zeros_like(grads[used:])


def finish_kernel(
    cotangent, d_node, d_centre, d_neigh, w_self, w_send, w_recv, sends, from_low, from_high, out
):
    rows = d_node.shape[0]
    returned = jnp.concatenate([from_low[...], from_high[...]], axis=0)
    out[0] = (
        cotangent[0].astype(F32)
        + nt(d_node[...], w_self[...])
        + nt(d_centre[...], w_send[...])
        + nt(d_neigh[...], w_recv[...])
        + nn(hot_columns(sends[...], rows), returned)
    ).astype(BF16)


def sum_kernel(parts, out):
    total = jnp.sum(parts[...].astype(F32), axis=0).astype(BF16)
    out[...] = jnp.broadcast_to(total[None], out.shape)


def norm_kernel(total, steps):
    count, width = steps.shape[0], steps.shape[1]
    for m in range(count):
        part = total[m * width : (m + 1) * width].astype(F32)
        mean = jnp.sum(jnp.sum(part * part, axis=0, keepdims=True), axis=1, keepdims=True)
        mean = mean / (part.shape[0] * part.shape[1])
        steps[m] = part / jnp.sqrt(mean + 1e-06)


def call(kernel, outs, scratch=()):
    return pl.pallas_call(
        kernel,
        out_shape=[jax.ShapeDtypeStruct(shape, kind) for shape, kind in outs],
        scratch_shapes=scratch,
        compiler_params=pltpu.CompilerParams(vmem_limit_bytes=40 * 1024 * 1024),
        cost_estimate=pl.CostEstimate(flops=2 * 10**9, bytes_accessed=1024, transcendentals=0),
    )


def shards(
    nodes,
    leave_list,
    arrive_list,
    send_list,
    neighbours,
    valid,
    w_send,
    w_recv,
    w_msg,
    w_self,
    w_agg,
    w_out,
    cotangent,
):
    rows, width = nodes.shape[1:]
    slots = neighbours.shape[2]
    migr = leave_list.shape[1] // 2
    border = send_list.shape[1] // 2
    table_rows = rows + 2 * border
    size = lax.axis_size("slab")
    devices = size * lax.axis_size("grp")
    axes = ("grp", "slab")

    def shift(array, by):
        return lax.ppermute(array, "slab", [(i, (i + by) % size) for i in range(size)])

    message = (border + migr + CODE_ROWS, width)
    message_down = (message[0] + CODE_ROWS, width)
    (token,) = call(first_kernel, [((8, LANES), F32)])()
    to_up, far_up, to_down, far_down = call(
        pack_kernel,
        [(message, BF16)] * 2 + [(message_down, BF16)] * 2,
    )(token, nodes, leave_list, arrive_list, send_list)
    low, low_far = shift(to_up, 1), shift(far_up, 2)
    high, high_far = shift(to_down, -1), shift(far_down, -2)

    matrices = 6
    pair_rows = rows * slots // 2
    half_rows = table_rows // 2
    hot_rows = -(-(half_rows + 1) // LANES) * LANES
    share = -(-matrices * width // (8 * devices)) * 8
    edges = rows * slots
    hot, hot_t, wide, ids, d_hid = call(
        prep_kernel,
        [
            ((edges, hot_rows), BF16),
            ((half_rows, edges), BF16),
            ((2, 2 * width, 2 * width), BF16),
            ((rows, LANES), jnp.int32),
            ((rows, width), F32),
        ],
    )(jnp.swapaxes(neighbours, 1, 2), jnp.swapaxes(valid, 1, 2), w_msg, w_out, cotangent)
    sources = (
        nodes,
        arrive_list,
        to_up,
        to_down,
        low,
        low_far,
        high,
        high_far,
        hot,
        hot_t,
        wide,
        ids,
        d_hid,
        w_send,
        w_recv,
        w_self,
        w_agg,
        w_out,
        cotangent,
    )
    updated, back_low, back_high, grads, d_node, d_centre, d_neigh = call(
        layer_kernel,
        [
            ((1, rows, width), BF16),
            ((border, width), BF16),
            ((border, width), BF16),
            ((devices * share, width), BF16),
            ((rows, width), BF16),
            ((rows, width), BF16),
            ((rows, width), BF16),
        ],
        [
            pltpu.VMEM((hot_rows, 2 * width), BF16),
            pltpu.VMEM((pair_rows, 2 * width), BF16),
            pltpu.VMEM((pair_rows, 2 * width), F32),
            pltpu.VMEM((pair_rows, 2 * width), F32),
            pltpu.VMEM((rows, width), F32),
            pltpu.VMEM((rows, width), F32),
            pltpu.VMEM((pair_rows, 2 * width), BF16),
            pltpu.VMEM((edges, 2 * width), BF16),
        ],
    )(*sources)
    from_low = shift(back_high, 1)
    from_high = shift(back_low, -1)
    parts = lax.all_to_all(
        grads.reshape(devices, share, width), axes, split_axis=0, concat_axis=0, tiled=True
    )
    sources = (
        cotangent,
        d_node,
        d_centre,
        d_neigh,
        w_self,
        w_send,
        w_recv,
        send_list,
        from_low,
        from_high,
    )
    (grad_nodes,) = call(
        finish_kernel,
        [((1, rows, width), BF16)],
    )(*sources)
    (shared,) = call(sum_kernel, [((devices, share, width), BF16)])(parts)
    total = lax.all_to_all(shared, axes, split_axis=0, concat_axis=0, tiled=True)
    total = total.reshape(devices * share, width)[: matrices * width]
    (weight_steps,) = call(norm_kernel, [((matrices, width, width), F32)])(total)
    return (updated, grad_nodes, weight_steps)


def solution(mesh):
    rows = P("grp", "slab", None)
    lists = P("grp", "slab")
    in_specs = (rows, lists, lists, lists, rows, rows, P(), P(), P(), P(), P(), P(), rows)
    out_specs = (rows, rows, P())
    return jax.shard_map(shards, mesh=mesh, in_specs=in_specs, out_specs=out_specs, check_vma=False)
```

```python
import functools

import jax
import jax.numpy as jnp
from jax import lax
from jax.experimental import pallas as pl
from jax.experimental.pallas import tpu as pltpu
from jax.sharding import PartitionSpec as P

F32 = jnp.float32
BF16 = jnp.bfloat16
CODE_ROWS = 16
LANES = 128
FAR = -1e30
GROUP = 32
BLOCK = 64


def nn(left, right):
    return lax.dot_general(left, right, (((1,), (0,)), ((), ())), preferred_element_type=F32)


def nt(left, right):
    return lax.dot_general(left, right, (((1,), (1,)), ((), ())), preferred_element_type=F32)


def tn(left, right):
    return lax.dot_general(left, right, (((0,), (0,)), ((), ())), preferred_element_type=F32)


def hot_columns(row, count):
    sub = lax.broadcasted_iota(jnp.int32, (count, row.shape[1]), 0)
    return jnp.where(sub == row, 1.0, 0.0).astype(BF16)


def silu_parts(half):
    tan = jnp.tanh(half)
    part = half * tan
    return half + part, (1.0 + tan) * ((1.0 + half) - part)


def first_kernel(out):
    out[...] = jnp.zeros_like(out)


def pack_kernel(_, nodes, leave, arrive, sends, to_up, far_up, to_down, far_down):
    rows = nodes.shape[1]
    migr = leave.shape[1] // 2
    border = sends.shape[1] // 2
    own = nodes[0]
    leaving = tn(hot_columns(leave[...], rows), own).astype(BF16)
    sub = lax.broadcasted_iota(jnp.int32, (rows, 2 * border), 0)
    column = jnp.transpose(
        jnp.broadcast_to(arrive[...].astype(F32), (2 * border, rows)), (1, 0)
    )
    source = jnp.sum(jnp.where(sub == sends[...], column, 0.0), axis=0, keepdims=True)
    source = source.astype(jnp.int32)
    rest = tn(hot_columns(source, rows), own).astype(BF16)
    code = jnp.where(source >= rows, source - rows, -1).astype(F32)
    for out, far, part in ((to_down, far_down, 0), (to_up, far_up, 1)):
        out[:border] = rest[part * border : (part + 1) * border]
        moving = leaving[part * migr : (part + 1) * migr]
        out[border : border + migr] = moving
        far[:migr] = moving
        far[migr:] = jnp.zeros_like(far[migr:])
        shifted = code if part == 0 else pltpu.roll(code, border, 1)
        tail = out.shape[0] - border - migr
        out[border + migr :] = jnp.broadcast_to(shifted, (tail, 2 * border)).astype(BF16)


def prep_kernel(nbr, valid, w_msg, w_out, cotangent, hot_o, hot_t_o, wide_o, ids_o, d_hid_o):
    slots, rows = nbr.shape[1:]
    width = w_msg.shape[0]
    half_rows, hot_rows = hot_t_o.shape[0], hot_o.shape[1]
    chunk = 4
    half_msg = 0.5 * w_msg[...].astype(F32)
    none = jnp.zeros((width, width), F32)
    for part, block in enumerate((half_msg, jnp.transpose(half_msg, (1, 0)))):
        wide_o[part] = jnp.concatenate(
            [
                jnp.concatenate([block, none], axis=1),
                jnp.concatenate([none, block], axis=1),
            ],
            axis=0,
        ).astype(BF16)
    d_hid_o[...] = nt(cotangent[0], w_out[...])
    upper = nbr[0] >= half_rows
    low_row = jnp.where(upper, nbr[0] - half_rows, nbr[0])
    index = jnp.where(valid[0] == 1, low_row, half_rows) + jnp.where(upper, hot_rows, 0)
    fill = jnp.zeros((LANES - slots, rows), jnp.int32)
    ids_o[...] = jnp.transpose(jnp.concatenate([index, fill], axis=0), (1, 0))

    lane = lax.broadcasted_iota(jnp.int32, (rows, hot_rows), 1).astype(jnp.int16)
    one = jnp.ones((rows, hot_rows), BF16)
    zero = jnp.zeros((rows, hot_rows), BF16)
    sub = lax.broadcasted_iota(jnp.int32, (half_rows, rows), 0).astype(jnp.int16)
    one_t = jnp.ones((half_rows, rows), BF16)
    zero_t = jnp.zeros((half_rows, rows), BF16)

    @pl.loop(0, slots // chunk)
    def build(step):
        for j, short in enumerate(slot_ids(ids_o, step, chunk)):
            slot = step * chunk + j
            short = (short & (hot_rows - 1)).astype(jnp.int16)
            short = jnp.concatenate([short] * (hot_rows // LANES), axis=1)
            hot_o[pl.ds(slot * rows, rows)] = jnp.where(short == lane, one, zero)
            row = nbr[0, pl.ds(slot, 1)]
            row = jnp.where(row >= half_rows, row - half_rows, row)
            short = jnp.broadcast_to(row, (16, rows)).astype(jnp.int16)
            short = jnp.concatenate([short] * (half_rows // 16), axis=0)
            hot_t_o[:, pl.ds(pl.multiple_of(slot * rows, LANES), rows)] = jnp.where(
                short == sub, one_t, zero_t
            )


def slot_ids(ids, step, chunk):
    near = pltpu.roll(ids[...], lax.rem(LANES - step * chunk, LANES), 1)
    shape = (ids.shape[0], LANES)
    return [jnp.broadcast_to(near[:, j : j + 1], shape) for j in range(chunk)]


def layer_kernel(
    nodes,
    arrive,
    my_up,
    my_down,
    low,
    low_far,
    high,
    high_far,
    hot,
    hot_t,
    wide,
    nbr_ids,
    d_hid,
    w_send,
    w_recv,
    w_self,
    w_agg,
    w_out,
    cotangent,
    updated,
    back_low,
    back_high,
    grads,
    d_node_o,
    d_centre_o,
    d_neigh_o,
    neigh_s,
    hid_s,
    ds1_s,
    ds2_s,
    agg_s,
    dcen_s,
    dpre2_s,
    dpre_s,
):
    rows, width = nodes.shape[1:]
    slots = hot.shape[0] // rows
    border = back_low.shape[0]
    migr = low.shape[0] - border - CODE_ROWS
    table_rows = rows + 2 * border

    pool = jnp.concatenate(
        [nodes[0], low[border : border + migr], high[border : border + migr]], axis=0
    )
    moved = tn(hot_columns(arrive[...], pool.shape[0]), pool).astype(BF16)

    def halo(message, first, second):
        code = message[border + migr : border + migr + 8].astype(F32)[:1]
        code = code.astype(jnp.int32)
        source = jnp.concatenate([first, second], axis=0)
        extra = tn(hot_columns(code, 2 * migr), source)
        return (message[:border].astype(F32) + extra[:border]).astype(BF16)

    below = halo(low[...], low_far[:migr], my_down[border : border + migr])
    above = halo(high[...], my_up[border : border + migr], high_far[:migr])
    table = jnp.concatenate([moved, below, above], axis=0)

    half_rows, hot_rows = hot_t.shape[0], hot.shape[1]
    half_centre = 0.5 * nn(moved, w_send[...])
    half_neigh = (0.5 * nn(table, w_recv[...]).astype(BF16).astype(F32)).astype(BF16)
    neigh_s[:half_rows] = jnp.concatenate([half_neigh[:half_rows], half_neigh[half_rows:]], axis=1)
    neigh_s[half_rows:] = jnp.full((hot_rows - half_rows, 2 * width), FAR, BF16)
    ids = slot_ids(nbr_ids, 0, slots)
    blocks = [slice(start, start + BLOCK) for start in range(0, rows, BLOCK)]
    sides = (slice(0, width), slice(width, 2 * width))

    for first in range(0, slots, GROUP):
        gathered = nn(hot[first * rows : (first + GROUP) * rows], neigh_s[...])
        for j in range(GROUP):
            pair, side = divmod(first + j, 2)
            for block in blocks:
                pick = gathered[j * rows + block.start : j * rows + block.stop]
                pick = jnp.where(
                    ids[first + j][block] >= hot_rows, pick[:, sides[1]], pick[:, sides[0]]
                )
                act, slope = silu_parts(half_centre[block] + pick)
                at = slice(pair * rows + block.start, pair * rows + block.stop)
                ds1_s[at, sides[side]] = slope
                hid_s[at, sides[side]] = act.astype(BF16)
        base = first // 2 * rows
        halves = nn(hid_s[base : base + GROUP // 2 * rows], wide[0])
        for block in blocks:
            total = jnp.zeros((BLOCK, width), F32) if first == 0 else agg_s[block]
            for j in range(GROUP):
                pair, side = divmod(j, 2)
                at = slice(pair * rows + block.start, pair * rows + block.stop)
                act, slope = silu_parts(halves[at, sides[side]])
                total = total + act
                ds2_s[base + at.start : base + at.stop, sides[side]] = slope
            agg_s[block] = total

    agg_b = agg_s[...].astype(BF16)
    node_pre = nn(moved, w_self[...]) + nn(agg_b, w_agg[...])
    act, slope = silu_parts(0.5 * node_pre)
    node_hid = act.astype(BF16)
    updated[0] = (moved.astype(F32) + nn(node_hid, w_out[...])).astype(BF16)
    cot = cotangent[0]
    d_node = (d_hid[...] * (0.5 * slope)).astype(BF16)
    half_d_agg = 0.5 * nt(d_node, w_agg[...])

    none = jnp.zeros((BLOCK, width), BF16)
    border_id = jnp.full((BLOCK, width), hot_rows, jnp.int16)
    for first in range(0, slots, GROUP):
        base = first // 2 * rows
        span = slice(base, base + GROUP // 2 * rows)
        for pair in range(GROUP // 2):
            for block in blocks:
                at = slice(base + pair * rows + block.start, base + pair * rows + block.stop)
                for side in sides:
                    dpre2_s[at, side] = (half_d_agg[block] * ds2_s[at, side]).astype(BF16)
        d_hids = nn(dpre2_s[span], wide[1])
        for block in blocks:
            total = jnp.zeros((BLOCK, width), F32) if first == 0 else dcen_s[block]
            for j in range(GROUP):
                pair, side = divmod(j, 2)
                at = slice(pair * rows + block.start, pair * rows + block.stop)
                part = d_hids[at, sides[side]] * ds1_s[base + at.start : base + at.stop, sides[side]]
                total = total + part
                part = part.astype(BF16)
                is_up = ids[first + j][block].astype(jnp.int16) >= border_id
                at = slice((first + j) * rows + block.start, (first + j) * rows + block.stop)
                dpre_s[at, sides[0]] = jnp.where(is_up, none, part)
                dpre_s[at, sides[1]] = jnp.where(is_up, part, none)
            dcen_s[block] = total
    gmsg = tn(hid_s[...], dpre2_s[...])
    d_neigh = nn(hot_t[...], dpre_s[...]).astype(BF16)

    d_centre = dcen_s[...].astype(BF16)
    d_neigh = jnp.concatenate([d_neigh[:, :width], d_neigh[:, width:]], axis=0)
    d_borrowed = nt(d_neigh[rows:], w_recv[...]).astype(BF16)
    back_low[...] = d_borrowed[:border]
    back_high[...] = d_borrowed[border:]
    d_node_o[...] = d_node
    d_centre_o[...] = d_centre
    d_neigh_o[...] = d_neigh[:rows]
    parts = (
        tn(moved, d_centre),
        tn(table, d_neigh),
        gmsg[:width, :width] + gmsg[width:, width:],
        tn(moved, d_node),
        tn(agg_b, d_node),
        tn(node_hid, cot),
    )
    for m, part in enumerate(parts):
        grads[m * width : (m + 1) * width] = part.astype(BF16)
    used = len(parts) * width
    if grads.shape[0] > used:
        grads[used:] = jnp.zeros_like(grads[used:])


def finish_kernel(
    cotangent, d_node, d_centre, d_neigh, w_self, w_send, w_recv, sends, from_low, from_high, out
):
    rows = d_node.shape[0]
    returned = jnp.concatenate([from_low[...], from_high[...]], axis=0)
    out[0] = (
        cotangent[0].astype(F32)
        + nt(d_node[...], w_self[...])
        + nt(d_centre[...], w_send[...])
        + nt(d_neigh[...], w_recv[...])
        + nn(hot_columns(sends[...], rows), returned)
    ).astype(BF16)


def sum_kernel(parts, out):
    total = jnp.sum(parts[...].astype(F32), axis=0).astype(BF16)
    out[...] = jnp.broadcast_to(total[None], out.shape)


def norm_kernel(total, steps):
    count, width = steps.shape[0], steps.shape[1]
    for m in range(count):
        part = total[m * width : (m + 1) * width].astype(F32)
        mean = jnp.sum(jnp.sum(part * part, axis=0, keepdims=True), axis=1, keepdims=True)
        mean = mean / (part.shape[0] * part.shape[1])
        steps[m] = part / jnp.sqrt(mean + 1e-06)


def call(kernel, outs, scratch=()):
    return pl.pallas_call(
        kernel,
        out_shape=[jax.ShapeDtypeStruct(shape, kind) for shape, kind in outs],
        scratch_shapes=scratch,
        compiler_params=pltpu.CompilerParams(vmem_limit_bytes=40 * 1024 * 1024),
        cost_estimate=pl.CostEstimate(flops=2 * 10**9, bytes_accessed=1024, transcendentals=0),
    )


def shards(
    nodes,
    leave_list,
    arrive_list,
    send_list,
    neighbours,
    valid,
    w_send,
    w_recv,
    w_msg,
    w_self,
    w_agg,
    w_out,
    cotangent,
):
    rows, width = nodes.shape[1:]
    slots = neighbours.shape[2]
    migr = leave_list.shape[1] // 2
    border = send_list.shape[1] // 2
    table_rows = rows + 2 * border
    size = lax.axis_size("slab")
    devices = size * lax.axis_size("grp")
    axes = ("grp", "slab")

    def shift(array, by):
        return lax.ppermute(array, "slab", [(i, (i + by) % size) for i in range(size)])

    message = (border + migr + CODE_ROWS, width)
    message_down = (message[0] + CODE_ROWS, width)
    (token,) = call(first_kernel, [((8, LANES), F32)])()
    to_up, far_up, to_down, far_down = call(
        pack_kernel,
        [(message, BF16)] * 2 + [(message_down, BF16)] * 2,
    )(token, nodes, leave_list, arrive_list, send_list)
    low, low_far = shift(to_up, 1), shift(far_up, 2)
    high, high_far = shift(to_down, -1), shift(far_down, -2)

    matrices = 6
    pair_rows = rows * slots // 2
    half_rows = table_rows // 2
    hot_rows = -(-(half_rows + 1) // LANES) * LANES
    share = -(-matrices * width // (8 * devices)) * 8
    edges = rows * slots
    hot, hot_t, wide, ids, d_hid = call(
        prep_kernel,
        [
            ((edges, hot_rows), BF16),
            ((half_rows, edges), BF16),
            ((2, 2 * width, 2 * width), BF16),
            ((rows, LANES), jnp.int32),
            ((rows, width), F32),
        ],
    )(jnp.swapaxes(neighbours, 1, 2), jnp.swapaxes(valid, 1, 2), w_msg, w_out, cotangent)
    sources = (
        nodes,
        arrive_list,
        to_up,
        to_down,
        low,
        low_far,
        high,
        high_far,
        hot,
        hot_t,
        wide,
        ids,
        d_hid,
        w_send,
        w_recv,
        w_self,
        w_agg,
        w_out,
        cotangent,
    )
    updated, back_low, back_high, grads, d_node, d_centre, d_neigh = call(
        layer_kernel,
        [
            ((1, rows, width), BF16),
            ((border, width), BF16),
            ((border, width), BF16),
            ((devices * share, width), BF16),
            ((rows, width), BF16),
            ((rows, width), BF16),
            ((rows, width), BF16),
        ],
        [
            pltpu.VMEM((hot_rows, 2 * width), BF16),
            pltpu.VMEM((pair_rows, 2 * width), BF16),
            pltpu.VMEM((pair_rows, 2 * width), F32),
            pltpu.VMEM((pair_rows, 2 * width), F32),
            pltpu.VMEM((rows, width), F32),
            pltpu.VMEM((rows, width), F32),
            pltpu.VMEM((pair_rows, 2 * width), BF16),
            pltpu.VMEM((edges, 2 * width), BF16),
        ],
    )(*sources)
    from_low = shift(back_high, 1)
    from_high = shift(back_low, -1)
    parts = lax.all_to_all(
        grads.reshape(devices, share, width), axes, split_axis=0, concat_axis=0, tiled=True
    )
    sources = (
        cotangent,
        d_node,
        d_centre,
        d_neigh,
        w_self,
        w_send,
        w_recv,
        send_list,
        from_low,
        from_high,
    )
    (grad_nodes,) = call(
        finish_kernel,
        [((1, rows, width), BF16)],
    )(*sources)
    (shared,) = call(sum_kernel, [((devices, share, width), BF16)])(parts)
    total = lax.all_to_all(shared, axes, split_axis=0, concat_axis=0, tiled=True)
    total = total.reshape(devices * share, width)[: matrices * width]
    (weight_steps,) = call(norm_kernel, [((matrices, width, width), F32)])(total)
    return (updated, grad_nodes, weight_steps)


def solution(mesh):
    rows = P("grp", "slab", None)
    lists = P("grp", "slab")
    in_specs = (rows, lists, lists, lists, rows, rows, P(), P(), P(), P(), P(), P(), rows)
    out_specs = (rows, rows, P())
    return jax.shard_map(shards, mesh=mesh, in_specs=in_specs, out_specs=out_specs, check_vma=False)
```

```python
import functools

import jax
import jax.numpy as jnp
from jax import lax
from jax.experimental import pallas as pl
from jax.experimental.pallas import tpu as pltpu
from jax.sharding import PartitionSpec as P

F32 = jnp.float32
BF16 = jnp.bfloat16
CODE_ROWS = 16
LANES = 128
FAR = -1e30
GROUP = 32
BLOCK = 64


def nn(left, right):
    return lax.dot_general(left, right, (((1,), (0,)), ((), ())), preferred_element_type=F32)


def nt(left, right):
    return lax.dot_general(left, right, (((1,), (1,)), ((), ())), preferred_element_type=F32)


def tn(left, right):
    return lax.dot_general(left, right, (((0,), (0,)), ((), ())), preferred_element_type=F32)


def hot_columns(row, count):
    sub = lax.broadcasted_iota(jnp.int32, (count, row.shape[1]), 0)
    return jnp.where(sub == row, 1.0, 0.0).astype(BF16)


def silu_parts(half):
    tan = jnp.tanh(half)
    part = half * tan
    return half + part, (1.0 + tan) * ((1.0 + half) - part)


def first_kernel(out):
    out[...] = jnp.zeros_like(out)


def parities():
    slab = lax.axis_index("slab")
    return lax.rem(slab, 2) == 1, lax.rem(slab // 2, 2) == 1


def pack_kernel(_, nodes, leave, arrive, sends, near_off, near_on, far_off, far_on):
    odd, odd_pair = parities()
    rows = nodes.shape[1]
    migr = leave.shape[1] // 2
    border = sends.shape[1] // 2
    own = nodes[0]
    leaving = tn(hot_columns(leave[...], rows), own).astype(BF16)
    sub = lax.broadcasted_iota(jnp.int32, (rows, 2 * border), 0)
    column = jnp.transpose(
        jnp.broadcast_to(arrive[...].astype(F32), (2 * border, rows)), (1, 0)
    )
    source = jnp.sum(jnp.where(sub == sends[...], column, 0.0), axis=0, keepdims=True)
    source = source.astype(jnp.int32)
    rest = tn(hot_columns(source, rows), own).astype(BF16)
    code = jnp.where(source >= rows, source - rows, -1).astype(F32)
    messages = []
    for part in range(2):
        shifted = code if part == 0 else pltpu.roll(code, border, 1)
        messages.append(
            jnp.concatenate(
                [
                    rest[part * border : (part + 1) * border],
                    leaving[part * migr : (part + 1) * migr],
                    jnp.broadcast_to(shifted, (CODE_ROWS, 2 * border)).astype(BF16),
                ],
                axis=0,
            )
        )
    down, up = messages
    near_off[...] = jnp.where(odd, up, down)
    near_on[...] = jnp.where(odd, down, up)
    down, up = leaving[:migr], leaving[migr:]
    far_off[...] = jnp.where(odd_pair, up, down)
    far_on[...] = jnp.where(odd_pair, down, up)


def prep_kernel(nbr, valid, w_msg, w_out, cotangent, hot_o, hot_t_o, wide_o, ids_o, d_hid_o):
    slots, rows = nbr.shape[1:]
    width = w_msg.shape[0]
    half_rows, hot_rows = hot_t_o.shape[0], hot_o.shape[1]
    chunk = 4
    half_msg = 0.5 * w_msg[...].astype(F32)
    none = jnp.zeros((width, width), F32)
    for part, block in enumerate((half_msg, jnp.transpose(half_msg, (1, 0)))):
        wide_o[part] = jnp.concatenate(
            [
                jnp.concatenate([block, none], axis=1),
                jnp.concatenate([none, block], axis=1),
            ],
            axis=0,
        ).astype(BF16)
    d_hid_o[...] = nt(cotangent[0], w_out[...])
    upper = nbr[0] >= half_rows
    low_row = jnp.where(upper, nbr[0] - half_rows, nbr[0])
    index = jnp.where(valid[0] == 1, low_row, half_rows) + jnp.where(upper, hot_rows, 0)
    fill = jnp.zeros((LANES - slots, rows), jnp.int32)
    ids_o[...] = jnp.transpose(jnp.concatenate([index, fill], axis=0), (1, 0))

    lane = lax.broadcasted_iota(jnp.int32, (rows, hot_rows), 1).astype(jnp.int16)
    one = jnp.ones((rows, hot_rows), BF16)
    zero = jnp.zeros((rows, hot_rows), BF16)
    sub = lax.broadcasted_iota(jnp.int32, (half_rows, rows), 0).astype(jnp.int16)
    one_t = jnp.ones((half_rows, rows), BF16)
    zero_t = jnp.zeros((half_rows, rows), BF16)

    @pl.loop(0, slots // chunk)
    def build(step):
        for j, short in enumerate(slot_ids(ids_o, step, chunk)):
            slot = step * chunk + j
            short = (short & (hot_rows - 1)).astype(jnp.int16)
            short = jnp.concatenate([short] * (hot_rows // LANES), axis=1)
            hot_o[pl.ds(slot * rows, rows)] = jnp.where(short == lane, one, zero)
            row = nbr[0, pl.ds(slot, 1)]
            row = jnp.where(row >= half_rows, row - half_rows, row)
            short = jnp.broadcast_to(row, (16, rows)).astype(jnp.int16)
            short = jnp.concatenate([short] * (half_rows // 16), axis=0)
            hot_t_o[:, pl.ds(pl.multiple_of(slot * rows, LANES), rows)] = jnp.where(
                short == sub, one_t, zero_t
            )


def slot_ids(ids, step, chunk):
    near = pltpu.roll(ids[...], lax.rem(LANES - step * chunk, LANES), 1)
    shape = (ids.shape[0], LANES)
    return [jnp.broadcast_to(near[:, j : j + 1], shape) for j in range(chunk)]


def layer_kernel(
    nodes,
    arrive,
    my_far_off,
    my_far_on,
    got_off,
    got_on,
    got_far_off,
    got_far_on,
    hot,
    hot_t,
    wide,
    nbr_ids,
    d_hid,
    w_send,
    w_recv,
    w_self,
    w_agg,
    w_out,
    cotangent,
    updated,
    back_off,
    back_on,
    grads,
    d_node_o,
    d_centre_o,
    d_neigh_o,
    neigh_s,
    hid_s,
    ds1_s,
    ds2_s,
    agg_s,
    dcen_s,
    dpre2_s,
    dpre_s,
):
    rows, width = nodes.shape[1:]
    slots = hot.shape[0] // rows
    border, migr = back_off.shape[0], got_far_off.shape[0]
    odd, odd_pair = parities()
    low = jnp.where(odd, got_on[...], got_off[...])
    high = jnp.where(odd, got_off[...], got_on[...])
    low_far = jnp.where(odd_pair, got_far_on[...], got_far_off[...])
    high_far = jnp.where(odd_pair, got_far_off[...], got_far_on[...])
    my_up = jnp.where(odd_pair, my_far_off[...], my_far_on[...])
    my_down = jnp.where(odd_pair, my_far_on[...], my_far_off[...])
    table_rows = rows + 2 * border

    pool = jnp.concatenate(
        [nodes[0], low[border : border + migr], high[border : border + migr]], axis=0
    )
    moved = tn(hot_columns(arrive[...], pool.shape[0]), pool).astype(BF16)

    def halo(message, first, second):
        code = message[border + migr : border + migr + 8].astype(F32)[:1]
        code = code.astype(jnp.int32)
        source = jnp.concatenate([first, second], axis=0)
        extra = tn(hot_columns(code, 2 * migr), source)
        return (message[:border].astype(F32) + extra[:border]).astype(BF16)

    below = halo(low, low_far, my_down)
    above = halo(high, my_up, high_far)
    table = jnp.concatenate([moved, below, above], axis=0)

    half_rows, hot_rows = hot_t.shape[0], hot.shape[1]
    half_centre = 0.5 * nn(moved, w_send[...])
    half_neigh = (0.5 * nn(table, w_recv[...]).astype(BF16).astype(F32)).astype(BF16)
    neigh_s[:half_rows] = jnp.concatenate([half_neigh[:half_rows], half_neigh[half_rows:]], axis=1)
    neigh_s[half_rows:] = jnp.full((hot_rows - half_rows, 2 * width), FAR, BF16)
    ids = slot_ids(nbr_ids, 0, slots)
    blocks = [slice(start, start + BLOCK) for start in range(0, rows, BLOCK)]
    sides = (slice(0, width), slice(width, 2 * width))

    for first in range(0, slots, GROUP):
        gathered = nn(hot[first * rows : (first + GROUP) * rows], neigh_s[...])
        for j in range(GROUP):
            pair, side = divmod(first + j, 2)
            for block in blocks:
                pick = gathered[j * rows + block.start : j * rows + block.stop]
                pick = jnp.where(
                    ids[first + j][block] >= hot_rows, pick[:, sides[1]], pick[:, sides[0]]
                )
                act, slope = silu_parts(half_centre[block] + pick)
                at = slice(pair * rows + block.start, pair * rows + block.stop)
                ds1_s[at, sides[side]] = slope
                hid_s[at, sides[side]] = act.astype(BF16)
        base = first // 2 * rows
        halves = nn(hid_s[base : base + GROUP // 2 * rows], wide[0])
        for block in blocks:
            total = jnp.zeros((BLOCK, width), F32) if first == 0 else agg_s[block]
            for j in range(GROUP):
                pair, side = divmod(j, 2)
                at = slice(pair * rows + block.start, pair * rows + block.stop)
                act, slope = silu_parts(halves[at, sides[side]])
                total = total + act
                ds2_s[base + at.start : base + at.stop, sides[side]] = slope
            agg_s[block] = total

    agg_b = agg_s[...].astype(BF16)
    node_pre = nn(moved, w_self[...]) + nn(agg_b, w_agg[...])
    act, slope = silu_parts(0.5 * node_pre)
    node_hid = act.astype(BF16)
    updated[0] = (moved.astype(F32) + nn(node_hid, w_out[...])).astype(BF16)
    cot = cotangent[0]
    d_node = (d_hid[...] * (0.5 * slope)).astype(BF16)
    half_d_agg = 0.5 * nt(d_node, w_agg[...])

    none = jnp.zeros((BLOCK, width), BF16)
    border_id = jnp.full((BLOCK, width), hot_rows, jnp.int16)
    for first in range(0, slots, GROUP):
        base = first // 2 * rows
        span = slice(base, base + GROUP // 2 * rows)
        for pair in range(GROUP // 2):
            for block in blocks:
                at = slice(base + pair * rows + block.start, base + pair * rows + block.stop)
                for side in sides:
                    dpre2_s[at, side] = (half_d_agg[block] * ds2_s[at, side]).astype(BF16)
        d_hids = nn(dpre2_s[span], wide[1])
        for block in blocks:
            total = jnp.zeros((BLOCK, width), F32) if first == 0 else dcen_s[block]
            for j in range(GROUP):
                pair, side = divmod(j, 2)
                at = slice(pair * rows + block.start, pair * rows + block.stop)
                part = d_hids[at, sides[side]] * ds1_s[base + at.start : base + at.stop, sides[side]]
                total = total + part
                part = part.astype(BF16)
                is_up = ids[first + j][block].astype(jnp.int16) >= border_id
                at = slice((first + j) * rows + block.start, (first + j) * rows + block.stop)
                dpre_s[at, sides[0]] = jnp.where(is_up, none, part)
                dpre_s[at, sides[1]] = jnp.where(is_up, part, none)
            dcen_s[block] = total
    gmsg = tn(hid_s[...], dpre2_s[...])
    d_neigh = nn(hot_t[...], dpre_s[...]).astype(BF16)

    d_centre = dcen_s[...].astype(BF16)
    d_neigh = jnp.concatenate([d_neigh[:, :width], d_neigh[:, width:]], axis=0)
    d_borrowed = nt(d_neigh[rows:], w_recv[...]).astype(BF16)
    back_off[...] = jnp.where(odd, d_borrowed[border:], d_borrowed[:border])
    back_on[...] = jnp.where(odd, d_borrowed[:border], d_borrowed[border:])
    d_node_o[...] = d_node
    d_centre_o[...] = d_centre
    d_neigh_o[...] = d_neigh[:rows]
    parts = (
        tn(moved, d_centre),
        tn(table, d_neigh),
        gmsg[:width, :width] + gmsg[width:, width:],
        tn(moved, d_node),
        tn(agg_b, d_node),
        tn(node_hid, cot),
    )
    for m, part in enumerate(parts):
        grads[m * width : (m + 1) * width] = part.astype(BF16)
    used = len(parts) * width
    if grads.shape[0] > used:
        grads[used:] = jnp.zeros_like(grads[used:])


def finish_kernel(
    cotangent, d_node, d_centre, d_neigh, w_self, w_send, w_recv, sends, got_off, got_on, out
):
    rows = d_node.shape[0]
    odd, _ = parities()
    from_low = jnp.where(odd, got_on[...], got_off[...])
    from_high = jnp.where(odd, got_off[...], got_on[...])
    returned = jnp.concatenate([from_low, from_high], axis=0)
    out[0] = (
        cotangent[0].astype(F32)
        + nt(d_node[...], w_self[...])
        + nt(d_centre[...], w_send[...])
        + nt(d_neigh[...], w_recv[...])
        + nn(hot_columns(sends[...], rows), returned)
    ).astype(BF16)


def sum_kernel(parts, out):
    total = jnp.sum(parts[...].astype(F32), axis=0).astype(BF16)
    out[...] = jnp.broadcast_to(total[None], out.shape)


def norm_kernel(total, steps):
    count, width = steps.shape[0], steps.shape[1]
    for m in range(count):
        part = total[m * width : (m + 1) * width].astype(F32)
        mean = jnp.sum(jnp.sum(part * part, axis=0, keepdims=True), axis=1, keepdims=True)
        mean = mean / (part.shape[0] * part.shape[1])
        steps[m] = part / jnp.sqrt(mean + 1e-06)


def call(kernel, outs, scratch=()):
    return pl.pallas_call(
        kernel,
        out_shape=[jax.ShapeDtypeStruct(shape, kind) for shape, kind in outs],
        scratch_shapes=scratch,
        compiler_params=pltpu.CompilerParams(vmem_limit_bytes=40 * 1024 * 1024),
        cost_estimate=pl.CostEstimate(flops=2 * 10**9, bytes_accessed=1024, transcendentals=0),
    )


def shards(
    nodes,
    leave_list,
    arrive_list,
    send_list,
    neighbours,
    valid,
    w_send,
    w_recv,
    w_msg,
    w_self,
    w_agg,
    w_out,
    cotangent,
):
    rows, width = nodes.shape[1:]
    slots = neighbours.shape[2]
    migr = leave_list.shape[1] // 2
    border = send_list.shape[1] // 2
    table_rows = rows + 2 * border
    size = lax.axis_size("slab")
    devices = size * lax.axis_size("grp")
    axes = ("grp", "slab")

    def swap(array, by):
        step = abs(by)
        pairs = [
            (i, (i + by if i // step % 2 == 0 else i - by) % size) for i in range(size)
        ]
        return lax.ppermute(array, "slab", pairs)

    message = (border + migr + CODE_ROWS, width)
    (token,) = call(first_kernel, [((8, LANES), F32)])()
    near_off, near_on, far_off, far_on = call(
        pack_kernel,
        [(message, BF16)] * 2 + [((migr, width), BF16)] * 2,
    )(token, nodes, leave_list, arrive_list, send_list)
    got_on = swap(near_on, 1)
    got_off = swap(near_off, -1)
    got_far_on = swap(far_on, 2)
    got_far_off = swap(far_off, -2)

    matrices = 6
    pair_rows = rows * slots // 2
    half_rows = table_rows // 2
    hot_rows = -(-(half_rows + 1) // LANES) * LANES
    share = -(-matrices * width // (8 * devices)) * 8
    edges = rows * slots
    hot, hot_t, wide, ids, d_hid = call(
        prep_kernel,
        [
            ((edges, hot_rows), BF16),
            ((half_rows, edges), BF16),
            ((2, 2 * width, 2 * width), BF16),
            ((rows, LANES), jnp.int32),
            ((rows, width), F32),
        ],
    )(jnp.swapaxes(neighbours, 1, 2), jnp.swapaxes(valid, 1, 2), w_msg, w_out, cotangent)
    sources = (
        nodes,
        arrive_list,
        far_off,
        far_on,
        got_off,
        got_on,
        got_far_off,
        got_far_on,
        hot,
        hot_t,
        wide,
        ids,
        d_hid,
        w_send,
        w_recv,
        w_self,
        w_agg,
        w_out,
        cotangent,
    )
    updated, back_off, back_on, grads, d_node, d_centre, d_neigh = call(
        layer_kernel,
        [
            ((1, rows, width), BF16),
            ((border, width), BF16),
            ((border, width), BF16),
            ((devices * share, width), BF16),
            ((rows, width), BF16),
            ((rows, width), BF16),
            ((rows, width), BF16),
        ],
        [
            pltpu.VMEM((hot_rows, 2 * width), BF16),
            pltpu.VMEM((pair_rows, 2 * width), BF16),
            pltpu.VMEM((pair_rows, 2 * width), F32),
            pltpu.VMEM((pair_rows, 2 * width), F32),
            pltpu.VMEM((rows, width), F32),
            pltpu.VMEM((rows, width), F32),
            pltpu.VMEM((pair_rows, 2 * width), BF16),
            pltpu.VMEM((edges, 2 * width), BF16),
        ],
    )(*sources)
    got_on = swap(back_on, 1)
    got_off = swap(back_off, -1)
    parts = lax.all_to_all(
        grads.reshape(devices, share, width), axes, split_axis=0, concat_axis=0, tiled=True
    )
    sources = (
        cotangent,
        d_node,
        d_centre,
        d_neigh,
        w_self,
        w_send,
        w_recv,
        send_list,
        got_off,
        got_on,
    )
    (grad_nodes,) = call(
        finish_kernel,
        [((1, rows, width), BF16)],
    )(*sources)
    (shared,) = call(sum_kernel, [((devices, share, width), BF16)])(parts)
    total = lax.all_to_all(shared, axes, split_axis=0, concat_axis=0, tiled=True)
    total = total.reshape(devices * share, width)[: matrices * width]
    (weight_steps,) = call(norm_kernel, [((matrices, width, width), F32)])(total)
    return (updated, grad_nodes, weight_steps)


def solution(mesh):
    rows = P("grp", "slab", None)
    lists = P("grp", "slab")
    in_specs = (rows, lists, lists, lists, rows, rows, P(), P(), P(), P(), P(), P(), rows)
    out_specs = (rows, rows, P())
    return jax.shard_map(shards, mesh=mesh, in_specs=in_specs, out_specs=out_specs, check_vma=False)
```

```python
import functools

import jax
import jax.numpy as jnp
from jax import lax
from jax.experimental import pallas as pl
from jax.experimental.pallas import tpu as pltpu
from jax.sharding import PartitionSpec as P

F32 = jnp.float32
BF16 = jnp.bfloat16
CODE_ROWS = 16
LANES = 128
FAR = -1e30
GROUP = 32
BLOCK = 64


def nn(left, right):
    return lax.dot_general(left, right, (((1,), (0,)), ((), ())), preferred_element_type=F32)


def nt(left, right):
    return lax.dot_general(left, right, (((1,), (1,)), ((), ())), preferred_element_type=F32)


def tn(left, right):
    return lax.dot_general(left, right, (((0,), (0,)), ((), ())), preferred_element_type=F32)


def hot_columns(row, count):
    sub = lax.broadcasted_iota(jnp.int32, (count, row.shape[1]), 0)
    return jnp.where(sub == row, 1.0, 0.0).astype(BF16)


def silu_parts(half):
    tan = jnp.tanh(half)
    part = half * tan
    return half + part, (1.0 + tan) * ((1.0 + half) - part)


def first_kernel(out):
    out[...] = jnp.zeros_like(out)


def parities():
    slab = lax.axis_index("slab")
    return lax.rem(slab, 2) == 1, lax.rem(slab // 2, 2) == 1


def pack_kernel(_, nodes, leave, arrive, sends, near_off, near_on, far_off, far_on):
    odd, odd_pair = parities()
    rows = nodes.shape[1]
    migr = leave.shape[1] // 2
    border = sends.shape[1] // 2
    own = nodes[0]
    leaving = tn(hot_columns(leave[...], rows), own).astype(BF16)
    sub = lax.broadcasted_iota(jnp.int32, (rows, 2 * border), 0)
    column = jnp.transpose(
        jnp.broadcast_to(arrive[...].astype(F32), (2 * border, rows)), (1, 0)
    )
    source = jnp.sum(jnp.where(sub == sends[...], column, 0.0), axis=0, keepdims=True)
    source = source.astype(jnp.int32)
    rest = tn(hot_columns(source, rows), own).astype(BF16)
    code = jnp.where(source >= rows, source - rows, -1).astype(F32)
    messages = []
    for part in range(2):
        shifted = code if part == 0 else pltpu.roll(code, border, 1)
        messages.append(
            jnp.concatenate(
                [
                    rest[part * border : (part + 1) * border],
                    leaving[part * migr : (part + 1) * migr],
                    jnp.broadcast_to(shifted, (CODE_ROWS, 2 * border)).astype(BF16),
                ],
                axis=0,
            )
        )
    down, up = messages
    near_off[...] = jnp.where(odd, up, down)
    near_on[...] = jnp.where(odd, down, up)
    down, up = leaving[:migr], leaving[migr:]
    far_off[:migr] = jnp.where(odd_pair, up, down)
    far_on[:migr] = jnp.where(odd_pair, down, up)
    for out in (far_off, far_on):
        out[migr:] = jnp.zeros_like(out[migr:])


def prep_kernel(nbr, valid, w_msg, w_out, cotangent, hot_o, hot_t_o, wide_o, ids_o, d_hid_o):
    slots, rows = nbr.shape[1:]
    width = w_msg.shape[0]
    half_rows, hot_rows = hot_t_o.shape[0], hot_o.shape[1]
    chunk = 4
    half_msg = 0.5 * w_msg[...].astype(F32)
    none = jnp.zeros((width, width), F32)
    for part, block in enumerate((half_msg, jnp.transpose(half_msg, (1, 0)))):
        wide_o[part] = jnp.concatenate(
            [
                jnp.concatenate([block, none], axis=1),
                jnp.concatenate([none, block], axis=1),
            ],
            axis=0,
        ).astype(BF16)
    d_hid_o[...] = nt(cotangent[0], w_out[...])
    upper = nbr[0] >= half_rows
    low_row = jnp.where(upper, nbr[0] - half_rows, nbr[0])
    index = jnp.where(valid[0] == 1, low_row, half_rows) + jnp.where(upper, hot_rows, 0)
    fill = jnp.zeros((LANES - slots, rows), jnp.int32)
    ids_o[...] = jnp.transpose(jnp.concatenate([index, fill], axis=0), (1, 0))

    lane = lax.broadcasted_iota(jnp.int32, (rows, hot_rows), 1).astype(jnp.int16)
    one = jnp.ones((rows, hot_rows), BF16)
    zero = jnp.zeros((rows, hot_rows), BF16)
    sub = lax.broadcasted_iota(jnp.int32, (half_rows, rows), 0).astype(jnp.int16)
    one_t = jnp.ones((half_rows, rows), BF16)
    zero_t = jnp.zeros((half_rows, rows), BF16)

    @pl.loop(0, slots // chunk)
    def build(step):
        for j, short in enumerate(slot_ids(ids_o, step, chunk)):
            slot = step * chunk + j
            short = (short & (hot_rows - 1)).astype(jnp.int16)
            short = jnp.concatenate([short] * (hot_rows // LANES), axis=1)
            hot_o[pl.ds(slot * rows, rows)] = jnp.where(short == lane, one, zero)
            row = nbr[0, pl.ds(slot, 1)]
            row = jnp.where(row >= half_rows, row - half_rows, row)
            short = jnp.broadcast_to(row, (16, rows)).astype(jnp.int16)
            short = jnp.concatenate([short] * (half_rows // 16), axis=0)
            hot_t_o[:, pl.ds(pl.multiple_of(slot * rows, LANES), rows)] = jnp.where(
                short == sub, one_t, zero_t
            )


def slot_ids(ids, step, chunk):
    near = pltpu.roll(ids[...], lax.rem(LANES - step * chunk, LANES), 1)
    shape = (ids.shape[0], LANES)
    return [jnp.broadcast_to(near[:, j : j + 1], shape) for j in range(chunk)]


def layer_kernel(
    nodes,
    arrive,
    my_far_off,
    my_far_on,
    got_off,
    got_on,
    got_far_off,
    got_far_on,
    hot,
    hot_t,
    wide,
    nbr_ids,
    d_hid,
    w_send,
    w_recv,
    w_self,
    w_agg,
    w_out,
    cotangent,
    updated,
    back_off,
    back_on,
    grads,
    d_node_o,
    d_centre_o,
    d_neigh_o,
    neigh_s,
    hid_s,
    ds1_s,
    ds2_s,
    agg_s,
    dcen_s,
    dpre2_s,
    dpre_s,
):
    rows, width = nodes.shape[1:]
    slots = hot.shape[0] // rows
    border = back_off.shape[0]
    migr = got_off.shape[0] - border - CODE_ROWS
    odd, odd_pair = parities()
    low = jnp.where(odd, got_on[...], got_off[...])
    high = jnp.where(odd, got_off[...], got_on[...])
    low_far = jnp.where(odd_pair, got_far_on[:migr], got_far_off[:migr])
    high_far = jnp.where(odd_pair, got_far_off[:migr], got_far_on[:migr])
    my_up = jnp.where(odd_pair, my_far_off[:migr], my_far_on[:migr])
    my_down = jnp.where(odd_pair, my_far_on[:migr], my_far_off[:migr])
    table_rows = rows + 2 * border

    pool = jnp.concatenate(
        [nodes[0], low[border : border + migr], high[border : border + migr]], axis=0
    )
    moved = tn(hot_columns(arrive[...], pool.shape[0]), pool).astype(BF16)

    def halo(message, first, second):
        code = message[border + migr : border + migr + 8].astype(F32)[:1]
        code = code.astype(jnp.int32)
        source = jnp.concatenate([first, second], axis=0)
        extra = tn(hot_columns(code, 2 * migr), source)
        return (message[:border].astype(F32) + extra[:border]).astype(BF16)

    below = halo(low, low_far, my_down)
    above = halo(high, my_up, high_far)
    table = jnp.concatenate([moved, below, above], axis=0)

    half_rows, hot_rows = hot_t.shape[0], hot.shape[1]
    half_centre = 0.5 * nn(moved, w_send[...])
    half_neigh = (0.5 * nn(table, w_recv[...]).astype(BF16).astype(F32)).astype(BF16)
    neigh_s[:half_rows] = jnp.concatenate([half_neigh[:half_rows], half_neigh[half_rows:]], axis=1)
    neigh_s[half_rows:] = jnp.full((hot_rows - half_rows, 2 * width), FAR, BF16)
    ids = slot_ids(nbr_ids, 0, slots)
    blocks = [slice(start, start + BLOCK) for start in range(0, rows, BLOCK)]
    sides = (slice(0, width), slice(width, 2 * width))

    for first in range(0, slots, GROUP):
        gathered = nn(hot[first * rows : (first + GROUP) * rows], neigh_s[...])
        for j in range(GROUP):
            pair, side = divmod(first + j, 2)
            for block in blocks:
                pick = gathered[j * rows + block.start : j * rows + block.stop]
                pick = jnp.where(
                    ids[first + j][block] >= hot_rows, pick[:, sides[1]], pick[:, sides[0]]
                )
                act, slope = silu_parts(half_centre[block] + pick)
                at = slice(pair * rows + block.start, pair * rows + block.stop)
                ds1_s[at, sides[side]] = slope
                hid_s[at, sides[side]] = act.astype(BF16)
        base = first // 2 * rows
        halves = nn(hid_s[base : base + GROUP // 2 * rows], wide[0])
        for block in blocks:
            total = jnp.zeros((BLOCK, width), F32) if first == 0 else agg_s[block]
            for j in range(GROUP):
                pair, side = divmod(j, 2)
                at = slice(pair * rows + block.start, pair * rows + block.stop)
                act, slope = silu_parts(halves[at, sides[side]])
                total = total + act
                ds2_s[base + at.start : base + at.stop, sides[side]] = slope
            agg_s[block] = total

    agg_b = agg_s[...].astype(BF16)
    node_pre = nn(moved, w_self[...]) + nn(agg_b, w_agg[...])
    act, slope = silu_parts(0.5 * node_pre)
    node_hid = act.astype(BF16)
    updated[0] = (moved.astype(F32) + nn(node_hid, w_out[...])).astype(BF16)
    cot = cotangent[0]
    d_node = (d_hid[...] * (0.5 * slope)).astype(BF16)
    half_d_agg = 0.5 * nt(d_node, w_agg[...])

    none = jnp.zeros((BLOCK, width), BF16)
    border_id = jnp.full((BLOCK, width), hot_rows, jnp.int16)
    for first in range(0, slots, GROUP):
        base = first // 2 * rows
        span = slice(base, base + GROUP // 2 * rows)
        for pair in range(GROUP // 2):
            for block in blocks:
                at = slice(base + pair * rows + block.start, base + pair * rows + block.stop)
                for side in sides:
                    dpre2_s[at, side] = (half_d_agg[block] * ds2_s[at, side]).astype(BF16)
        d_hids = nn(dpre2_s[span], wide[1])
        for block in blocks:
            total = jnp.zeros((BLOCK, width), F32) if first == 0 else dcen_s[block]
            for j in range(GROUP):
                pair, side = divmod(j, 2)
                at = slice(pair * rows + block.start, pair * rows + block.stop)
                part = d_hids[at, sides[side]] * ds1_s[base + at.start : base + at.stop, sides[side]]
                total = total + part
                part = part.astype(BF16)
                is_up = ids[first + j][block].astype(jnp.int16) >= border_id
                at = slice((first + j) * rows + block.start, (first + j) * rows + block.stop)
                dpre_s[at, sides[0]] = jnp.where(is_up, none, part)
                dpre_s[at, sides[1]] = jnp.where(is_up, part, none)
            dcen_s[block] = total
    gmsg = tn(hid_s[...], dpre2_s[...])
    d_neigh = nn(hot_t[...], dpre_s[...]).astype(BF16)

    d_centre = dcen_s[...].astype(BF16)
    d_neigh = jnp.concatenate([d_neigh[:, :width], d_neigh[:, width:]], axis=0)
    d_borrowed = nt(d_neigh[rows:], w_recv[...]).astype(BF16)
    back_off[...] = jnp.where(odd, d_borrowed[border:], d_borrowed[:border])
    back_on[...] = jnp.where(odd, d_borrowed[:border], d_borrowed[border:])
    d_node_o[...] = d_node
    d_centre_o[...] = d_centre
    d_neigh_o[...] = d_neigh[:rows]
    parts = (
        tn(moved, d_centre),
        tn(table, d_neigh),
        gmsg[:width, :width] + gmsg[width:, width:],
        tn(moved, d_node),
        tn(agg_b, d_node),
        tn(node_hid, cot),
    )
    for m, part in enumerate(parts):
        grads[m * width : (m + 1) * width] = part.astype(BF16)
    used = len(parts) * width
    if grads.shape[0] > used:
        grads[used:] = jnp.zeros_like(grads[used:])


def finish_kernel(
    cotangent, d_node, d_centre, d_neigh, w_self, w_send, w_recv, sends, got_off, got_on, out
):
    rows = d_node.shape[0]
    odd, _ = parities()
    from_low = jnp.where(odd, got_on[...], got_off[...])
    from_high = jnp.where(odd, got_off[...], got_on[...])
    returned = jnp.concatenate([from_low, from_high], axis=0)
    out[0] = (
        cotangent[0].astype(F32)
        + nt(d_node[...], w_self[...])
        + nt(d_centre[...], w_send[...])
        + nt(d_neigh[...], w_recv[...])
        + nn(hot_columns(sends[...], rows), returned)
    ).astype(BF16)


def sum_kernel(parts, out):
    total = jnp.sum(parts[...].astype(F32), axis=0).astype(BF16)
    out[...] = jnp.broadcast_to(total[None], out.shape)


def norm_kernel(total, steps):
    count, width = steps.shape[0], steps.shape[1]
    for m in range(count):
        part = total[m * width : (m + 1) * width].astype(F32)
        mean = jnp.sum(jnp.sum(part * part, axis=0, keepdims=True), axis=1, keepdims=True)
        mean = mean / (part.shape[0] * part.shape[1])
        steps[m] = part / jnp.sqrt(mean + 1e-06)


def call(kernel, outs, scratch=()):
    return pl.pallas_call(
        kernel,
        out_shape=[jax.ShapeDtypeStruct(shape, kind) for shape, kind in outs],
        scratch_shapes=scratch,
        compiler_params=pltpu.CompilerParams(vmem_limit_bytes=40 * 1024 * 1024),
        cost_estimate=pl.CostEstimate(flops=2 * 10**9, bytes_accessed=1024, transcendentals=0),
    )


def shards(
    nodes,
    leave_list,
    arrive_list,
    send_list,
    neighbours,
    valid,
    w_send,
    w_recv,
    w_msg,
    w_self,
    w_agg,
    w_out,
    cotangent,
):
    rows, width = nodes.shape[1:]
    slots = neighbours.shape[2]
    migr = leave_list.shape[1] // 2
    border = send_list.shape[1] // 2
    table_rows = rows + 2 * border
    size = lax.axis_size("slab")
    devices = size * lax.axis_size("grp")
    axes = ("grp", "slab")

    def swap(array, by):
        step = abs(by)
        pairs = [
            (i, (i + by if i // step % 2 == 0 else i - by) % size) for i in range(size)
        ]
        return lax.ppermute(array, "slab", pairs)

    message = (border + migr + CODE_ROWS, width)
    (token,) = call(first_kernel, [((8, LANES), F32)])()
    near_off, near_on, far_off, far_on = call(
        pack_kernel,
        [(message, BF16)] * 4,
    )(token, nodes, leave_list, arrive_list, send_list)
    got_on = swap(near_on, 1)
    got_far_on = swap(far_on, 2)
    got_far_off = swap(far_off, -2)
    got_off = swap(near_off, -1)

    matrices = 6
    pair_rows = rows * slots // 2
    half_rows = table_rows // 2
    hot_rows = -(-(half_rows + 1) // LANES) * LANES
    share = -(-matrices * width // (8 * devices)) * 8
    edges = rows * slots
    hot, hot_t, wide, ids, d_hid = call(
        prep_kernel,
        [
            ((edges, hot_rows), BF16),
            ((half_rows, edges), BF16),
            ((2, 2 * width, 2 * width), BF16),
            ((rows, LANES), jnp.int32),
            ((rows, width), F32),
        ],
    )(jnp.swapaxes(neighbours, 1, 2), jnp.swapaxes(valid, 1, 2), w_msg, w_out, cotangent)
    sources = (
        nodes,
        arrive_list,
        far_off,
        far_on,
        got_off,
        got_on,
        got_far_off,
        got_far_on,
        hot,
        hot_t,
        wide,
        ids,
        d_hid,
        w_send,
        w_recv,
        w_self,
        w_agg,
        w_out,
        cotangent,
    )
    updated, back_off, back_on, grads, d_node, d_centre, d_neigh = call(
        layer_kernel,
        [
            ((1, rows, width), BF16),
            ((border, width), BF16),
            ((border, width), BF16),
            ((devices * share, width), BF16),
            ((rows, width), BF16),
            ((rows, width), BF16),
            ((rows, width), BF16),
        ],
        [
            pltpu.VMEM((hot_rows, 2 * width), BF16),
            pltpu.VMEM((pair_rows, 2 * width), BF16),
            pltpu.VMEM((pair_rows, 2 * width), F32),
            pltpu.VMEM((pair_rows, 2 * width), F32),
            pltpu.VMEM((rows, width), F32),
            pltpu.VMEM((rows, width), F32),
            pltpu.VMEM((pair_rows, 2 * width), BF16),
            pltpu.VMEM((edges, 2 * width), BF16),
        ],
    )(*sources)
    got_on = swap(back_on, 1)
    got_off = swap(back_off, -1)
    parts = lax.all_to_all(
        grads.reshape(devices, share, width), axes, split_axis=0, concat_axis=0, tiled=True
    )
    sources = (
        cotangent,
        d_node,
        d_centre,
        d_neigh,
        w_self,
        w_send,
        w_recv,
        send_list,
        got_off,
        got_on,
    )
    (grad_nodes,) = call(
        finish_kernel,
        [((1, rows, width), BF16)],
    )(*sources)
    (shared,) = call(sum_kernel, [((devices, share, width), BF16)])(parts)
    total = lax.all_to_all(shared, axes, split_axis=0, concat_axis=0, tiled=True)
    total = total.reshape(devices * share, width)[: matrices * width]
    (weight_steps,) = call(norm_kernel, [((matrices, width, width), F32)])(total)
    return (updated, grad_nodes, weight_steps)


def solution(mesh):
    rows = P("grp", "slab", None)
    lists = P("grp", "slab")
    in_specs = (rows, lists, lists, lists, rows, rows, P(), P(), P(), P(), P(), P(), rows)
    out_specs = (rows, rows, P())
    return jax.shard_map(shards, mesh=mesh, in_specs=in_specs, out_specs=out_specs, check_vma=False)
```

```python
import functools

import jax
import jax.numpy as jnp
from jax import lax
from jax.experimental import pallas as pl
from jax.experimental.pallas import tpu as pltpu
from jax.sharding import PartitionSpec as P

F32 = jnp.float32
BF16 = jnp.bfloat16
CODE_ROWS = 16
LANES = 128
SLAB = ("chip", "core")
FAR = -1e30
GROUP = 32
BLOCK = 64


def nn(left, right):
    return lax.dot_general(left, right, (((1,), (0,)), ((), ())), preferred_element_type=F32)


def nt(left, right):
    return lax.dot_general(left, right, (((1,), (1,)), ((), ())), preferred_element_type=F32)


def tn(left, right):
    return lax.dot_general(left, right, (((0,), (0,)), ((), ())), preferred_element_type=F32)


def hot_columns(row, count):
    sub = lax.broadcasted_iota(jnp.int32, (count, row.shape[1]), 0)
    return jnp.where(sub == row, 1.0, 0.0).astype(BF16)


def silu_parts(half):
    tan = jnp.tanh(half)
    part = half * tan
    return half + part, (1.0 + tan) * ((1.0 + half) - part)


def first_kernel(out):
    out[...] = jnp.zeros_like(out)


def parities():
    return lax.axis_index("core") == 1, lax.rem(lax.axis_index("chip"), 2) == 1


def pack_kernel(_, nodes, leave, arrive, sends, near_off, near_on, far_off, far_on):
    odd, odd_pair = parities()
    rows = nodes.shape[1]
    migr = leave.shape[1] // 2
    border = sends.shape[1] // 2
    own = nodes[0]
    leaving = tn(hot_columns(leave[...], rows), own).astype(BF16)
    sub = lax.broadcasted_iota(jnp.int32, (rows, 2 * border), 0)
    column = jnp.transpose(
        jnp.broadcast_to(arrive[...].astype(F32), (2 * border, rows)), (1, 0)
    )
    source = jnp.sum(jnp.where(sub == sends[...], column, 0.0), axis=0, keepdims=True)
    source = source.astype(jnp.int32)
    rest = tn(hot_columns(source, rows), own).astype(BF16)
    code = jnp.where(source >= rows, source - rows, -1).astype(F32)
    messages = []
    for part in range(2):
        shifted = code if part == 0 else pltpu.roll(code, border, 1)
        messages.append(
            jnp.concatenate(
                [
                    rest[part * border : (part + 1) * border],
                    leaving[part * migr : (part + 1) * migr],
                    jnp.broadcast_to(shifted, (CODE_ROWS, 2 * border)).astype(BF16),
                ],
                axis=0,
            )
        )
    down, up = messages
    near_off[...] = jnp.where(odd, up, down)
    near_on[...] = jnp.where(odd, down, up)
    down, up = leaving[:migr], leaving[migr:]
    far_off[...] = jnp.where(odd_pair, up, down)
    far_on[...] = jnp.where(odd_pair, down, up)


def prep_kernel(nbr, valid, w_msg, w_out, cotangent, hot_o, hot_t_o, wide_o, ids_o, d_hid_o):
    slots, rows = nbr.shape[1:]
    width = w_msg.shape[0]
    half_rows, hot_rows = hot_t_o.shape[0], hot_o.shape[1]
    chunk = 4
    half_msg = 0.5 * w_msg[...].astype(F32)
    none = jnp.zeros((width, width), F32)
    for part, block in enumerate((half_msg, jnp.transpose(half_msg, (1, 0)))):
        wide_o[part] = jnp.concatenate(
            [
                jnp.concatenate([block, none], axis=1),
                jnp.concatenate([none, block], axis=1),
            ],
            axis=0,
        ).astype(BF16)
    d_hid_o[...] = nt(cotangent[0], w_out[...])
    upper = nbr[0] >= half_rows
    low_row = jnp.where(upper, nbr[0] - half_rows, nbr[0])
    index = jnp.where(valid[0] == 1, low_row, half_rows) + jnp.where(upper, hot_rows, 0)
    fill = jnp.zeros((LANES - slots, rows), jnp.int32)
    ids_o[...] = jnp.transpose(jnp.concatenate([index, fill], axis=0), (1, 0))

    lane = lax.broadcasted_iota(jnp.int32, (rows, hot_rows), 1).astype(jnp.int16)
    one = jnp.ones((rows, hot_rows), BF16)
    zero = jnp.zeros((rows, hot_rows), BF16)
    sub = lax.broadcasted_iota(jnp.int32, (half_rows, rows), 0).astype(jnp.int16)
    one_t = jnp.ones((half_rows, rows), BF16)
    zero_t = jnp.zeros((half_rows, rows), BF16)

    @pl.loop(0, slots // chunk)
    def build(step):
        for j, short in enumerate(slot_ids(ids_o, step, chunk)):
            slot = step * chunk + j
            short = (short & (hot_rows - 1)).astype(jnp.int16)
            short = jnp.concatenate([short] * (hot_rows // LANES), axis=1)
            hot_o[pl.ds(slot * rows, rows)] = jnp.where(short == lane, one, zero)
            row = nbr[0, pl.ds(slot, 1)]
            row = jnp.where(row >= half_rows, row - half_rows, row)
            short = jnp.broadcast_to(row, (16, rows)).astype(jnp.int16)
            short = jnp.concatenate([short] * (half_rows // 16), axis=0)
            hot_t_o[:, pl.ds(pl.multiple_of(slot * rows, LANES), rows)] = jnp.where(
                short == sub, one_t, zero_t
            )


def slot_ids(ids, step, chunk):
    near = pltpu.roll(ids[...], lax.rem(LANES - step * chunk, LANES), 1)
    shape = (ids.shape[0], LANES)
    return [jnp.broadcast_to(near[:, j : j + 1], shape) for j in range(chunk)]


def layer_kernel(
    nodes,
    arrive,
    my_far_off,
    my_far_on,
    got_off,
    got_on,
    got_far_off,
    got_far_on,
    hot,
    hot_t,
    wide,
    nbr_ids,
    d_hid,
    w_send,
    w_recv,
    w_self,
    w_agg,
    w_out,
    cotangent,
    updated,
    back_off,
    back_on,
    keep,
    give,
    d_node_o,
    d_centre_o,
    d_neigh_o,
    neigh_s,
    hid_s,
    ds1_s,
    ds2_s,
    agg_s,
    dcen_s,
    dpre2_s,
    dpre_s,
):
    rows, width = nodes.shape[1:]
    slots = hot.shape[0] // rows
    border, migr = back_off.shape[0], got_far_off.shape[0]
    odd, odd_pair = parities()
    low = jnp.where(odd, got_on[...], got_off[...])
    high = jnp.where(odd, got_off[...], got_on[...])
    low_far = jnp.where(odd_pair, got_far_on[...], got_far_off[...])
    high_far = jnp.where(odd_pair, got_far_off[...], got_far_on[...])
    my_up = jnp.where(odd_pair, my_far_off[...], my_far_on[...])
    my_down = jnp.where(odd_pair, my_far_on[...], my_far_off[...])
    table_rows = rows + 2 * border

    pool = jnp.concatenate(
        [nodes[0], low[border : border + migr], high[border : border + migr]], axis=0
    )
    moved = tn(hot_columns(arrive[...], pool.shape[0]), pool).astype(BF16)

    def halo(message, first, second):
        code = message[border + migr : border + migr + 8].astype(F32)[:1]
        code = code.astype(jnp.int32)
        source = jnp.concatenate([first, second], axis=0)
        extra = tn(hot_columns(code, 2 * migr), source)
        return (message[:border].astype(F32) + extra[:border]).astype(BF16)

    below = halo(low, low_far, my_down)
    above = halo(high, my_up, high_far)
    table = jnp.concatenate([moved, below, above], axis=0)

    half_rows, hot_rows = hot_t.shape[0], hot.shape[1]
    half_centre = 0.5 * nn(moved, w_send[...])
    half_neigh = (0.5 * nn(table, w_recv[...]).astype(BF16).astype(F32)).astype(BF16)
    neigh_s[:half_rows] = jnp.concatenate([half_neigh[:half_rows], half_neigh[half_rows:]], axis=1)
    neigh_s[half_rows:] = jnp.full((hot_rows - half_rows, 2 * width), FAR, BF16)
    ids = slot_ids(nbr_ids, 0, slots)
    blocks = [slice(start, start + BLOCK) for start in range(0, rows, BLOCK)]
    sides = (slice(0, width), slice(width, 2 * width))

    for first in range(0, slots, GROUP):
        gathered = nn(hot[first * rows : (first + GROUP) * rows], neigh_s[...])
        for j in range(GROUP):
            pair, side = divmod(first + j, 2)
            for block in blocks:
                pick = gathered[j * rows + block.start : j * rows + block.stop]
                pick = jnp.where(
                    ids[first + j][block] >= hot_rows, pick[:, sides[1]], pick[:, sides[0]]
                )
                act, slope = silu_parts(half_centre[block] + pick)
                at = slice(pair * rows + block.start, pair * rows + block.stop)
                ds1_s[at, sides[side]] = slope
                hid_s[at, sides[side]] = act.astype(BF16)
        base = first // 2 * rows
        halves = nn(hid_s[base : base + GROUP // 2 * rows], wide[0])
        for block in blocks:
            total = jnp.zeros((BLOCK, width), F32) if first == 0 else agg_s[block]
            for j in range(GROUP):
                pair, side = divmod(j, 2)
                at = slice(pair * rows + block.start, pair * rows + block.stop)
                act, slope = silu_parts(halves[at, sides[side]])
                total = total + act
                ds2_s[base + at.start : base + at.stop, sides[side]] = slope
            agg_s[block] = total

    agg_b = agg_s[...].astype(BF16)
    node_pre = nn(moved, w_self[...]) + nn(agg_b, w_agg[...])
    act, slope = silu_parts(0.5 * node_pre)
    node_hid = act.astype(BF16)
    updated[0] = (moved.astype(F32) + nn(node_hid, w_out[...])).astype(BF16)
    cot = cotangent[0]
    d_node = (d_hid[...] * (0.5 * slope)).astype(BF16)
    half_d_agg = 0.5 * nt(d_node, w_agg[...])

    none = jnp.zeros((BLOCK, width), BF16)
    border_id = jnp.full((BLOCK, width), hot_rows, jnp.int16)
    for first in range(0, slots, GROUP):
        base = first // 2 * rows
        span = slice(base, base + GROUP // 2 * rows)
        for pair in range(GROUP // 2):
            for block in blocks:
                at = slice(base + pair * rows + block.start, base + pair * rows + block.stop)
                for side in sides:
                    dpre2_s[at, side] = (half_d_agg[block] * ds2_s[at, side]).astype(BF16)
        d_hids = nn(dpre2_s[span], wide[1])
        for block in blocks:
            total = jnp.zeros((BLOCK, width), F32) if first == 0 else dcen_s[block]
            for j in range(GROUP):
                pair, side = divmod(j, 2)
                at = slice(pair * rows + block.start, pair * rows + block.stop)
                part = d_hids[at, sides[side]] * ds1_s[base + at.start : base + at.stop, sides[side]]
                total = total + part
                part = part.astype(BF16)
                is_up = ids[first + j][block].astype(jnp.int16) >= border_id
                at = slice((first + j) * rows + block.start, (first + j) * rows + block.stop)
                dpre_s[at, sides[0]] = jnp.where(is_up, none, part)
                dpre_s[at, sides[1]] = jnp.where(is_up, part, none)
            dcen_s[block] = total
    gmsg = tn(hid_s[...], dpre2_s[...])
    d_neigh = nn(hot_t[...], dpre_s[...]).astype(BF16)

    d_centre = dcen_s[...].astype(BF16)
    d_neigh = jnp.concatenate([d_neigh[:, :width], d_neigh[:, width:]], axis=0)
    d_borrowed = nt(d_neigh[rows:], w_recv[...]).astype(BF16)
    back_off[...] = jnp.where(odd, d_borrowed[border:], d_borrowed[:border])
    back_on[...] = jnp.where(odd, d_borrowed[:border], d_borrowed[border:])
    d_node_o[...] = d_node
    d_centre_o[...] = d_centre
    d_neigh_o[...] = d_neigh[:rows]
    parts = (
        tn(moved, d_centre),
        tn(table, d_neigh),
        gmsg[:width, :width] + gmsg[width:, width:],
        tn(moved, d_node),
        tn(agg_b, d_node),
        tn(node_hid, cot),
    )
    count = len(parts) // 2
    for m in range(count):
        at = slice(m * width, (m + 1) * width)
        keep[at] = jnp.where(odd, parts[count + m], parts[m])
        give[at] = jnp.where(odd, parts[m], parts[count + m]).astype(BF16)


def finish_kernel(
    cotangent, d_node, d_centre, d_neigh, w_self, w_send, w_recv, sends, got_off, got_on, out
):
    rows = d_node.shape[0]
    odd, _ = parities()
    from_low = jnp.where(odd, got_on[...], got_off[...])
    from_high = jnp.where(odd, got_off[...], got_on[...])
    returned = jnp.concatenate([from_low, from_high], axis=0)
    out[0] = (
        cotangent[0].astype(F32)
        + nt(d_node[...], w_self[...])
        + nt(d_centre[...], w_send[...])
        + nt(d_neigh[...], w_recv[...])
        + nn(hot_columns(sends[...], rows), returned)
    ).astype(BF16)


def add_kernel(keep, got, out):
    used = keep.shape[0]
    out[:used] = (keep[...] + got[...].astype(F32)).astype(BF16)
    if out.shape[0] > used:
        out[used:] = jnp.zeros_like(out[used:])


def sum_kernel(parts, back_off, back_on, out, back_off_o, back_on_o):
    total = jnp.sum(parts[...].astype(F32), axis=0).astype(BF16)
    out[...] = jnp.broadcast_to(total[None], out.shape)
    back_off_o[...] = back_off[...]
    back_on_o[...] = back_on[...]


def norm_kernel(mine, other, steps):
    count, width = steps.shape[0] // 2, steps.shape[1]
    odd, _ = parities()
    for m in range(2 * count):
        at = slice(m % count * width, (m % count + 1) * width)
        own, got = mine[at].astype(F32), other[at].astype(F32)
        part = jnp.where(odd, got, own) if m < count else jnp.where(odd, own, got)
        mean = jnp.sum(jnp.sum(part * part, axis=0, keepdims=True), axis=1, keepdims=True)
        mean = mean / (part.shape[0] * part.shape[1])
        steps[m] = part / jnp.sqrt(mean + 1e-06)


def call(kernel, outs, scratch=()):
    return pl.pallas_call(
        kernel,
        out_shape=[jax.ShapeDtypeStruct(shape, kind) for shape, kind in outs],
        scratch_shapes=scratch,
        compiler_params=pltpu.CompilerParams(vmem_limit_bytes=40 * 1024 * 1024),
        cost_estimate=pl.CostEstimate(flops=2 * 10**9, bytes_accessed=1024, transcendentals=0),
    )


def shards(
    nodes,
    leave_list,
    arrive_list,
    send_list,
    neighbours,
    valid,
    w_send,
    w_recv,
    w_msg,
    w_self,
    w_agg,
    w_out,
    cotangent,
):
    rows, width = nodes.shape[1:]
    slots = neighbours.shape[2]
    migr = leave_list.shape[1] // 2
    border = send_list.shape[1] // 2
    table_rows = rows + 2 * border
    size = lax.axis_size(SLAB)
    axes = ("grp", "chip")
    chips = lax.axis_size(axes)

    def swap(array, by):
        step = abs(by)
        pairs = [
            (i, (i + by if i // step % 2 == 0 else i - by) % size) for i in range(size)
        ]
        return lax.ppermute(array, SLAB, pairs)

    message = (border + migr + CODE_ROWS, width)
    (token,) = call(first_kernel, [((8, LANES), F32)])()
    near_off, near_on, far_off, far_on = call(
        pack_kernel,
        [(message, BF16)] * 2 + [((migr, width), BF16)] * 2,
    )(token, nodes, leave_list, arrive_list, send_list)
    got_on = swap(near_on, 1)
    got_off = swap(near_off, -1)
    got_far_on = swap(far_on, 2)
    got_far_off = swap(far_off, -2)

    matrices = 6
    pair_rows = rows * slots // 2
    half_rows = table_rows // 2
    hot_rows = -(-(half_rows + 1) // LANES) * LANES
    half = matrices // 2 * width
    share = -(-half // (8 * chips)) * 8
    edges = rows * slots
    hot, hot_t, wide, ids, d_hid = call(
        prep_kernel,
        [
            ((edges, hot_rows), BF16),
            ((half_rows, edges), BF16),
            ((2, 2 * width, 2 * width), BF16),
            ((rows, LANES), jnp.int32),
            ((rows, width), F32),
        ],
    )(jnp.swapaxes(neighbours, 1, 2), jnp.swapaxes(valid, 1, 2), w_msg, w_out, cotangent)
    sources = (
        nodes,
        arrive_list,
        far_off,
        far_on,
        got_off,
        got_on,
        got_far_off,
        got_far_on,
        hot,
        hot_t,
        wide,
        ids,
        d_hid,
        w_send,
        w_recv,
        w_self,
        w_agg,
        w_out,
        cotangent,
    )
    updated, back_off, back_on, keep, give, d_node, d_centre, d_neigh = call(
        layer_kernel,
        [
            ((1, rows, width), BF16),
            ((border, width), BF16),
            ((border, width), BF16),
            ((half, width), F32),
            ((half, width), BF16),
            ((rows, width), BF16),
            ((rows, width), BF16),
            ((rows, width), BF16),
        ],
        [
            pltpu.VMEM((hot_rows, 2 * width), BF16),
            pltpu.VMEM((pair_rows, 2 * width), BF16),
            pltpu.VMEM((pair_rows, 2 * width), F32),
            pltpu.VMEM((pair_rows, 2 * width), F32),
            pltpu.VMEM((rows, width), F32),
            pltpu.VMEM((rows, width), F32),
            pltpu.VMEM((pair_rows, 2 * width), BF16),
            pltpu.VMEM((edges, 2 * width), BF16),
        ],
    )(*sources)
    (chip,) = call(add_kernel, [((chips * share, width), BF16)])(keep, swap(give, 1))
    parts = lax.all_to_all(
        chip.reshape(chips, share, width), axes, split_axis=0, concat_axis=0, tiled=True
    )
    shared, back_off, back_on = call(
        sum_kernel,
        [((chips, share, width), BF16), ((border, width), BF16), ((border, width), BF16)],
    )(parts, back_off, back_on)
    got_on = swap(back_on, 1)
    got_off = swap(back_off, -1)
    sources = (
        cotangent,
        d_node,
        d_centre,
        d_neigh,
        w_self,
        w_send,
        w_recv,
        send_list,
        got_off,
        got_on,
    )
    (grad_nodes,) = call(
        finish_kernel,
        [((1, rows, width), BF16)],
    )(*sources)
    total = lax.all_to_all(shared, axes, split_axis=0, concat_axis=0, tiled=True)
    total = total.reshape(chips * share, width)[:half]
    (weight_steps,) = call(norm_kernel, [((matrices, width, width), F32)])(total, swap(total, 1))
    return (updated, grad_nodes, weight_steps)


def solution(mesh):
    groups, slabs = mesh.devices.shape
    mesh = jax.sharding.Mesh(mesh.devices.reshape(groups, slabs // 2, 2), ("grp", *SLAB))
    rows = P("grp", SLAB, None)
    lists = P("grp", SLAB)
    in_specs = (rows, lists, lists, lists, rows, rows, P(), P(), P(), P(), P(), P(), rows)
    out_specs = (rows, rows, P())
    return jax.shard_map(shards, mesh=mesh, in_specs=in_specs, out_specs=out_specs, check_vma=False)
```

```python
import functools

import jax
import jax.numpy as jnp
from jax import lax
from jax.experimental import pallas as pl
from jax.experimental.pallas import tpu as pltpu
from jax.sharding import PartitionSpec as P

F32 = jnp.float32
BF16 = jnp.bfloat16
CODE_ROWS = 16
LANES = 128
FAR = -1e30
GROUP = 32
BLOCK = 64


def nn(left, right):
    return lax.dot_general(left, right, (((1,), (0,)), ((), ())), preferred_element_type=F32)


def nt(left, right):
    return lax.dot_general(left, right, (((1,), (1,)), ((), ())), preferred_element_type=F32)


def tn(left, right):
    return lax.dot_general(left, right, (((0,), (0,)), ((), ())), preferred_element_type=F32)


def hot_columns(row, count):
    sub = lax.broadcasted_iota(jnp.int32, (count, row.shape[1]), 0)
    return jnp.where(sub == row, 1.0, 0.0).astype(BF16)


def silu_parts(half):
    tan = jnp.tanh(half)
    part = half * tan
    return half + part, (1.0 + tan) * ((1.0 + half) - part)


def first_kernel(out):
    out[...] = jnp.zeros_like(out)


def is_odd():
    return lax.rem(lax.axis_index("slab"), 2) == 1


def pack_kernel(_, nodes, leave, arrive, sends, near_off, near_on, far_up, far_down):
    odd = is_odd()
    rows = nodes.shape[1]
    migr = leave.shape[1] // 2
    border = sends.shape[1] // 2
    own = nodes[0]
    leaving = tn(hot_columns(leave[...], rows), own).astype(BF16)
    sub = lax.broadcasted_iota(jnp.int32, (rows, 2 * border), 0)
    column = jnp.transpose(
        jnp.broadcast_to(arrive[...].astype(F32), (2 * border, rows)), (1, 0)
    )
    source = jnp.sum(jnp.where(sub == sends[...], column, 0.0), axis=0, keepdims=True)
    source = source.astype(jnp.int32)
    rest = tn(hot_columns(source, rows), own).astype(BF16)
    code = jnp.where(source >= rows, source - rows, -1).astype(F32)
    messages = []
    for part in range(2):
        shifted = code if part == 0 else pltpu.roll(code, border, 1)
        messages.append(
            jnp.concatenate(
                [
                    rest[part * border : (part + 1) * border],
                    leaving[part * migr : (part + 1) * migr],
                    jnp.broadcast_to(shifted, (CODE_ROWS, 2 * border)).astype(BF16),
                ],
                axis=0,
            )
        )
    down, up = messages
    near_off[...] = jnp.where(odd, up, down)
    near_on[...] = jnp.where(odd, down, up)
    far_down[...], far_up[...] = leaving[:migr], leaving[migr:]


def prep_kernel(
    arrive, nbr, valid, w_msg, w_out, cotangent, hot_o, hot_t_o, wide_o, ids_o, d_hid_o, moves_o
):
    slots, rows = nbr.shape[1:]
    width = w_msg.shape[0]
    half_rows, hot_rows = hot_t_o.shape[0], hot_o.shape[1]
    chunk = 4
    half_msg = 0.5 * w_msg[...].astype(F32)
    none = jnp.zeros((width, width), F32)
    for part, block in enumerate((half_msg, jnp.transpose(half_msg, (1, 0)))):
        wide_o[part] = jnp.concatenate(
            [
                jnp.concatenate([block, none], axis=1),
                jnp.concatenate([none, block], axis=1),
            ],
            axis=0,
        ).astype(BF16)
    d_hid_o[...] = nt(cotangent[0], w_out[...])
    sub = lax.broadcasted_iota(jnp.int32, (moves_o.shape[1], rows), 0)
    moves = jnp.where(sub == arrive[...], 1.0, 0.0)
    moves_o[...] = jnp.transpose(moves, (1, 0)).astype(BF16)
    upper = nbr[0] >= half_rows
    low_row = jnp.where(upper, nbr[0] - half_rows, nbr[0])
    index = jnp.where(valid[0] == 1, low_row, half_rows) + jnp.where(upper, hot_rows, 0)
    fill = jnp.zeros((LANES - slots, rows), jnp.int32)
    ids_o[...] = jnp.transpose(jnp.concatenate([index, fill], axis=0), (1, 0))

    lane = lax.broadcasted_iota(jnp.int32, (rows, hot_rows), 1).astype(jnp.int16)
    one = jnp.ones((rows, hot_rows), BF16)
    zero = jnp.zeros((rows, hot_rows), BF16)
    sub = lax.broadcasted_iota(jnp.int32, (half_rows, rows), 0).astype(jnp.int16)
    one_t = jnp.ones((half_rows, rows), BF16)
    zero_t = jnp.zeros((half_rows, rows), BF16)

    @pl.loop(0, slots // chunk)
    def build(step):
        for j, short in enumerate(slot_ids(ids_o, step, chunk)):
            slot = step * chunk + j
            short = (short & (hot_rows - 1)).astype(jnp.int16)
            short = jnp.concatenate([short] * (hot_rows // LANES), axis=1)
            hot_o[pl.ds(slot * rows, rows)] = jnp.where(short == lane, one, zero)
            row = nbr[0, pl.ds(slot, 1)]
            row = jnp.where(row >= half_rows, row - half_rows, row)
            short = jnp.broadcast_to(row, (16, rows)).astype(jnp.int16)
            short = jnp.concatenate([short] * (half_rows // 16), axis=0)
            hot_t_o[:, pl.ds(pl.multiple_of(slot * rows, LANES), rows)] = jnp.where(
                short == sub, one_t, zero_t
            )


def slot_ids(ids, step, chunk):
    near = pltpu.roll(ids[...], lax.rem(LANES - step * chunk, LANES), 1)
    shape = (ids.shape[0], LANES)
    return [jnp.broadcast_to(near[:, j : j + 1], shape) for j in range(chunk)]


def layer_kernel(
    nodes,
    moves,
    my_up,
    my_down,
    got_off,
    got_on,
    low_far,
    high_far,
    hot,
    hot_t,
    wide,
    nbr_ids,
    d_hid,
    w_send,
    w_recv,
    w_self,
    w_agg,
    w_out,
    cotangent,
    updated,
    back_off,
    back_on,
    grads,
    d_node_o,
    d_centre_o,
    d_neigh_o,
    neigh_s,
    hid_s,
    ds1_s,
    ds2_s,
    agg_s,
    dcen_s,
    dpre2_s,
    dpre_s,
):
    rows, width = nodes.shape[1:]
    slots = hot.shape[0] // rows
    border, migr = back_off.shape[0], low_far.shape[0]
    odd = is_odd()
    low = jnp.where(odd, got_on[...], got_off[...])
    high = jnp.where(odd, got_off[...], got_on[...])

    pool = jnp.concatenate(
        [nodes[0], low[border : border + migr], high[border : border + migr]], axis=0
    )
    moved = nn(moves[...], pool).astype(BF16)

    def halo(message, first, second):
        code = message[border + migr : border + migr + 8].astype(F32)[:1]
        code = code.astype(jnp.int32)
        source = jnp.concatenate([first, second], axis=0)
        extra = tn(hot_columns(code, 2 * migr), source)
        return (message[:border].astype(F32) + extra[:border]).astype(BF16)

    below = halo(low, low_far[...], my_down[...])
    above = halo(high, my_up[...], high_far[...])
    table = jnp.concatenate([moved, below, above], axis=0)

    half_rows, hot_rows = hot_t.shape[0], hot.shape[1]
    half_centre = 0.5 * nn(moved, w_send[...])
    half_neigh = (0.5 * nn(table, w_recv[...]).astype(BF16).astype(F32)).astype(BF16)
    neigh_s[:half_rows] = jnp.concatenate([half_neigh[:half_rows], half_neigh[half_rows:]], axis=1)
    neigh_s[half_rows:] = jnp.full((hot_rows - half_rows, 2 * width), FAR, BF16)
    ids = slot_ids(nbr_ids, 0, slots)
    blocks = [slice(start, start + BLOCK) for start in range(0, rows, BLOCK)]
    sides = (slice(0, width), slice(width, 2 * width))

    for first in range(0, slots, GROUP):
        gathered = nn(hot[first * rows : (first + GROUP) * rows], neigh_s[...])
        for j in range(GROUP):
            pair, side = divmod(first + j, 2)
            for block in blocks:
                pick = gathered[j * rows + block.start : j * rows + block.stop]
                pick = jnp.where(
                    ids[first + j][block] >= hot_rows, pick[:, sides[1]], pick[:, sides[0]]
                )
                act, slope = silu_parts(half_centre[block] + pick)
                at = slice(pair * rows + block.start, pair * rows + block.stop)
                ds1_s[at, sides[side]] = slope
                hid_s[at, sides[side]] = act.astype(BF16)
        base = first // 2 * rows
        halves = nn(hid_s[base : base + GROUP // 2 * rows], wide[0])
        for block in blocks:
            total = jnp.zeros((BLOCK, width), F32) if first == 0 else agg_s[block]
            for j in range(GROUP):
                pair, side = divmod(j, 2)
                at = slice(pair * rows + block.start, pair * rows + block.stop)
                act, slope = silu_parts(halves[at, sides[side]])
                total = total + act
                ds2_s[base + at.start : base + at.stop, sides[side]] = slope
            agg_s[block] = total

    agg_b = agg_s[...].astype(BF16)
    node_pre = nn(moved, w_self[...]) + nn(agg_b, w_agg[...])
    act, slope = silu_parts(0.5 * node_pre)
    node_hid = act.astype(BF16)
    updated[0] = (moved.astype(F32) + nn(node_hid, w_out[...])).astype(BF16)
    cot = cotangent[0]
    d_node = (d_hid[...] * (0.5 * slope)).astype(BF16)
    half_d_agg = 0.5 * nt(d_node, w_agg[...])

    def store(m, gradient):
        grads[m * width : (m + 1) * width] = gradient.astype(BF16)

    store(3, tn(moved, d_node))
    store(4, tn(agg_b, d_node))
    store(5, tn(node_hid, cot))

    none = jnp.zeros((BLOCK, width), BF16)
    border_id = jnp.full((BLOCK, width), hot_rows, jnp.int16)
    for first in range(0, slots, GROUP):
        base = first // 2 * rows
        span = slice(base, base + GROUP // 2 * rows)
        for pair in range(GROUP // 2):
            for block in blocks:
                at = slice(base + pair * rows + block.start, base + pair * rows + block.stop)
                for side in sides:
                    dpre2_s[at, side] = (half_d_agg[block] * ds2_s[at, side]).astype(BF16)
        d_hids = nn(dpre2_s[span], wide[1])
        for block in blocks:
            total = jnp.zeros((BLOCK, width), F32) if first == 0 else dcen_s[block]
            for j in range(GROUP):
                pair, side = divmod(j, 2)
                at = slice(pair * rows + block.start, pair * rows + block.stop)
                part = d_hids[at, sides[side]] * ds1_s[base + at.start : base + at.stop, sides[side]]
                total = total + part
                part = part.astype(BF16)
                is_up = ids[first + j][block].astype(jnp.int16) >= border_id
                at = slice((first + j) * rows + block.start, (first + j) * rows + block.stop)
                dpre_s[at, sides[0]] = jnp.where(is_up, none, part)
                dpre_s[at, sides[1]] = jnp.where(is_up, part, none)
            dcen_s[block] = total
    gmsg = tn(hid_s[...], dpre2_s[...])
    d_neigh = nn(hot_t[...], dpre_s[...]).astype(BF16)

    d_centre = dcen_s[...].astype(BF16)
    d_neigh = jnp.concatenate([d_neigh[:, :width], d_neigh[:, width:]], axis=0)
    d_borrowed = nt(d_neigh[rows:], w_recv[...]).astype(BF16)
    back_off[...] = jnp.where(odd, d_borrowed[border:], d_borrowed[:border])
    back_on[...] = jnp.where(odd, d_borrowed[:border], d_borrowed[border:])
    d_node_o[...] = d_node
    d_centre_o[...] = d_centre
    d_neigh_o[...] = d_neigh[:rows]
    store(2, gmsg[:width, :width] + gmsg[width:, width:])
    store(0, tn(moved, d_centre))
    store(1, tn(table, d_neigh))
    used = 6 * width
    if grads.shape[0] > used:
        grads[used:] = jnp.zeros_like(grads[used:])


def finish_kernel(
    cotangent, d_node, d_centre, d_neigh, w_self, w_send, w_recv, sends, got_off, got_on, out
):
    rows = d_node.shape[0]
    odd = is_odd()
    from_low = jnp.where(odd, got_on[...], got_off[...])
    from_high = jnp.where(odd, got_off[...], got_on[...])
    returned = jnp.concatenate([from_low, from_high], axis=0)
    out[0] = (
        cotangent[0].astype(F32)
        + nt(d_node[...], w_self[...])
        + nt(d_centre[...], w_send[...])
        + nt(d_neigh[...], w_recv[...])
        + nn(hot_columns(sends[...], rows), returned)
    ).astype(BF16)


def sum_kernel(parts, out):
    total = jnp.sum(parts[...].astype(F32), axis=0).astype(BF16)
    out[...] = jnp.broadcast_to(total[None], out.shape)


def norm_kernel(total, steps):
    count, width = steps.shape[0], steps.shape[1]
    for m in range(count):
        part = total[m * width : (m + 1) * width].astype(F32)
        mean = jnp.sum(jnp.sum(part * part, axis=0, keepdims=True), axis=1, keepdims=True)
        mean = mean / (part.shape[0] * part.shape[1])
        steps[m] = part / jnp.sqrt(mean + 1e-06)


def call(kernel, outs, scratch=()):
    return pl.pallas_call(
        kernel,
        out_shape=[jax.ShapeDtypeStruct(shape, kind) for shape, kind in outs],
        scratch_shapes=scratch,
        compiler_params=pltpu.CompilerParams(vmem_limit_bytes=40 * 1024 * 1024),
        cost_estimate=pl.CostEstimate(flops=2 * 10**9, bytes_accessed=1024, transcendentals=0),
    )


def shards(
    nodes,
    leave_list,
    arrive_list,
    send_list,
    neighbours,
    valid,
    w_send,
    w_recv,
    w_msg,
    w_self,
    w_agg,
    w_out,
    cotangent,
):
    rows, width = nodes.shape[1:]
    slots = neighbours.shape[2]
    migr = leave_list.shape[1] // 2
    border = send_list.shape[1] // 2
    table_rows = rows + 2 * border
    size = lax.axis_size("slab")
    devices = size * lax.axis_size("grp")
    axes = ("grp", "slab")

    def shift(array, by):
        return lax.ppermute(array, "slab", [(i, (i + by) % size) for i in range(size)])

    def swap(array, by):
        pairs = [(i, (i + (by if i % 2 == 0 else -by)) % size) for i in range(size)]
        return lax.ppermute(array, "slab", pairs)

    message = (border + migr + CODE_ROWS, width)
    (token,) = call(first_kernel, [((8, LANES), F32)])()
    near_off, near_on, far_up, far_down = call(
        pack_kernel,
        [(message, BF16)] * 2 + [((migr, width), BF16)] * 2,
    )(token, nodes, leave_list, arrive_list, send_list)
    got_on = swap(near_on, 1)
    got_off = swap(near_off, -1)
    high_far = shift(far_down, -2)
    low_far = shift(far_up, 2)

    matrices = 6
    pair_rows = rows * slots // 2
    half_rows = table_rows // 2
    hot_rows = -(-(half_rows + 1) // LANES) * LANES
    share = -(-matrices * width // (8 * devices)) * 8
    edges = rows * slots
    hot, hot_t, wide, ids, d_hid, moves = call(
        prep_kernel,
        [
            ((edges, hot_rows), BF16),
            ((half_rows, edges), BF16),
            ((2, 2 * width, 2 * width), BF16),
            ((rows, LANES), jnp.int32),
            ((rows, width), F32),
            ((rows, rows + 2 * migr), BF16),
        ],
    )(arrive_list, jnp.swapaxes(neighbours, 1, 2), jnp.swapaxes(valid, 1, 2), w_msg, w_out, cotangent)
    sources = (
        nodes,
        moves,
        far_up,
        far_down,
        got_off,
        got_on,
        low_far,
        high_far,
        hot,
        hot_t,
        wide,
        ids,
        d_hid,
        w_send,
        w_recv,
        w_self,
        w_agg,
        w_out,
        cotangent,
    )
    updated, back_off, back_on, grads, d_node, d_centre, d_neigh = call(
        layer_kernel,
        [
            ((1, rows, width), BF16),
            ((border, width), BF16),
            ((border, width), BF16),
            ((devices * share, width), BF16),
            ((rows, width), BF16),
            ((rows, width), BF16),
            ((rows, width), BF16),
        ],
        [
            pltpu.VMEM((hot_rows, 2 * width), BF16),
            pltpu.VMEM((pair_rows, 2 * width), BF16),
            pltpu.VMEM((pair_rows, 2 * width), F32),
            pltpu.VMEM((pair_rows, 2 * width), F32),
            pltpu.VMEM((rows, width), F32),
            pltpu.VMEM((rows, width), F32),
            pltpu.VMEM((pair_rows, 2 * width), BF16),
            pltpu.VMEM((edges, 2 * width), BF16),
        ],
    )(*sources)
    got_on = swap(back_on, 1)
    got_off = swap(back_off, -1)
    parts = lax.all_to_all(
        grads.reshape(devices, share, width), axes, split_axis=0, concat_axis=0, tiled=True
    )
    sources = (
        cotangent,
        d_node,
        d_centre,
        d_neigh,
        w_self,
        w_send,
        w_recv,
        send_list,
        got_off,
        got_on,
    )
    (grad_nodes,) = call(
        finish_kernel,
        [((1, rows, width), BF16)],
    )(*sources)
    (shared,) = call(sum_kernel, [((devices, share, width), BF16)])(parts)
    total = lax.all_to_all(shared, axes, split_axis=0, concat_axis=0, tiled=True)
    total = total.reshape(devices * share, width)[: matrices * width]
    (weight_steps,) = call(norm_kernel, [((matrices, width, width), F32)])(total)
    return (updated, grad_nodes, weight_steps)


def solution(mesh):
    rows = P("grp", "slab", None)
    lists = P("grp", "slab")
    in_specs = (rows, lists, lists, lists, rows, rows, P(), P(), P(), P(), P(), P(), rows)
    out_specs = (rows, rows, P())
    return jax.shard_map(shards, mesh=mesh, in_specs=in_specs, out_specs=out_specs, check_vma=False)
```

```python
import functools

import jax
import jax.numpy as jnp
from jax import lax
from jax.experimental import pallas as pl
from jax.experimental.pallas import tpu as pltpu
from jax.sharding import PartitionSpec as P

F32 = jnp.float32
BF16 = jnp.bfloat16
CODE_ROWS = 16
LANES = 128
FAR = -1e30
GROUP = 32
BLOCK = 64


def nn(left, right):
    return lax.dot_general(left, right, (((1,), (0,)), ((), ())), preferred_element_type=F32)


def nt(left, right):
    return lax.dot_general(left, right, (((1,), (1,)), ((), ())), preferred_element_type=F32)


def tn(left, right):
    return lax.dot_general(left, right, (((0,), (0,)), ((), ())), preferred_element_type=F32)


def hot_columns(row, count):
    sub = lax.broadcasted_iota(jnp.int32, (count, row.shape[1]), 0)
    return jnp.where(sub == row, 1.0, 0.0).astype(BF16)


def silu_parts(half):
    tan = jnp.tanh(half.astype(BF16)).astype(F32)
    part = half * tan
    return half + part, (1.0 + tan) * ((1.0 + half) - part)


def first_kernel(out):
    out[...] = jnp.zeros_like(out)


def parities():
    slab = lax.axis_index("slab")
    return lax.rem(slab, 2) == 1, lax.rem(slab // 2, 2) == 1


def pack_kernel(_, nodes, leave, arrive, sends, near_off, near_on, far_off, far_on):
    odd, odd_pair = parities()
    rows = nodes.shape[1]
    migr = leave.shape[1] // 2
    border = sends.shape[1] // 2
    own = nodes[0]
    leaving = tn(hot_columns(leave[...], rows), own).astype(BF16)
    sub = lax.broadcasted_iota(jnp.int32, (rows, 2 * border), 0)
    column = jnp.transpose(
        jnp.broadcast_to(arrive[...].astype(F32), (2 * border, rows)), (1, 0)
    )
    source = jnp.sum(jnp.where(sub == sends[...], column, 0.0), axis=0, keepdims=True)
    source = source.astype(jnp.int32)
    rest = tn(hot_columns(source, rows), own).astype(BF16)
    code = jnp.where(source >= rows, source - rows, -1).astype(F32)
    messages = []
    for part in range(2):
        shifted = code if part == 0 else pltpu.roll(code, border, 1)
        messages.append(
            jnp.concatenate(
                [
                    rest[part * border : (part + 1) * border],
                    leaving[part * migr : (part + 1) * migr],
                    jnp.broadcast_to(shifted, (CODE_ROWS, 2 * border)).astype(BF16),
                ],
                axis=0,
            )
        )
    down, up = messages
    near_off[...] = jnp.where(odd, up, down)
    near_on[...] = jnp.where(odd, down, up)
    down, up = leaving[:migr], leaving[migr:]
    far_off[...] = jnp.where(odd_pair, up, down)
    far_on[...] = jnp.where(odd_pair, down, up)


def prep_kernel(nbr, valid, w_msg, w_out, cotangent, hot_o, hot_t_o, wide_o, ids_o, d_hid_o):
    slots, rows = nbr.shape[1:]
    width = w_msg.shape[0]
    half_rows, hot_rows = hot_t_o.shape[0], hot_o.shape[1]
    chunk = 4
    half_msg = 0.5 * w_msg[...].astype(F32)
    none = jnp.zeros((width, width), F32)
    for part, block in enumerate((half_msg, jnp.transpose(half_msg, (1, 0)))):
        wide_o[part] = jnp.concatenate(
            [
                jnp.concatenate([block, none], axis=1),
                jnp.concatenate([none, block], axis=1),
            ],
            axis=0,
        ).astype(BF16)
    d_hid_o[...] = nt(cotangent[0], w_out[...])
    upper = nbr[0] >= half_rows
    low_row = jnp.where(upper, nbr[0] - half_rows, nbr[0])
    index = jnp.where(valid[0] == 1, low_row, half_rows) + jnp.where(upper, hot_rows, 0)
    fill = jnp.zeros((LANES - slots, rows), jnp.int32)
    ids_o[...] = jnp.transpose(jnp.concatenate([index, fill], axis=0), (1, 0))

    lane = lax.broadcasted_iota(jnp.int32, (rows, hot_rows), 1).astype(jnp.int16)
    one = jnp.ones((rows, hot_rows), BF16)
    zero = jnp.zeros((rows, hot_rows), BF16)
    sub = lax.broadcasted_iota(jnp.int32, (half_rows, rows), 0).astype(jnp.int16)
    one_t = jnp.ones((half_rows, rows), BF16)
    zero_t = jnp.zeros((half_rows, rows), BF16)

    @pl.loop(0, slots // chunk)
    def build(step):
        for j, short in enumerate(slot_ids(ids_o, step, chunk)):
            slot = step * chunk + j
            short = (short & (hot_rows - 1)).astype(jnp.int16)
            short = jnp.concatenate([short] * (hot_rows // LANES), axis=1)
            hot_o[pl.ds(slot * rows, rows)] = jnp.where(short == lane, one, zero)
            row = nbr[0, pl.ds(slot, 1)]
            row = jnp.where(row >= half_rows, row - half_rows, row)
            short = jnp.broadcast_to(row, (16, rows)).astype(jnp.int16)
            short = jnp.concatenate([short] * (half_rows // 16), axis=0)
            hot_t_o[:, pl.ds(pl.multiple_of(slot * rows, LANES), rows)] = jnp.where(
                short == sub, one_t, zero_t
            )


def slot_ids(ids, step, chunk):
    near = pltpu.roll(ids[...], lax.rem(LANES - step * chunk, LANES), 1)
    shape = (ids.shape[0], LANES)
    return [jnp.broadcast_to(near[:, j : j + 1], shape) for j in range(chunk)]


def layer_kernel(
    nodes,
    arrive,
    my_far_off,
    my_far_on,
    got_off,
    got_on,
    got_far_off,
    got_far_on,
    hot,
    hot_t,
    wide,
    nbr_ids,
    d_hid,
    w_send,
    w_recv,
    w_self,
    w_agg,
    w_out,
    cotangent,
    updated,
    back_off,
    back_on,
    grads,
    d_node_o,
    d_centre_o,
    d_neigh_o,
    neigh_s,
    hid_s,
    ds1_s,
    ds2_s,
    agg_s,
    dcen_s,
    dpre2_s,
    dpre_s,
):
    rows, width = nodes.shape[1:]
    slots = hot.shape[0] // rows
    border, migr = back_off.shape[0], got_far_off.shape[0]
    odd, odd_pair = parities()
    low = jnp.where(odd, got_on[...], got_off[...])
    high = jnp.where(odd, got_off[...], got_on[...])
    low_far = jnp.where(odd_pair, got_far_on[...], got_far_off[...])
    high_far = jnp.where(odd_pair, got_far_off[...], got_far_on[...])
    my_up = jnp.where(odd_pair, my_far_off[...], my_far_on[...])
    my_down = jnp.where(odd_pair, my_far_on[...], my_far_off[...])
    table_rows = rows + 2 * border

    pool = jnp.concatenate(
        [nodes[0], low[border : border + migr], high[border : border + migr]], axis=0
    )
    moved = tn(hot_columns(arrive[...], pool.shape[0]), pool).astype(BF16)

    def halo(message, first, second):
        code = message[border + migr : border + migr + 8].astype(F32)[:1]
        code = code.astype(jnp.int32)
        source = jnp.concatenate([first, second], axis=0)
        extra = tn(hot_columns(code, 2 * migr), source)
        return (message[:border].astype(F32) + extra[:border]).astype(BF16)

    below = halo(low, low_far, my_down)
    above = halo(high, my_up, high_far)
    table = jnp.concatenate([moved, below, above], axis=0)

    half_rows, hot_rows = hot_t.shape[0], hot.shape[1]
    half_centre = 0.5 * nn(moved, w_send[...])
    half_neigh = (0.5 * nn(table, w_recv[...]).astype(BF16).astype(F32)).astype(BF16)
    neigh_s[:half_rows] = jnp.concatenate([half_neigh[:half_rows], half_neigh[half_rows:]], axis=1)
    neigh_s[half_rows:] = jnp.full((hot_rows - half_rows, 2 * width), FAR, BF16)
    ids = slot_ids(nbr_ids, 0, slots)
    blocks = [slice(start, start + BLOCK) for start in range(0, rows, BLOCK)]
    sides = (slice(0, width), slice(width, 2 * width))

    for first in range(0, slots, GROUP):
        gathered = nn(hot[first * rows : (first + GROUP) * rows], neigh_s[...])
        for j in range(GROUP):
            pair, side = divmod(first + j, 2)
            for block in blocks:
                pick = gathered[j * rows + block.start : j * rows + block.stop]
                pick = jnp.where(
                    ids[first + j][block] >= hot_rows, pick[:, sides[1]], pick[:, sides[0]]
                )
                act, slope = silu_parts(half_centre[block] + pick)
                at = slice(pair * rows + block.start, pair * rows + block.stop)
                ds1_s[at, sides[side]] = slope.astype(BF16)
                hid_s[at, sides[side]] = act.astype(BF16)
        base = first // 2 * rows
        halves = nn(hid_s[base : base + GROUP // 2 * rows], wide[0])
        for block in blocks:
            total = jnp.zeros((BLOCK, width), F32) if first == 0 else agg_s[block]
            for j in range(GROUP):
                pair, side = divmod(j, 2)
                at = slice(pair * rows + block.start, pair * rows + block.stop)
                act, slope = silu_parts(halves[at, sides[side]])
                total = total + act
                ds2_s[base + at.start : base + at.stop, sides[side]] = slope.astype(BF16)
            agg_s[block] = total

    agg_b = agg_s[...].astype(BF16)
    node_pre = nn(moved, w_self[...]) + nn(agg_b, w_agg[...])
    act, slope = silu_parts(0.5 * node_pre)
    node_hid = act.astype(BF16)
    updated[0] = (moved.astype(F32) + nn(node_hid, w_out[...])).astype(BF16)
    cot = cotangent[0]
    d_node = (d_hid[...] * (0.5 * slope)).astype(BF16)
    half_d_agg = 0.5 * nt(d_node, w_agg[...])

    none = jnp.zeros((BLOCK, width), BF16)
    border_id = jnp.full((BLOCK, width), hot_rows, jnp.int16)
    for first in range(0, slots, GROUP):
        base = first // 2 * rows
        span = slice(base, base + GROUP // 2 * rows)
        for pair in range(GROUP // 2):
            for block in blocks:
                at = slice(base + pair * rows + block.start, base + pair * rows + block.stop)
                for side in sides:
                    dpre2_s[at, side] = (half_d_agg[block] * ds2_s[at, side]).astype(BF16)
        d_hids = nn(dpre2_s[span], wide[1])
        for block in blocks:
            total = jnp.zeros((BLOCK, width), F32) if first == 0 else dcen_s[block]
            for j in range(GROUP):
                pair, side = divmod(j, 2)
                at = slice(pair * rows + block.start, pair * rows + block.stop)
                part = d_hids[at, sides[side]] * ds1_s[base + at.start : base + at.stop, sides[side]]
                total = total + part
                part = part.astype(BF16)
                is_up = ids[first + j][block].astype(jnp.int16) >= border_id
                at = slice((first + j) * rows + block.start, (first + j) * rows + block.stop)
                dpre_s[at, sides[0]] = jnp.where(is_up, none, part)
                dpre_s[at, sides[1]] = jnp.where(is_up, part, none)
            dcen_s[block] = total
    gmsg = tn(hid_s[...], dpre2_s[...])
    d_neigh = nn(hot_t[...], dpre_s[...]).astype(BF16)

    d_centre = dcen_s[...].astype(BF16)
    d_neigh = jnp.concatenate([d_neigh[:, :width], d_neigh[:, width:]], axis=0)
    d_borrowed = nt(d_neigh[rows:], w_recv[...]).astype(BF16)
    back_off[...] = jnp.where(odd, d_borrowed[border:], d_borrowed[:border])
    back_on[...] = jnp.where(odd, d_borrowed[:border], d_borrowed[border:])
    d_node_o[...] = d_node
    d_centre_o[...] = d_centre
    d_neigh_o[...] = d_neigh[:rows]
    parts = (
        tn(moved, d_centre),
        tn(table, d_neigh),
        gmsg[:width, :width] + gmsg[width:, width:],
        tn(moved, d_node),
        tn(agg_b, d_node),
        tn(node_hid, cot),
    )
    for m, part in enumerate(parts):
        grads[m * width : (m + 1) * width] = part.astype(BF16)
    used = len(parts) * width
    if grads.shape[0] > used:
        grads[used:] = jnp.zeros_like(grads[used:])


def finish_kernel(
    cotangent, d_node, d_centre, d_neigh, w_self, w_send, w_recv, sends, got_off, got_on, out
):
    rows = d_node.shape[0]
    odd, _ = parities()
    from_low = jnp.where(odd, got_on[...], got_off[...])
    from_high = jnp.where(odd, got_off[...], got_on[...])
    returned = jnp.concatenate([from_low, from_high], axis=0)
    out[0] = (
        cotangent[0].astype(F32)
        + nt(d_node[...], w_self[...])
        + nt(d_centre[...], w_send[...])
        + nt(d_neigh[...], w_recv[...])
        + nn(hot_columns(sends[...], rows), returned)
    ).astype(BF16)


def sum_kernel(parts, out):
    total = jnp.sum(parts[...].astype(F32), axis=0).astype(BF16)
    out[...] = jnp.broadcast_to(total[None], out.shape)


def norm_kernel(total, steps):
    count, width = steps.shape[0], steps.shape[1]
    for m in range(count):
        part = total[m * width : (m + 1) * width].astype(F32)
        mean = jnp.sum(jnp.sum(part * part, axis=0, keepdims=True), axis=1, keepdims=True)
        mean = mean / (part.shape[0] * part.shape[1])
        steps[m] = part / jnp.sqrt(mean + 1e-06)


def call(kernel, outs, scratch=()):
    return pl.pallas_call(
        kernel,
        out_shape=[jax.ShapeDtypeStruct(shape, kind) for shape, kind in outs],
        scratch_shapes=scratch,
        compiler_params=pltpu.CompilerParams(vmem_limit_bytes=40 * 1024 * 1024),
        cost_estimate=pl.CostEstimate(flops=2 * 10**9, bytes_accessed=1024, transcendentals=0),
    )


def shards(
    nodes,
    leave_list,
    arrive_list,
    send_list,
    neighbours,
    valid,
    w_send,
    w_recv,
    w_msg,
    w_self,
    w_agg,
    w_out,
    cotangent,
):
    rows, width = nodes.shape[1:]
    slots = neighbours.shape[2]
    migr = leave_list.shape[1] // 2
    border = send_list.shape[1] // 2
    table_rows = rows + 2 * border
    size = lax.axis_size("slab")
    devices = size * lax.axis_size("grp")
    axes = ("grp", "slab")

    def swap(array, by):
        step = abs(by)
        pairs = [
            (i, (i + by if i // step % 2 == 0 else i - by) % size) for i in range(size)
        ]
        return lax.ppermute(array, "slab", pairs)

    message = (border + migr + CODE_ROWS, width)
    (token,) = call(first_kernel, [((8, LANES), F32)])()
    near_off, near_on, far_off, far_on = call(
        pack_kernel,
        [(message, BF16)] * 2 + [((migr, width), BF16)] * 2,
    )(token, nodes, leave_list, arrive_list, send_list)
    got_on = swap(near_on, 1)
    got_off = swap(near_off, -1)
    got_far_on = swap(far_on, 2)
    got_far_off = swap(far_off, -2)

    matrices = 6
    pair_rows = rows * slots // 2
    half_rows = table_rows // 2
    hot_rows = -(-(half_rows + 1) // LANES) * LANES
    share = -(-matrices * width // (8 * devices)) * 8
    edges = rows * slots
    hot, hot_t, wide, ids, d_hid = call(
        prep_kernel,
        [
            ((edges, hot_rows), BF16),
            ((half_rows, edges), BF16),
            ((2, 2 * width, 2 * width), BF16),
            ((rows, LANES), jnp.int32),
            ((rows, width), F32),
        ],
    )(jnp.swapaxes(neighbours, 1, 2), jnp.swapaxes(valid, 1, 2), w_msg, w_out, cotangent)
    sources = (
        nodes,
        arrive_list,
        far_off,
        far_on,
        got_off,
        got_on,
        got_far_off,
        got_far_on,
        hot,
        hot_t,
        wide,
        ids,
        d_hid,
        w_send,
        w_recv,
        w_self,
        w_agg,
        w_out,
        cotangent,
    )
    updated, back_off, back_on, grads, d_node, d_centre, d_neigh = call(
        layer_kernel,
        [
            ((1, rows, width), BF16),
            ((border, width), BF16),
            ((border, width), BF16),
            ((devices * share, width), BF16),
            ((rows, width), BF16),
            ((rows, width), BF16),
            ((rows, width), BF16),
        ],
        [
            pltpu.VMEM((hot_rows, 2 * width), BF16),
            pltpu.VMEM((pair_rows, 2 * width), BF16),
            pltpu.VMEM((pair_rows, 2 * width), BF16),
            pltpu.VMEM((pair_rows, 2 * width), BF16),
            pltpu.VMEM((rows, width), F32),
            pltpu.VMEM((rows, width), F32),
            pltpu.VMEM((pair_rows, 2 * width), BF16),
            pltpu.VMEM((edges, 2 * width), BF16),
        ],
    )(*sources)
    got_on = swap(back_on, 1)
    got_off = swap(back_off, -1)
    parts = lax.all_to_all(
        grads.reshape(devices, share, width), axes, split_axis=0, concat_axis=0, tiled=True
    )
    sources = (
        cotangent,
        d_node,
        d_centre,
        d_neigh,
        w_self,
        w_send,
        w_recv,
        send_list,
        got_off,
        got_on,
    )
    (grad_nodes,) = call(
        finish_kernel,
        [((1, rows, width), BF16)],
    )(*sources)
    (shared,) = call(sum_kernel, [((devices, share, width), BF16)])(parts)
    total = lax.all_to_all(shared, axes, split_axis=0, concat_axis=0, tiled=True)
    total = total.reshape(devices * share, width)[: matrices * width]
    (weight_steps,) = call(norm_kernel, [((matrices, width, width), F32)])(total)
    return (updated, grad_nodes, weight_steps)


def solution(mesh):
    rows = P("grp", "slab", None)
    lists = P("grp", "slab")
    in_specs = (rows, lists, lists, lists, rows, rows, P(), P(), P(), P(), P(), P(), rows)
    out_specs = (rows, rows, P())
    return jax.shard_map(shards, mesh=mesh, in_specs=in_specs, out_specs=out_specs, check_vma=False)
```

```python
import functools

import jax
import jax.numpy as jnp
from jax import lax
from jax.experimental import pallas as pl
from jax.experimental.pallas import tpu as pltpu
from jax.sharding import PartitionSpec as P

F32 = jnp.float32
BF16 = jnp.bfloat16
CODE_ROWS = 16
LANES = 128
FAR = -1e30
GROUP = 32
BLOCK = 64


def nn(left, right):
    return lax.dot_general(left, right, (((1,), (0,)), ((), ())), preferred_element_type=F32)


def nt(left, right):
    return lax.dot_general(left, right, (((1,), (1,)), ((), ())), preferred_element_type=F32)


def tn(left, right):
    return lax.dot_general(left, right, (((0,), (0,)), ((), ())), preferred_element_type=F32)


def hot_columns(row, count):
    sub = lax.broadcasted_iota(jnp.int32, (count, row.shape[1]), 0)
    return jnp.where(sub == row, 1.0, 0.0).astype(BF16)


def silu_parts(half):
    tan = jnp.tanh(half)
    twice = 1.0 + tan
    act = half * twice
    return act, twice + act * (1.0 - tan)


def first_kernel(out):
    out[...] = jnp.zeros_like(out)


def parities():
    slab = lax.axis_index("slab")
    return lax.rem(slab, 2) == 1, lax.rem(slab // 2, 2) == 1


def pack_kernel(_, nodes, leave, arrive, sends, near_off, near_on, far_off, far_on):
    odd, odd_pair = parities()
    rows = nodes.shape[1]
    migr = leave.shape[1] // 2
    border = sends.shape[1] // 2
    own = nodes[0]
    leaving = tn(hot_columns(leave[...], rows), own).astype(BF16)
    sub = lax.broadcasted_iota(jnp.int32, (rows, 2 * border), 0)
    column = jnp.transpose(
        jnp.broadcast_to(arrive[...].astype(F32), (2 * border, rows)), (1, 0)
    )
    source = jnp.sum(jnp.where(sub == sends[...], column, 0.0), axis=0, keepdims=True)
    source = source.astype(jnp.int32)
    rest = tn(hot_columns(source, rows), own).astype(BF16)
    code = jnp.where(source >= rows, source - rows, -1).astype(F32)
    messages = []
    for part in range(2):
        shifted = code if part == 0 else pltpu.roll(code, border, 1)
        messages.append(
            jnp.concatenate(
                [
                    rest[part * border : (part + 1) * border],
                    leaving[part * migr : (part + 1) * migr],
                    jnp.broadcast_to(shifted, (CODE_ROWS, 2 * border)).astype(BF16),
                ],
                axis=0,
            )
        )
    down, up = messages
    near_off[...] = jnp.where(odd, up, down)
    near_on[...] = jnp.where(odd, down, up)
    down, up = leaving[:migr], leaving[migr:]
    far_off[...] = jnp.where(odd_pair, up, down)
    far_on[...] = jnp.where(odd_pair, down, up)


def prep_kernel(nbr, valid, w_msg, w_out, cotangent, hot_o, hot_t_o, up_o, wide_o, ids_o, d_hid_o):
    slots, rows = nbr.shape[1:]
    width = w_msg.shape[0]
    half_rows, hot_rows = hot_t_o.shape[0], hot_o.shape[1]
    chunk = 4
    half_msg = 0.5 * w_msg[...].astype(F32)
    none = jnp.zeros((width, width), F32)
    for part, block in enumerate((half_msg, jnp.transpose(half_msg, (1, 0)))):
        wide_o[part] = jnp.concatenate(
            [
                jnp.concatenate([block, none], axis=1),
                jnp.concatenate([none, block], axis=1),
            ],
            axis=0,
        ).astype(BF16)
    d_hid_o[...] = nt(cotangent[0], w_out[...])
    upper = nbr[0] >= half_rows
    low_row = jnp.where(upper, nbr[0] - half_rows, nbr[0])
    index = jnp.where(valid[0] == 1, low_row, half_rows) + jnp.where(upper, hot_rows, 0)
    fill = jnp.zeros((LANES - slots, rows), jnp.int32)
    ids_o[...] = jnp.transpose(jnp.concatenate([index, fill], axis=0), (1, 0))

    lane = lax.broadcasted_iota(jnp.int32, (rows, hot_rows), 1).astype(jnp.int16)
    one = jnp.ones((rows, hot_rows), BF16)
    zero = jnp.zeros((rows, hot_rows), BF16)
    sub = lax.broadcasted_iota(jnp.int32, (half_rows, rows), 0).astype(jnp.int16)
    one_t = jnp.ones((half_rows, rows), BF16)
    zero_t = jnp.zeros((half_rows, rows), BF16)

    border_id = jnp.full((rows, LANES), hot_rows, jnp.int16)

    @pl.loop(0, slots // chunk)
    def build(step):
        for j, short in enumerate(slot_ids(ids_o, step, chunk)):
            slot = step * chunk + j
            at_up = short.astype(jnp.int16) >= border_id
            up_o[pl.ds(slot * rows, rows)] = jnp.where(at_up, one[:, :LANES], zero[:, :LANES])
            short = (short & (hot_rows - 1)).astype(jnp.int16)
            short = jnp.concatenate([short] * (hot_rows // LANES), axis=1)
            hot_o[pl.ds(slot * rows, rows)] = jnp.where(short == lane, one, zero)
            row = nbr[0, pl.ds(slot, 1)]
            row = jnp.where(row >= half_rows, row - half_rows, row)
            short = jnp.broadcast_to(row, (16, rows)).astype(jnp.int16)
            short = jnp.concatenate([short] * (half_rows // 16), axis=0)
            hot_t_o[:, pl.ds(pl.multiple_of(slot * rows, LANES), rows)] = jnp.where(
                short == sub, one_t, zero_t
            )


def slot_ids(ids, step, chunk):
    near = pltpu.roll(ids[...], lax.rem(LANES - step * chunk, LANES), 1)
    shape = (ids.shape[0], LANES)
    return [jnp.broadcast_to(near[:, j : j + 1], shape) for j in range(chunk)]


def layer_kernel(
    nodes,
    arrive,
    my_far_off,
    my_far_on,
    got_off,
    got_on,
    got_far_off,
    got_far_on,
    hot,
    hot_t,
    upper,
    wide,
    nbr_ids,
    d_hid,
    w_send,
    w_recv,
    w_self,
    w_agg,
    w_out,
    cotangent,
    updated,
    back_off,
    back_on,
    grads,
    d_node_o,
    d_centre_o,
    d_neigh_o,
    neigh_s,
    hid_s,
    ds1_s,
    ds2_s,
    agg_s,
    dcen_s,
    dpre2_s,
    dpre_s,
):
    rows, width = nodes.shape[1:]
    slots = hot.shape[0] // rows
    border, migr = back_off.shape[0], got_far_off.shape[0]
    odd, odd_pair = parities()
    low = jnp.where(odd, got_on[...], got_off[...])
    high = jnp.where(odd, got_off[...], got_on[...])
    low_far = jnp.where(odd_pair, got_far_on[...], got_far_off[...])
    high_far = jnp.where(odd_pair, got_far_off[...], got_far_on[...])
    my_up = jnp.where(odd_pair, my_far_off[...], my_far_on[...])
    my_down = jnp.where(odd_pair, my_far_on[...], my_far_off[...])
    table_rows = rows + 2 * border

    pool = jnp.concatenate(
        [nodes[0], low[border : border + migr], high[border : border + migr]], axis=0
    )
    moved = tn(hot_columns(arrive[...], pool.shape[0]), pool).astype(BF16)

    def halo(message, first, second):
        code = message[border + migr : border + migr + 8].astype(F32)[:1]
        code = code.astype(jnp.int32)
        source = jnp.concatenate([first, second], axis=0)
        extra = tn(hot_columns(code, 2 * migr), source)
        return (message[:border].astype(F32) + extra[:border]).astype(BF16)

    below = halo(low, low_far, my_down)
    above = halo(high, my_up, high_far)
    table = jnp.concatenate([moved, below, above], axis=0)

    half_rows, hot_rows = hot_t.shape[0], hot.shape[1]
    half_centre = 0.5 * nn(moved, w_send[...])
    half_neigh = (0.5 * nn(table, w_recv[...]).astype(BF16).astype(F32)).astype(BF16)
    neigh_s[:half_rows] = jnp.concatenate([half_neigh[:half_rows], half_neigh[half_rows:]], axis=1)
    neigh_s[half_rows:] = jnp.full((hot_rows - half_rows, 2 * width), FAR, BF16)
    ids = slot_ids(nbr_ids, 0, slots)
    blocks = [slice(start, start + BLOCK) for start in range(0, rows, BLOCK)]
    sides = (slice(0, width), slice(width, 2 * width))

    for first in range(0, slots, GROUP):
        gathered = nn(hot[first * rows : (first + GROUP) * rows], neigh_s[...])
        for j in range(GROUP):
            pair, side = divmod(first + j, 2)
            for block in blocks:
                pick = gathered[j * rows + block.start : j * rows + block.stop]
                pick = jnp.where(
                    ids[first + j][block] >= hot_rows, pick[:, sides[1]], pick[:, sides[0]]
                )
                act, slope = silu_parts(half_centre[block] + pick)
                at = slice(pair * rows + block.start, pair * rows + block.stop)
                ds1_s[at, sides[side]] = slope
                hid_s[at, sides[side]] = act.astype(BF16)
        base = first // 2 * rows
        halves = nn(hid_s[base : base + GROUP // 2 * rows], wide[0])
        for block in blocks:
            total = jnp.zeros((BLOCK, width), F32) if first == 0 else agg_s[block]
            for j in range(GROUP):
                pair, side = divmod(j, 2)
                at = slice(pair * rows + block.start, pair * rows + block.stop)
                act, slope = silu_parts(halves[at, sides[side]])
                total = total + act
                ds2_s[base + at.start : base + at.stop, sides[side]] = slope
            agg_s[block] = total

    agg_b = agg_s[...].astype(BF16)
    node_pre = nn(moved, w_self[...]) + nn(agg_b, w_agg[...])
    act, slope = silu_parts(0.5 * node_pre)
    node_hid = act.astype(BF16)
    updated[0] = (moved.astype(F32) + nn(node_hid, w_out[...])).astype(BF16)
    cot = cotangent[0]
    d_node = (d_hid[...] * (0.5 * slope)).astype(BF16)
    half_d_agg = 0.5 * nt(d_node, w_agg[...])

    for first in range(0, slots, GROUP):
        base = first // 2 * rows
        span = slice(base, base + GROUP // 2 * rows)
        for pair in range(GROUP // 2):
            for block in blocks:
                at = slice(base + pair * rows + block.start, base + pair * rows + block.stop)
                for side in sides:
                    dpre2_s[at, side] = (half_d_agg[block] * ds2_s[at, side]).astype(BF16)
        d_hids = nn(dpre2_s[span], wide[1])
        for block in blocks:
            total = jnp.zeros((BLOCK, width), F32) if first == 0 else dcen_s[block]
            for j in range(GROUP):
                pair, side = divmod(j, 2)
                at = slice(pair * rows + block.start, pair * rows + block.stop)
                part = d_hids[at, sides[side]] * ds1_s[base + at.start : base + at.stop, sides[side]]
                total = total + part
                part = part.astype(BF16)
                at = slice((first + j) * rows + block.start, (first + j) * rows + block.stop)
                part_up = part * upper[at]
                dpre_s[at, sides[0]] = part - part_up
                dpre_s[at, sides[1]] = part_up
            dcen_s[block] = total
    gmsg = tn(hid_s[...], dpre2_s[...])
    d_neigh = nn(hot_t[...], dpre_s[...]).astype(BF16)

    d_centre = dcen_s[...].astype(BF16)
    d_neigh = jnp.concatenate([d_neigh[:, :width], d_neigh[:, width:]], axis=0)
    d_borrowed = nt(d_neigh[rows:], w_recv[...]).astype(BF16)
    back_off[...] = jnp.where(odd, d_borrowed[border:], d_borrowed[:border])
    back_on[...] = jnp.where(odd, d_borrowed[:border], d_borrowed[border:])
    d_node_o[...] = d_node
    d_centre_o[...] = d_centre
    d_neigh_o[...] = d_neigh[:rows]
    parts = (
        tn(moved, d_centre),
        tn(table, d_neigh),
        gmsg[:width, :width] + gmsg[width:, width:],
        tn(moved, d_node),
        tn(agg_b, d_node),
        tn(node_hid, cot),
    )
    for m, part in enumerate(parts):
        grads[m * width : (m + 1) * width] = part.astype(BF16)
    used = len(parts) * width
    if grads.shape[0] > used:
        grads[used:] = jnp.zeros_like(grads[used:])


def finish_kernel(
    cotangent, d_node, d_centre, d_neigh, w_self, w_send, w_recv, sends, got_off, got_on, out
):
    rows = d_node.shape[0]
    odd, _ = parities()
    from_low = jnp.where(odd, got_on[...], got_off[...])
    from_high = jnp.where(odd, got_off[...], got_on[...])
    returned = jnp.concatenate([from_low, from_high], axis=0)
    out[0] = (
        cotangent[0].astype(F32)
        + nt(d_node[...], w_self[...])
        + nt(d_centre[...], w_send[...])
        + nt(d_neigh[...], w_recv[...])
        + nn(hot_columns(sends[...], rows), returned)
    ).astype(BF16)


def sum_kernel(parts, out):
    total = jnp.sum(parts[...].astype(F32), axis=0).astype(BF16)
    out[...] = jnp.broadcast_to(total[None], out.shape)


def norm_kernel(total, steps):
    count, width = steps.shape[0], steps.shape[1]
    for m in range(count):
        part = total[m * width : (m + 1) * width].astype(F32)
        mean = jnp.sum(jnp.sum(part * part, axis=0, keepdims=True), axis=1, keepdims=True)
        mean = mean / (part.shape[0] * part.shape[1])
        steps[m] = part / jnp.sqrt(mean + 1e-06)


def call(kernel, outs, scratch=()):
    return pl.pallas_call(
        kernel,
        out_shape=[jax.ShapeDtypeStruct(shape, kind) for shape, kind in outs],
        scratch_shapes=scratch,
        compiler_params=pltpu.CompilerParams(vmem_limit_bytes=40 * 1024 * 1024),
        cost_estimate=pl.CostEstimate(flops=2 * 10**9, bytes_accessed=1024, transcendentals=0),
    )


def shards(
    nodes,
    leave_list,
    arrive_list,
    send_list,
    neighbours,
    valid,
    w_send,
    w_recv,
    w_msg,
    w_self,
    w_agg,
    w_out,
    cotangent,
):
    rows, width = nodes.shape[1:]
    slots = neighbours.shape[2]
    migr = leave_list.shape[1] // 2
    border = send_list.shape[1] // 2
    table_rows = rows + 2 * border
    size = lax.axis_size("slab")
    devices = size * lax.axis_size("grp")
    axes = ("grp", "slab")

    def swap(array, by):
        step = abs(by)
        pairs = [
            (i, (i + by if i // step % 2 == 0 else i - by) % size) for i in range(size)
        ]
        return lax.ppermute(array, "slab", pairs)

    message = (border + migr + CODE_ROWS, width)
    (token,) = call(first_kernel, [((8, LANES), F32)])()
    near_off, near_on, far_off, far_on = call(
        pack_kernel,
        [(message, BF16)] * 2 + [((migr, width), BF16)] * 2,
    )(token, nodes, leave_list, arrive_list, send_list)
    got_on = swap(near_on, 1)
    got_off = swap(near_off, -1)
    got_far_on = swap(far_on, 2)
    got_far_off = swap(far_off, -2)

    matrices = 6
    pair_rows = rows * slots // 2
    half_rows = table_rows // 2
    hot_rows = -(-(half_rows + 1) // LANES) * LANES
    share = -(-matrices * width // (8 * devices)) * 8
    edges = rows * slots
    hot, hot_t, upper, wide, ids, d_hid = call(
        prep_kernel,
        [
            ((edges, hot_rows), BF16),
            ((half_rows, edges), BF16),
            ((edges, width), BF16),
            ((2, 2 * width, 2 * width), BF16),
            ((rows, LANES), jnp.int32),
            ((rows, width), F32),
        ],
    )(jnp.swapaxes(neighbours, 1, 2), jnp.swapaxes(valid, 1, 2), w_msg, w_out, cotangent)
    sources = (
        nodes,
        arrive_list,
        far_off,
        far_on,
        got_off,
        got_on,
        got_far_off,
        got_far_on,
        hot,
        hot_t,
        upper,
        wide,
        ids,
        d_hid,
        w_send,
        w_recv,
        w_self,
        w_agg,
        w_out,
        cotangent,
    )
    updated, back_off, back_on, grads, d_node, d_centre, d_neigh = call(
        layer_kernel,
        [
            ((1, rows, width), BF16),
            ((border, width), BF16),
            ((border, width), BF16),
            ((devices * share, width), BF16),
            ((rows, width), BF16),
            ((rows, width), BF16),
            ((rows, width), BF16),
        ],
        [
            pltpu.VMEM((hot_rows, 2 * width), BF16),
            pltpu.VMEM((pair_rows, 2 * width), BF16),
            pltpu.VMEM((pair_rows, 2 * width), F32),
            pltpu.VMEM((pair_rows, 2 * width), F32),
            pltpu.VMEM((rows, width), F32),
            pltpu.VMEM((rows, width), F32),
            pltpu.VMEM((pair_rows, 2 * width), BF16),
            pltpu.VMEM((edges, 2 * width), BF16),
        ],
    )(*sources)
    got_on = swap(back_on, 1)
    got_off = swap(back_off, -1)
    parts = lax.all_to_all(
        grads.reshape(devices, share, width), axes, split_axis=0, concat_axis=0, tiled=True
    )
    sources = (
        cotangent,
        d_node,
        d_centre,
        d_neigh,
        w_self,
        w_send,
        w_recv,
        send_list,
        got_off,
        got_on,
    )
    (grad_nodes,) = call(
        finish_kernel,
        [((1, rows, width), BF16)],
    )(*sources)
    (shared,) = call(sum_kernel, [((devices, share, width), BF16)])(parts)
    total = lax.all_to_all(shared, axes, split_axis=0, concat_axis=0, tiled=True)
    total = total.reshape(devices * share, width)[: matrices * width]
    (weight_steps,) = call(norm_kernel, [((matrices, width, width), F32)])(total)
    return (updated, grad_nodes, weight_steps)


def solution(mesh):
    rows = P("grp", "slab", None)
    lists = P("grp", "slab")
    in_specs = (rows, lists, lists, lists, rows, rows, P(), P(), P(), P(), P(), P(), rows)
    out_specs = (rows, rows, P())
    return jax.shard_map(shards, mesh=mesh, in_specs=in_specs, out_specs=out_specs, check_vma=False)
```

```python
import functools

import jax
import jax.numpy as jnp
from jax import lax
from jax.experimental import pallas as pl
from jax.experimental.pallas import tpu as pltpu
from jax.sharding import PartitionSpec as P

F32 = jnp.float32
BF16 = jnp.bfloat16
CODE_ROWS = 16
LANES = 128
FAR = -1e30
GROUP = 16
BLOCK = 64


def nn(left, right):
    return lax.dot_general(left, right, (((1,), (0,)), ((), ())), preferred_element_type=F32)


def nt(left, right):
    return lax.dot_general(left, right, (((1,), (1,)), ((), ())), preferred_element_type=F32)


def tn(left, right):
    return lax.dot_general(left, right, (((0,), (0,)), ((), ())), preferred_element_type=F32)


def hot_columns(row, count):
    sub = lax.broadcasted_iota(jnp.int32, (count, row.shape[1]), 0)
    return jnp.where(sub == row, 1.0, 0.0).astype(BF16)


def silu_parts(half):
    tan = jnp.tanh(half)
    twice = 1.0 + tan
    act = half * twice
    return act, twice + act * (1.0 - tan)


def first_kernel(out):
    out[...] = jnp.zeros_like(out)


def parities():
    slab = lax.axis_index("slab")
    return lax.rem(slab, 2) == 1, lax.rem(slab // 2, 2) == 1


def pack_kernel(_, nodes, leave, arrive, sends, near_off, near_on, far_off, far_on):
    odd, odd_pair = parities()
    rows = nodes.shape[1]
    migr = leave.shape[1] // 2
    border = sends.shape[1] // 2
    own = nodes[0]
    leaving = tn(hot_columns(leave[...], rows), own).astype(BF16)
    sub = lax.broadcasted_iota(jnp.int32, (rows, 2 * border), 0)
    column = jnp.transpose(
        jnp.broadcast_to(arrive[...].astype(F32), (2 * border, rows)), (1, 0)
    )
    source = jnp.sum(jnp.where(sub == sends[...], column, 0.0), axis=0, keepdims=True)
    source = source.astype(jnp.int32)
    rest = tn(hot_columns(source, rows), own).astype(BF16)
    code = jnp.where(source >= rows, source - rows, -1).astype(F32)
    messages = []
    for part in range(2):
        shifted = code if part == 0 else pltpu.roll(code, border, 1)
        messages.append(
            jnp.concatenate(
                [
                    rest[part * border : (part + 1) * border],
                    leaving[part * migr : (part + 1) * migr],
                    jnp.broadcast_to(shifted, (CODE_ROWS, 2 * border)).astype(BF16),
                ],
                axis=0,
            )
        )
    down, up = messages
    near_off[...] = jnp.where(odd, up, down)
    near_on[...] = jnp.where(odd, down, up)
    down, up = leaving[:migr], leaving[migr:]
    far_off[...] = jnp.where(odd_pair, up, down)
    far_on[...] = jnp.where(odd_pair, down, up)


def prep_kernel(nbr, valid, w_msg, w_out, cotangent, hot_o, hot_t_o, up_o, wide_o, ids_o, d_hid_o):
    slots, rows = nbr.shape[1:]
    width = w_msg.shape[0]
    half_rows, hot_rows = hot_t_o.shape[0], hot_o.shape[1]
    chunk = 4
    half_msg = 0.5 * w_msg[...].astype(F32)
    none = jnp.zeros((width, width), F32)
    for part, block in enumerate((half_msg, jnp.transpose(half_msg, (1, 0)))):
        wide_o[part] = jnp.concatenate(
            [
                jnp.concatenate([block, none], axis=1),
                jnp.concatenate([none, block], axis=1),
            ],
            axis=0,
        ).astype(BF16)
    d_hid_o[...] = nt(cotangent[0], w_out[...])
    upper = nbr[0] >= half_rows
    low_row = jnp.where(upper, nbr[0] - half_rows, nbr[0])
    index = jnp.where(valid[0] == 1, low_row, half_rows) + jnp.where(upper, hot_rows, 0)
    fill = jnp.zeros((LANES - slots, rows), jnp.int32)
    ids_o[...] = jnp.transpose(jnp.concatenate([index, fill], axis=0), (1, 0))

    lane = lax.broadcasted_iota(jnp.int32, (rows, hot_rows), 1).astype(jnp.int16)
    one = jnp.ones((rows, hot_rows), BF16)
    zero = jnp.zeros((rows, hot_rows), BF16)
    sub = lax.broadcasted_iota(jnp.int32, (half_rows, rows), 0).astype(jnp.int16)
    one_t = jnp.ones((half_rows, rows), BF16)
    zero_t = jnp.zeros((half_rows, rows), BF16)

    border_id = jnp.full((rows, LANES), hot_rows, jnp.int16)

    @pl.loop(0, slots // chunk)
    def build(step):
        for j, short in enumerate(slot_ids(ids_o, step, chunk)):
            slot = step * chunk + j
            at_up = short.astype(jnp.int16) >= border_id
            up_o[pl.ds(slot * rows, rows)] = jnp.where(at_up, one[:, :LANES], zero[:, :LANES])
            short = (short & (hot_rows - 1)).astype(jnp.int16)
            short = jnp.concatenate([short] * (hot_rows // LANES), axis=1)
            hot_o[pl.ds(slot * rows, rows)] = jnp.where(short == lane, one, zero)
            row = nbr[0, pl.ds(slot, 1)]
            row = jnp.where(row >= half_rows, row - half_rows, row)
            short = jnp.broadcast_to(row, (16, rows)).astype(jnp.int16)
            short = jnp.concatenate([short] * (half_rows // 16), axis=0)
            hot_t_o[:, pl.ds(pl.multiple_of(slot * rows, LANES), rows)] = jnp.where(
                short == sub, one_t, zero_t
            )


def slot_ids(ids, step, chunk):
    near = pltpu.roll(ids[...], lax.rem(LANES - step * chunk, LANES), 1)
    shape = (ids.shape[0], LANES)
    return [jnp.broadcast_to(near[:, j : j + 1], shape) for j in range(chunk)]


def layer_kernel(
    nodes,
    arrive,
    my_far_off,
    my_far_on,
    got_off,
    got_on,
    got_far_off,
    got_far_on,
    hot,
    hot_t,
    upper,
    wide,
    nbr_ids,
    d_hid,
    w_send,
    w_recv,
    w_self,
    w_agg,
    w_out,
    cotangent,
    updated,
    back_off,
    back_on,
    grads,
    d_node_o,
    d_centre_o,
    d_neigh_o,
    neigh_s,
    hid_s,
    ds1_s,
    ds2_s,
    agg_s,
    dcen_s,
    dpre2_s,
    dpre_s,
):
    rows, width = nodes.shape[1:]
    slots = hot.shape[0] // rows
    border, migr = back_off.shape[0], got_far_off.shape[0]
    odd, odd_pair = parities()
    low = jnp.where(odd, got_on[...], got_off[...])
    high = jnp.where(odd, got_off[...], got_on[...])
    low_far = jnp.where(odd_pair, got_far_on[...], got_far_off[...])
    high_far = jnp.where(odd_pair, got_far_off[...], got_far_on[...])
    my_up = jnp.where(odd_pair, my_far_off[...], my_far_on[...])
    my_down = jnp.where(odd_pair, my_far_on[...], my_far_off[...])
    table_rows = rows + 2 * border

    pool = jnp.concatenate(
        [nodes[0], low[border : border + migr], high[border : border + migr]], axis=0
    )
    moved = tn(hot_columns(arrive[...], pool.shape[0]), pool).astype(BF16)

    def halo(message, first, second):
        code = message[border + migr : border + migr + 8].astype(F32)[:1]
        code = code.astype(jnp.int32)
        source = jnp.concatenate([first, second], axis=0)
        extra = tn(hot_columns(code, 2 * migr), source)
        return (message[:border].astype(F32) + extra[:border]).astype(BF16)

    below = halo(low, low_far, my_down)
    above = halo(high, my_up, high_far)
    table = jnp.concatenate([moved, below, above], axis=0)

    half_rows, hot_rows = hot_t.shape[0], hot.shape[1]
    half_centre = 0.5 * nn(moved, w_send[...])
    half_neigh = (0.5 * nn(table, w_recv[...]).astype(BF16).astype(F32)).astype(BF16)
    neigh_s[:half_rows] = jnp.concatenate([half_neigh[:half_rows], half_neigh[half_rows:]], axis=1)
    neigh_s[half_rows:] = jnp.full((hot_rows - half_rows, 2 * width), FAR, BF16)
    ids = slot_ids(nbr_ids, 0, slots)
    blocks = [slice(start, start + BLOCK) for start in range(0, rows, BLOCK)]
    sides = (slice(0, width), slice(width, 2 * width))

    firsts = range(0, slots, GROUP)
    group_rows = GROUP // 2 * rows

    def first_half(first, gathered):
        for j in range(GROUP):
            pair, side = divmod(first + j, 2)
            for block in blocks:
                pick = gathered[j * rows + block.start : j * rows + block.stop]
                pick = jnp.where(
                    ids[first + j][block] >= hot_rows, pick[:, sides[1]], pick[:, sides[0]]
                )
                act, slope = silu_parts(half_centre[block] + pick)
                at = slice(pair * rows + block.start, pair * rows + block.stop)
                ds1_s[at, sides[side]] = slope
                hid_s[at, sides[side]] = act.astype(BF16)

    def second_half(first, halves):
        base = first // 2 * rows
        for block in blocks:
            total = jnp.zeros((BLOCK, width), F32) if first == 0 else agg_s[block]
            for j in range(GROUP):
                pair, side = divmod(j, 2)
                at = slice(pair * rows + block.start, pair * rows + block.stop)
                act, slope = silu_parts(halves[at, sides[side]])
                total = total + act
                ds2_s[base + at.start : base + at.stop, sides[side]] = slope
            agg_s[block] = total

    def staggered(matmul, arithmetic):
        ready = matmul(firsts[0])
        for first, after in zip(firsts, [*firsts[1:], None]):
            held, ready = ready, None if after is None else matmul(after)
            arithmetic(first, held)

    staggered(lambda first: nn(hot[first * rows : (first + GROUP) * rows], neigh_s[...]), first_half)
    staggered(
        lambda first: nn(hid_s[first // 2 * rows : first // 2 * rows + group_rows], wide[0]),
        second_half,
    )

    agg_b = agg_s[...].astype(BF16)
    node_pre = nn(moved, w_self[...]) + nn(agg_b, w_agg[...])
    act, slope = silu_parts(0.5 * node_pre)
    node_hid = act.astype(BF16)
    updated[0] = (moved.astype(F32) + nn(node_hid, w_out[...])).astype(BF16)
    cot = cotangent[0]
    d_node = (d_hid[...] * (0.5 * slope)).astype(BF16)
    half_d_agg = 0.5 * nt(d_node, w_agg[...])

    def message_slope(first):
        base = first // 2 * rows
        for pair in range(GROUP // 2):
            for block in blocks:
                at = slice(base + pair * rows + block.start, base + pair * rows + block.stop)
                for side in sides:
                    dpre2_s[at, side] = (half_d_agg[block] * ds2_s[at, side]).astype(BF16)
        return nn(dpre2_s[base : base + group_rows], wide[1])

    def edge_slope(first, d_hids):
        base = first // 2 * rows
        for block in blocks:
            total = jnp.zeros((BLOCK, width), F32) if first == 0 else dcen_s[block]
            for j in range(GROUP):
                pair, side = divmod(j, 2)
                at = slice(pair * rows + block.start, pair * rows + block.stop)
                part = d_hids[at, sides[side]] * ds1_s[base + at.start : base + at.stop, sides[side]]
                total = total + part
                part = part.astype(BF16)
                at = slice((first + j) * rows + block.start, (first + j) * rows + block.stop)
                part_up = part * upper[at]
                dpre_s[at, sides[0]] = part - part_up
                dpre_s[at, sides[1]] = part_up
            dcen_s[block] = total

    staggered(message_slope, edge_slope)
    gmsg = tn(hid_s[...], dpre2_s[...])
    d_neigh = nn(hot_t[...], dpre_s[...]).astype(BF16)

    d_centre = dcen_s[...].astype(BF16)
    d_neigh = jnp.concatenate([d_neigh[:, :width], d_neigh[:, width:]], axis=0)
    d_borrowed = nt(d_neigh[rows:], w_recv[...]).astype(BF16)
    back_off[...] = jnp.where(odd, d_borrowed[border:], d_borrowed[:border])
    back_on[...] = jnp.where(odd, d_borrowed[:border], d_borrowed[border:])
    d_node_o[...] = d_node
    d_centre_o[...] = d_centre
    d_neigh_o[...] = d_neigh[:rows]
    parts = (
        tn(moved, d_centre),
        tn(table, d_neigh),
        gmsg[:width, :width] + gmsg[width:, width:],
        tn(moved, d_node),
        tn(agg_b, d_node),
        tn(node_hid, cot),
    )
    for m, part in enumerate(parts):
        grads[m * width : (m + 1) * width] = part.astype(BF16)
    used = len(parts) * width
    if grads.shape[0] > used:
        grads[used:] = jnp.zeros_like(grads[used:])


def finish_kernel(
    cotangent, d_node, d_centre, d_neigh, w_self, w_send, w_recv, sends, got_off, got_on, out
):
    rows = d_node.shape[0]
    odd, _ = parities()
    from_low = jnp.where(odd, got_on[...], got_off[...])
    from_high = jnp.where(odd, got_off[...], got_on[...])
    returned = jnp.concatenate([from_low, from_high], axis=0)
    out[0] = (
        cotangent[0].astype(F32)
        + nt(d_node[...], w_self[...])
        + nt(d_centre[...], w_send[...])
        + nt(d_neigh[...], w_recv[...])
        + nn(hot_columns(sends[...], rows), returned)
    ).astype(BF16)


def sum_kernel(parts, out):
    total = jnp.sum(parts[...].astype(F32), axis=0).astype(BF16)
    out[...] = jnp.broadcast_to(total[None], out.shape)


def norm_kernel(total, steps):
    count, width = steps.shape[0], steps.shape[1]
    for m in range(count):
        part = total[m * width : (m + 1) * width].astype(F32)
        mean = jnp.sum(jnp.sum(part * part, axis=0, keepdims=True), axis=1, keepdims=True)
        mean = mean / (part.shape[0] * part.shape[1])
        steps[m] = part / jnp.sqrt(mean + 1e-06)


def call(kernel, outs, scratch=()):
    return pl.pallas_call(
        kernel,
        out_shape=[jax.ShapeDtypeStruct(shape, kind) for shape, kind in outs],
        scratch_shapes=scratch,
        compiler_params=pltpu.CompilerParams(vmem_limit_bytes=40 * 1024 * 1024),
        cost_estimate=pl.CostEstimate(flops=2 * 10**9, bytes_accessed=1024, transcendentals=0),
    )


def shards(
    nodes,
    leave_list,
    arrive_list,
    send_list,
    neighbours,
    valid,
    w_send,
    w_recv,
    w_msg,
    w_self,
    w_agg,
    w_out,
    cotangent,
):
    rows, width = nodes.shape[1:]
    slots = neighbours.shape[2]
    migr = leave_list.shape[1] // 2
    border = send_list.shape[1] // 2
    table_rows = rows + 2 * border
    size = lax.axis_size("slab")
    devices = size * lax.axis_size("grp")
    axes = ("grp", "slab")

    def swap(array, by):
        step = abs(by)
        pairs = [
            (i, (i + by if i // step % 2 == 0 else i - by) % size) for i in range(size)
        ]
        return lax.ppermute(array, "slab", pairs)

    message = (border + migr + CODE_ROWS, width)
    (token,) = call(first_kernel, [((8, LANES), F32)])()
    near_off, near_on, far_off, far_on = call(
        pack_kernel,
        [(message, BF16)] * 2 + [((migr, width), BF16)] * 2,
    )(token, nodes, leave_list, arrive_list, send_list)
    got_on = swap(near_on, 1)
    got_off = swap(near_off, -1)
    got_far_on = swap(far_on, 2)
    got_far_off = swap(far_off, -2)

    matrices = 6
    pair_rows = rows * slots // 2
    half_rows = table_rows // 2
    hot_rows = -(-(half_rows + 1) // LANES) * LANES
    share = -(-matrices * width // (8 * devices)) * 8
    edges = rows * slots
    hot, hot_t, upper, wide, ids, d_hid = call(
        prep_kernel,
        [
            ((edges, hot_rows), BF16),
            ((half_rows, edges), BF16),
            ((edges, width), BF16),
            ((2, 2 * width, 2 * width), BF16),
            ((rows, LANES), jnp.int32),
            ((rows, width), F32),
        ],
    )(jnp.swapaxes(neighbours, 1, 2), jnp.swapaxes(valid, 1, 2), w_msg, w_out, cotangent)
    sources = (
        nodes,
        arrive_list,
        far_off,
        far_on,
        got_off,
        got_on,
        got_far_off,
        got_far_on,
        hot,
        hot_t,
        upper,
        wide,
        ids,
        d_hid,
        w_send,
        w_recv,
        w_self,
        w_agg,
        w_out,
        cotangent,
    )
    updated, back_off, back_on, grads, d_node, d_centre, d_neigh = call(
        layer_kernel,
        [
            ((1, rows, width), BF16),
            ((border, width), BF16),
            ((border, width), BF16),
            ((devices * share, width), BF16),
            ((rows, width), BF16),
            ((rows, width), BF16),
            ((rows, width), BF16),
        ],
        [
            pltpu.VMEM((hot_rows, 2 * width), BF16),
            pltpu.VMEM((pair_rows, 2 * width), BF16),
            pltpu.VMEM((pair_rows, 2 * width), F32),
            pltpu.VMEM((pair_rows, 2 * width), F32),
            pltpu.VMEM((rows, width), F32),
            pltpu.VMEM((rows, width), F32),
            pltpu.VMEM((pair_rows, 2 * width), BF16),
            pltpu.VMEM((edges, 2 * width), BF16),
        ],
    )(*sources)
    got_on = swap(back_on, 1)
    got_off = swap(back_off, -1)
    parts = lax.all_to_all(
        grads.reshape(devices, share, width), axes, split_axis=0, concat_axis=0, tiled=True
    )
    sources = (
        cotangent,
        d_node,
        d_centre,
        d_neigh,
        w_self,
        w_send,
        w_recv,
        send_list,
        got_off,
        got_on,
    )
    (grad_nodes,) = call(
        finish_kernel,
        [((1, rows, width), BF16)],
    )(*sources)
    (shared,) = call(sum_kernel, [((devices, share, width), BF16)])(parts)
    total = lax.all_to_all(shared, axes, split_axis=0, concat_axis=0, tiled=True)
    total = total.reshape(devices * share, width)[: matrices * width]
    (weight_steps,) = call(norm_kernel, [((matrices, width, width), F32)])(total)
    return (updated, grad_nodes, weight_steps)


def solution(mesh):
    rows = P("grp", "slab", None)
    lists = P("grp", "slab")
    in_specs = (rows, lists, lists, lists, rows, rows, P(), P(), P(), P(), P(), P(), rows)
    out_specs = (rows, rows, P())
    return jax.shard_map(shards, mesh=mesh, in_specs=in_specs, out_specs=out_specs, check_vma=False)
```

```python
import functools

import jax
import jax.numpy as jnp
from jax import lax
from jax.experimental import pallas as pl
from jax.experimental.pallas import tpu as pltpu
from jax.sharding import PartitionSpec as P

F32 = jnp.float32
BF16 = jnp.bfloat16
CODE_ROWS = 16
LANES = 128
FAR = -1e30
GROUP = 8
BLOCK = 64


def nn(left, right):
    return lax.dot_general(left, right, (((1,), (0,)), ((), ())), preferred_element_type=F32)


def nt(left, right):
    return lax.dot_general(left, right, (((1,), (1,)), ((), ())), preferred_element_type=F32)


def tn(left, right):
    return lax.dot_general(left, right, (((0,), (0,)), ((), ())), preferred_element_type=F32)


def hot_columns(row, count):
    sub = lax.broadcasted_iota(jnp.int32, (count, row.shape[1]), 0)
    return jnp.where(sub == row, 1.0, 0.0).astype(BF16)


def silu_parts(half):
    tan = jnp.tanh(half)
    twice = 1.0 + tan
    act = half * twice
    return act, twice + act * (1.0 - tan)


def first_kernel(out):
    out[...] = jnp.zeros_like(out)


def parities():
    slab = lax.axis_index("slab")
    return lax.rem(slab, 2) == 1, lax.rem(slab // 2, 2) == 1


def pack_kernel(_, nodes, leave, arrive, sends, near_off, near_on, far_off, far_on):
    odd, odd_pair = parities()
    rows = nodes.shape[1]
    migr = leave.shape[1] // 2
    border = sends.shape[1] // 2
    own = nodes[0]
    leaving = tn(hot_columns(leave[...], rows), own).astype(BF16)
    sub = lax.broadcasted_iota(jnp.int32, (rows, 2 * border), 0)
    column = jnp.transpose(
        jnp.broadcast_to(arrive[...].astype(F32), (2 * border, rows)), (1, 0)
    )
    source = jnp.sum(jnp.where(sub == sends[...], column, 0.0), axis=0, keepdims=True)
    source = source.astype(jnp.int32)
    rest = tn(hot_columns(source, rows), own).astype(BF16)
    code = jnp.where(source >= rows, source - rows, -1).astype(F32)
    messages = []
    for part in range(2):
        shifted = code if part == 0 else pltpu.roll(code, border, 1)
        messages.append(
            jnp.concatenate(
                [
                    rest[part * border : (part + 1) * border],
                    leaving[part * migr : (part + 1) * migr],
                    jnp.broadcast_to(shifted, (CODE_ROWS, 2 * border)).astype(BF16),
                ],
                axis=0,
            )
        )
    down, up = messages
    near_off[...] = jnp.where(odd, up, down)
    near_on[...] = jnp.where(odd, down, up)
    down, up = leaving[:migr], leaving[migr:]
    far_off[...] = jnp.where(odd_pair, up, down)
    far_on[...] = jnp.where(odd_pair, down, up)


def prep_kernel(nbr, valid, w_msg, w_out, cotangent, hot_o, hot_t_o, up_o, wide_o, ids_o, d_hid_o):
    slots, rows = nbr.shape[1:]
    width = w_msg.shape[0]
    half_rows, hot_rows = hot_t_o.shape[0], hot_o.shape[1]
    chunk = 4
    half_msg = 0.5 * w_msg[...].astype(F32)
    none = jnp.zeros((width, width), F32)
    for part, block in enumerate((half_msg, jnp.transpose(half_msg, (1, 0)))):
        wide_o[part] = jnp.concatenate(
            [
                jnp.concatenate([block, none], axis=1),
                jnp.concatenate([none, block], axis=1),
            ],
            axis=0,
        ).astype(BF16)
    d_hid_o[...] = nt(cotangent[0], w_out[...])
    upper = nbr[0] >= half_rows
    low_row = jnp.where(upper, nbr[0] - half_rows, nbr[0])
    index = jnp.where(valid[0] == 1, low_row, half_rows) + jnp.where(upper, hot_rows, 0)
    fill = jnp.zeros((LANES - slots, rows), jnp.int32)
    ids_o[...] = jnp.transpose(jnp.concatenate([index, fill], axis=0), (1, 0))

    lane = lax.broadcasted_iota(jnp.int32, (rows, hot_rows), 1).astype(jnp.int16)
    one = jnp.ones((rows, hot_rows), BF16)
    zero = jnp.zeros((rows, hot_rows), BF16)
    sub = lax.broadcasted_iota(jnp.int32, (half_rows, rows), 0).astype(jnp.int16)
    one_t = jnp.ones((half_rows, rows), BF16)
    zero_t = jnp.zeros((half_rows, rows), BF16)

    border_id = jnp.full((rows, LANES), hot_rows, jnp.int16)

    @pl.loop(0, slots // chunk)
    def build(step):
        for j, short in enumerate(slot_ids(ids_o, step, chunk)):
            slot = step * chunk + j
            at_up = short.astype(jnp.int16) >= border_id
            up_o[pl.ds(slot * rows, rows)] = jnp.where(at_up, one[:, :LANES], zero[:, :LANES])
            short = (short & (hot_rows - 1)).astype(jnp.int16)
            short = jnp.concatenate([short] * (hot_rows // LANES), axis=1)
            hot_o[pl.ds(slot * rows, rows)] = jnp.where(short == lane, one, zero)
            row = nbr[0, pl.ds(slot, 1)]
            row = jnp.where(row >= half_rows, row - half_rows, row)
            short = jnp.broadcast_to(row, (16, rows)).astype(jnp.int16)
            short = jnp.concatenate([short] * (half_rows // 16), axis=0)
            hot_t_o[:, pl.ds(pl.multiple_of(slot * rows, LANES), rows)] = jnp.where(
                short == sub, one_t, zero_t
            )


def slot_ids(ids, step, chunk):
    near = pltpu.roll(ids[...], lax.rem(LANES - step * chunk, LANES), 1)
    shape = (ids.shape[0], LANES)
    return [jnp.broadcast_to(near[:, j : j + 1], shape) for j in range(chunk)]


def layer_kernel(
    nodes,
    arrive,
    my_far_off,
    my_far_on,
    got_off,
    got_on,
    got_far_off,
    got_far_on,
    hot,
    hot_t,
    upper,
    wide,
    nbr_ids,
    d_hid,
    w_send,
    w_recv,
    w_self,
    w_agg,
    w_out,
    cotangent,
    updated,
    back_off,
    back_on,
    grads,
    d_node_o,
    d_centre_o,
    d_neigh_o,
    neigh_s,
    hid_s,
    ds1_s,
    ds2_s,
    agg_s,
    dcen_s,
    dpre2_s,
    dpre_s,
):
    rows, width = nodes.shape[1:]
    slots = hot.shape[0] // rows
    border, migr = back_off.shape[0], got_far_off.shape[0]
    odd, odd_pair = parities()
    low = jnp.where(odd, got_on[...], got_off[...])
    high = jnp.where(odd, got_off[...], got_on[...])
    low_far = jnp.where(odd_pair, got_far_on[...], got_far_off[...])
    high_far = jnp.where(odd_pair, got_far_off[...], got_far_on[...])
    my_up = jnp.where(odd_pair, my_far_off[...], my_far_on[...])
    my_down = jnp.where(odd_pair, my_far_on[...], my_far_off[...])
    table_rows = rows + 2 * border

    pool = jnp.concatenate(
        [nodes[0], low[border : border + migr], high[border : border + migr]], axis=0
    )
    moved = tn(hot_columns(arrive[...], pool.shape[0]), pool).astype(BF16)

    def halo(message, first, second):
        code = message[border + migr : border + migr + 8].astype(F32)[:1]
        code = code.astype(jnp.int32)
        source = jnp.concatenate([first, second], axis=0)
        extra = tn(hot_columns(code, 2 * migr), source)
        return (message[:border].astype(F32) + extra[:border]).astype(BF16)

    below = halo(low, low_far, my_down)
    above = halo(high, my_up, high_far)
    table = jnp.concatenate([moved, below, above], axis=0)

    half_rows, hot_rows = hot_t.shape[0], hot.shape[1]
    half_centre = 0.5 * nn(moved, w_send[...])
    half_neigh = (0.5 * nn(table, w_recv[...]).astype(BF16).astype(F32)).astype(BF16)
    neigh_s[:half_rows] = jnp.concatenate([half_neigh[:half_rows], half_neigh[half_rows:]], axis=1)
    neigh_s[half_rows:] = jnp.full((hot_rows - half_rows, 2 * width), FAR, BF16)
    ids = slot_ids(nbr_ids, 0, slots)
    blocks = [slice(start, start + BLOCK) for start in range(0, rows, BLOCK)]
    sides = (slice(0, width), slice(width, 2 * width))

    firsts = range(0, slots, GROUP)
    group_rows = GROUP // 2 * rows

    def first_half(first, gathered):
        for j in range(GROUP):
            pair, side = divmod(first + j, 2)
            for block in blocks:
                pick = gathered[j * rows + block.start : j * rows + block.stop]
                pick = jnp.where(
                    ids[first + j][block] >= hot_rows, pick[:, sides[1]], pick[:, sides[0]]
                )
                act, slope = silu_parts(half_centre[block] + pick)
                at = slice(pair * rows + block.start, pair * rows + block.stop)
                ds1_s[at, sides[side]] = slope
                hid_s[at, sides[side]] = act.astype(BF16)

    def second_half(first, halves):
        base = first // 2 * rows
        for block in blocks:
            total = jnp.zeros((BLOCK, width), F32) if first == 0 else agg_s[block]
            for j in range(GROUP):
                pair, side = divmod(j, 2)
                at = slice(pair * rows + block.start, pair * rows + block.stop)
                act, slope = silu_parts(halves[at, sides[side]])
                total = total + act
                ds2_s[base + at.start : base + at.stop, sides[side]] = slope
            agg_s[block] = total

    def gather(first):
        return nn(hot[first * rows : (first + GROUP) * rows], neigh_s[...])

    ready, message = gather(0), None
    for first in firsts:
        held, ready = ready, None if first + GROUP == slots else gather(first + GROUP)
        first_half(first, held)
        base = first // 2 * rows
        held, message = message, nn(hid_s[base : base + group_rows], wide[0])
        if first > 0:
            second_half(first - GROUP, held)
    second_half(slots - GROUP, message)

    agg_b = agg_s[...].astype(BF16)
    node_pre = nn(moved, w_self[...]) + nn(agg_b, w_agg[...])
    act, slope = silu_parts(0.5 * node_pre)
    node_hid = act.astype(BF16)
    updated[0] = (moved.astype(F32) + nn(node_hid, w_out[...])).astype(BF16)
    cot = cotangent[0]
    d_node = (d_hid[...] * (0.5 * slope)).astype(BF16)
    half_d_agg = 0.5 * nt(d_node, w_agg[...])

    def message_slope(first):
        base = first // 2 * rows
        for pair in range(GROUP // 2):
            for block in blocks:
                at = slice(base + pair * rows + block.start, base + pair * rows + block.stop)
                for side in sides:
                    dpre2_s[at, side] = (half_d_agg[block] * ds2_s[at, side]).astype(BF16)
        return nn(dpre2_s[base : base + group_rows], wide[1])

    def edge_slope(first, d_hids):
        base = first // 2 * rows
        for block in blocks:
            total = jnp.zeros((BLOCK, width), F32) if first == 0 else dcen_s[block]
            for j in range(GROUP):
                pair, side = divmod(j, 2)
                at = slice(pair * rows + block.start, pair * rows + block.stop)
                part = d_hids[at, sides[side]] * ds1_s[base + at.start : base + at.stop, sides[side]]
                total = total + part
                part = part.astype(BF16)
                at = slice((first + j) * rows + block.start, (first + j) * rows + block.stop)
                part_up = part * upper[at]
                dpre_s[at, sides[0]] = part - part_up
                dpre_s[at, sides[1]] = part_up
            dcen_s[block] = total

    def message_gradient(first, last):
        pairs = slice(first // 2 * rows, last // 2 * rows)
        return tn(hid_s[pairs], dpre2_s[pairs])

    def scatter(first, last):
        at = slice(first * rows, last * rows)
        return nn(hot_t[:, at], dpre_s[at])

    middle = slots // (2 * GROUP) * GROUP
    ready = message_slope(0)
    for first in firsts:
        after = first + GROUP
        held, ready = ready, None if after == slots else message_slope(after)
        if after == middle:
            gmsg = message_gradient(0, middle)
        elif after == slots:
            gmsg = gmsg + message_gradient(middle, slots)
        edge_slope(first, held)
        if after == middle:
            scattered = scatter(0, middle)
    d_neigh = (scattered + scatter(middle, slots)).astype(BF16)

    d_centre = dcen_s[...].astype(BF16)
    d_neigh = jnp.concatenate([d_neigh[:, :width], d_neigh[:, width:]], axis=0)
    d_borrowed = nt(d_neigh[rows:], w_recv[...]).astype(BF16)
    back_off[...] = jnp.where(odd, d_borrowed[border:], d_borrowed[:border])
    back_on[...] = jnp.where(odd, d_borrowed[:border], d_borrowed[border:])
    d_node_o[...] = d_node
    d_centre_o[...] = d_centre
    d_neigh_o[...] = d_neigh[:rows]
    parts = (
        tn(moved, d_centre),
        tn(table, d_neigh),
        gmsg[:width, :width] + gmsg[width:, width:],
        tn(moved, d_node),
        tn(agg_b, d_node),
        tn(node_hid, cot),
    )
    for m, part in enumerate(parts):
        grads[m * width : (m + 1) * width] = part.astype(BF16)
    used = len(parts) * width
    if grads.shape[0] > used:
        grads[used:] = jnp.zeros_like(grads[used:])


def finish_kernel(
    cotangent, d_node, d_centre, d_neigh, w_self, w_send, w_recv, sends, got_off, got_on, out
):
    rows = d_node.shape[0]
    odd, _ = parities()
    from_low = jnp.where(odd, got_on[...], got_off[...])
    from_high = jnp.where(odd, got_off[...], got_on[...])
    returned = jnp.concatenate([from_low, from_high], axis=0)
    out[0] = (
        cotangent[0].astype(F32)
        + nt(d_node[...], w_self[...])
        + nt(d_centre[...], w_send[...])
        + nt(d_neigh[...], w_recv[...])
        + nn(hot_columns(sends[...], rows), returned)
    ).astype(BF16)


def sum_kernel(parts, out):
    total = jnp.sum(parts[...].astype(F32), axis=0).astype(BF16)
    out[...] = jnp.broadcast_to(total[None], out.shape)


def norm_kernel(total, steps):
    count, width = steps.shape[0], steps.shape[1]
    for m in range(count):
        part = total[m * width : (m + 1) * width].astype(F32)
        mean = jnp.sum(jnp.sum(part * part, axis=0, keepdims=True), axis=1, keepdims=True)
        mean = mean / (part.shape[0] * part.shape[1])
        steps[m] = part / jnp.sqrt(mean + 1e-06)


def call(kernel, outs, scratch=()):
    return pl.pallas_call(
        kernel,
        out_shape=[jax.ShapeDtypeStruct(shape, kind) for shape, kind in outs],
        scratch_shapes=scratch,
        compiler_params=pltpu.CompilerParams(vmem_limit_bytes=40 * 1024 * 1024),
        cost_estimate=pl.CostEstimate(flops=2 * 10**9, bytes_accessed=1024, transcendentals=0),
    )


def shards(
    nodes,
    leave_list,
    arrive_list,
    send_list,
    neighbours,
    valid,
    w_send,
    w_recv,
    w_msg,
    w_self,
    w_agg,
    w_out,
    cotangent,
):
    rows, width = nodes.shape[1:]
    slots = neighbours.shape[2]
    migr = leave_list.shape[1] // 2
    border = send_list.shape[1] // 2
    table_rows = rows + 2 * border
    size = lax.axis_size("slab")
    devices = size * lax.axis_size("grp")
    axes = ("grp", "slab")

    def swap(array, by):
        step = abs(by)
        pairs = [
            (i, (i + by if i // step % 2 == 0 else i - by) % size) for i in range(size)
        ]
        return lax.ppermute(array, "slab", pairs)

    message = (border + migr + CODE_ROWS, width)
    (token,) = call(first_kernel, [((8, LANES), F32)])()
    near_off, near_on, far_off, far_on = call(
        pack_kernel,
        [(message, BF16)] * 2 + [((migr, width), BF16)] * 2,
    )(token, nodes, leave_list, arrive_list, send_list)
    got_on = swap(near_on, 1)
    got_off = swap(near_off, -1)
    got_far_on = swap(far_on, 2)
    got_far_off = swap(far_off, -2)

    matrices = 6
    pair_rows = rows * slots // 2
    half_rows = table_rows // 2
    hot_rows = -(-(half_rows + 1) // LANES) * LANES
    share = -(-matrices * width // (8 * devices)) * 8
    edges = rows * slots
    hot, hot_t, upper, wide, ids, d_hid = call(
        prep_kernel,
        [
            ((edges, hot_rows), BF16),
            ((half_rows, edges), BF16),
            ((edges, width), BF16),
            ((2, 2 * width, 2 * width), BF16),
            ((rows, LANES), jnp.int32),
            ((rows, width), F32),
        ],
    )(jnp.swapaxes(neighbours, 1, 2), jnp.swapaxes(valid, 1, 2), w_msg, w_out, cotangent)
    sources = (
        nodes,
        arrive_list,
        far_off,
        far_on,
        got_off,
        got_on,
        got_far_off,
        got_far_on,
        hot,
        hot_t,
        upper,
        wide,
        ids,
        d_hid,
        w_send,
        w_recv,
        w_self,
        w_agg,
        w_out,
        cotangent,
    )
    updated, back_off, back_on, grads, d_node, d_centre, d_neigh = call(
        layer_kernel,
        [
            ((1, rows, width), BF16),
            ((border, width), BF16),
            ((border, width), BF16),
            ((devices * share, width), BF16),
            ((rows, width), BF16),
            ((rows, width), BF16),
            ((rows, width), BF16),
        ],
        [
            pltpu.VMEM((hot_rows, 2 * width), BF16),
            pltpu.VMEM((pair_rows, 2 * width), BF16),
            pltpu.VMEM((pair_rows, 2 * width), F32),
            pltpu.VMEM((pair_rows, 2 * width), F32),
            pltpu.VMEM((rows, width), F32),
            pltpu.VMEM((rows, width), F32),
            pltpu.VMEM((pair_rows, 2 * width), BF16),
            pltpu.VMEM((edges, 2 * width), BF16),
        ],
    )(*sources)
    got_on = swap(back_on, 1)
    got_off = swap(back_off, -1)
    parts = lax.all_to_all(
        grads.reshape(devices, share, width), axes, split_axis=0, concat_axis=0, tiled=True
    )
    sources = (
        cotangent,
        d_node,
        d_centre,
        d_neigh,
        w_self,
        w_send,
        w_recv,
        send_list,
        got_off,
        got_on,
    )
    (grad_nodes,) = call(
        finish_kernel,
        [((1, rows, width), BF16)],
    )(*sources)
    (shared,) = call(sum_kernel, [((devices, share, width), BF16)])(parts)
    total = lax.all_to_all(shared, axes, split_axis=0, concat_axis=0, tiled=True)
    total = total.reshape(devices * share, width)[: matrices * width]
    (weight_steps,) = call(norm_kernel, [((matrices, width, width), F32)])(total)
    return (updated, grad_nodes, weight_steps)


def solution(mesh):
    rows = P("grp", "slab", None)
    lists = P("grp", "slab")
    in_specs = (rows, lists, lists, lists, rows, rows, P(), P(), P(), P(), P(), P(), rows)
    out_specs = (rows, rows, P())
    return jax.shard_map(shards, mesh=mesh, in_specs=in_specs, out_specs=out_specs, check_vma=False)
```

```python
import functools

import jax
import jax.numpy as jnp
from jax import lax
from jax.experimental import pallas as pl
from jax.experimental.pallas import tpu as pltpu
from jax.sharding import PartitionSpec as P

F32 = jnp.float32
BF16 = jnp.bfloat16
CODE_ROWS = 16
LANES = 128
FAR = -1e30
GROUP = 16
BLOCK = 64


def nn(left, right):
    return lax.dot_general(left, right, (((1,), (0,)), ((), ())), preferred_element_type=F32)


def nt(left, right):
    return lax.dot_general(left, right, (((1,), (1,)), ((), ())), preferred_element_type=F32)


def tn(left, right):
    return lax.dot_general(left, right, (((0,), (0,)), ((), ())), preferred_element_type=F32)


def hot_columns(row, count):
    sub = lax.broadcasted_iota(jnp.int32, (count, row.shape[1]), 0)
    return jnp.where(sub == row, 1.0, 0.0).astype(BF16)


def silu_parts(half):
    tan = jnp.tanh(half)
    twice = 1.0 + tan
    act = half * twice
    return act, twice + act * (1.0 - tan)


def first_kernel(out):
    out[...] = jnp.zeros_like(out)


def parities():
    slab = lax.axis_index("slab")
    return lax.rem(slab, 2) == 1, lax.rem(slab // 2, 2) == 1


def pack_kernel(_, nodes, leave, arrive, sends, near_off, near_on, far_off, far_on):
    odd, odd_pair = parities()
    rows = nodes.shape[1]
    migr = leave.shape[1] // 2
    border = sends.shape[1] // 2
    own = nodes[0]
    leaving = tn(hot_columns(leave[...], rows), own).astype(BF16)
    sub = lax.broadcasted_iota(jnp.int32, (rows, 2 * border), 0)
    column = jnp.transpose(
        jnp.broadcast_to(arrive[...].astype(F32), (2 * border, rows)), (1, 0)
    )
    source = jnp.sum(jnp.where(sub == sends[...], column, 0.0), axis=0, keepdims=True)
    source = source.astype(jnp.int32)
    rest = tn(hot_columns(source, rows), own).astype(BF16)
    code = jnp.where(source >= rows, source - rows, -1).astype(F32)
    messages = []
    for part in range(2):
        shifted = code if part == 0 else pltpu.roll(code, border, 1)
        messages.append(
            jnp.concatenate(
                [
                    rest[part * border : (part + 1) * border],
                    leaving[part * migr : (part + 1) * migr],
                    jnp.broadcast_to(shifted, (CODE_ROWS, 2 * border)).astype(BF16),
                ],
                axis=0,
            )
        )
    down, up = messages
    near_off[...] = jnp.where(odd, up, down)
    near_on[...] = jnp.where(odd, down, up)
    down, up = leaving[:migr], leaving[migr:]
    far_off[...] = jnp.where(odd_pair, up, down)
    far_on[...] = jnp.where(odd_pair, down, up)


def prep_kernel(nbr, valid, w_msg, w_out, cotangent, hot_o, hot_t_o, up_o, wide_o, ids_o, d_hid_o):
    slots, rows = nbr.shape[1:]
    width = w_msg.shape[0]
    half_rows, hot_rows = hot_t_o.shape[0], hot_o.shape[1]
    chunk = 4
    half_msg = 0.5 * w_msg[...].astype(F32)
    none = jnp.zeros((width, width), F32)
    for part, block in enumerate((half_msg, jnp.transpose(half_msg, (1, 0)))):
        wide_o[part] = jnp.concatenate(
            [
                jnp.concatenate([block, none], axis=1),
                jnp.concatenate([none, block], axis=1),
            ],
            axis=0,
        ).astype(BF16)
    d_hid_o[...] = nt(cotangent[0], w_out[...])
    upper = nbr[0] >= half_rows
    low_row = jnp.where(upper, nbr[0] - half_rows, nbr[0])
    index = jnp.where(valid[0] == 1, low_row, half_rows) + jnp.where(upper, hot_rows, 0)
    fill = jnp.zeros((LANES - slots, rows), jnp.int32)
    ids_o[...] = jnp.transpose(jnp.concatenate([index, fill], axis=0), (1, 0))

    lane = lax.broadcasted_iota(jnp.int32, (rows, hot_rows), 1).astype(jnp.int16)
    one = jnp.ones((rows, hot_rows), BF16)
    zero = jnp.zeros((rows, hot_rows), BF16)
    sub = lax.broadcasted_iota(jnp.int32, (half_rows, rows), 0).astype(jnp.int16)
    one_t = jnp.ones((half_rows, rows), BF16)
    zero_t = jnp.zeros((half_rows, rows), BF16)

    border_id = jnp.full((rows, LANES), hot_rows, jnp.int16)

    @pl.loop(0, slots // chunk)
    def build(step):
        for j, short in enumerate(slot_ids(ids_o, step, chunk)):
            slot = step * chunk + j
            at_up = short.astype(jnp.int16) >= border_id
            up_o[pl.ds(slot * rows, rows)] = jnp.where(at_up, one[:, :LANES], zero[:, :LANES])
            short = (short & (hot_rows - 1)).astype(jnp.int16)
            short = jnp.concatenate([short] * (hot_rows // LANES), axis=1)
            hot_o[pl.ds(slot * rows, rows)] = jnp.where(short == lane, one, zero)
            row = nbr[0, pl.ds(slot, 1)]
            row = jnp.where(row >= half_rows, row - half_rows, row)
            short = jnp.broadcast_to(row, (16, rows)).astype(jnp.int16)
            short = jnp.concatenate([short] * (half_rows // 16), axis=0)
            hot_t_o[:, pl.ds(pl.multiple_of(slot * rows, LANES), rows)] = jnp.where(
                short == sub, one_t, zero_t
            )


def slot_ids(ids, step, chunk):
    near = pltpu.roll(ids[...], lax.rem(LANES - step * chunk, LANES), 1)
    shape = (ids.shape[0], LANES)
    return [jnp.broadcast_to(near[:, j : j + 1], shape) for j in range(chunk)]


def layer_kernel(
    nodes,
    arrive,
    my_far_off,
    my_far_on,
    got_off,
    got_on,
    got_far_off,
    got_far_on,
    hot,
    hot_t,
    upper,
    wide,
    nbr_ids,
    d_hid,
    w_send,
    w_recv,
    w_self,
    w_agg,
    w_out,
    cotangent,
    updated,
    back_off,
    back_on,
    grads,
    d_node_o,
    d_centre_o,
    d_neigh_o,
    neigh_s,
    hid_s,
    ds1_s,
    ds2_s,
    agg_s,
    dcen_s,
    dpre2_s,
    dpre_s,
):
    rows, width = nodes.shape[1:]
    slots = hot.shape[0] // rows
    border, migr = back_off.shape[0], got_far_off.shape[0]
    odd, odd_pair = parities()
    low = jnp.where(odd, got_on[...], got_off[...])
    high = jnp.where(odd, got_off[...], got_on[...])
    low_far = jnp.where(odd_pair, got_far_on[...], got_far_off[...])
    high_far = jnp.where(odd_pair, got_far_off[...], got_far_on[...])
    my_up = jnp.where(odd_pair, my_far_off[...], my_far_on[...])
    my_down = jnp.where(odd_pair, my_far_on[...], my_far_off[...])
    table_rows = rows + 2 * border

    pool = jnp.concatenate(
        [nodes[0], low[border : border + migr], high[border : border + migr]], axis=0
    )
    moved = tn(hot_columns(arrive[...], pool.shape[0]), pool).astype(BF16)

    def halo(message, first, second):
        code = message[border + migr : border + migr + 8].astype(F32)[:1]
        code = code.astype(jnp.int32)
        source = jnp.concatenate([first, second], axis=0)
        extra = tn(hot_columns(code, 2 * migr), source)
        return (message[:border].astype(F32) + extra[:border]).astype(BF16)

    below = halo(low, low_far, my_down)
    above = halo(high, my_up, high_far)
    table = jnp.concatenate([moved, below, above], axis=0)

    half_rows, hot_rows = hot_t.shape[0], hot.shape[1]
    half_centre = 0.5 * nn(moved, w_send[...])
    half_neigh = (0.5 * nn(table, w_recv[...]).astype(BF16).astype(F32)).astype(BF16)
    neigh_s[:half_rows] = jnp.concatenate([half_neigh[:half_rows], half_neigh[half_rows:]], axis=1)
    neigh_s[half_rows:] = jnp.full((hot_rows - half_rows, 2 * width), FAR, BF16)
    ids = slot_ids(nbr_ids, 0, slots)
    blocks = [slice(start, start + BLOCK) for start in range(0, rows, BLOCK)]
    sides = (slice(0, width), slice(width, 2 * width))

    firsts = range(0, slots, GROUP)
    group_rows = GROUP // 2 * rows

    def first_half(first, gathered):
        for j in range(GROUP):
            pair, side = divmod(first + j, 2)
            for block in blocks:
                pick = gathered[j * rows + block.start : j * rows + block.stop]
                pick = jnp.where(
                    ids[first + j][block] >= hot_rows, pick[:, sides[1]], pick[:, sides[0]]
                )
                act, slope = silu_parts(half_centre[block] + pick)
                at = slice(pair * rows + block.start, pair * rows + block.stop)
                ds1_s[at, sides[side]] = slope
                hid_s[at, sides[side]] = act.astype(BF16)

    def second_half(first, halves):
        base = first // 2 * rows
        for block in blocks:
            total = jnp.zeros((BLOCK, width), F32) if first == 0 else agg_s[block]
            for j in range(GROUP):
                pair, side = divmod(j, 2)
                at = slice(pair * rows + block.start, pair * rows + block.stop)
                act, slope = silu_parts(halves[at, sides[side]])
                total = total + act
                ds2_s[base + at.start : base + at.stop, sides[side]] = slope
            agg_s[block] = total

    def gather(first):
        return nn(hot[first * rows : (first + GROUP) * rows], neigh_s[...])

    ready, message = gather(0), None
    for first in firsts:
        held, ready = ready, None if first + GROUP == slots else gather(first + GROUP)
        first_half(first, held)
        base = first // 2 * rows
        held, message = message, nn(hid_s[base : base + group_rows], wide[0])
        if first > 0:
            second_half(first - GROUP, held)
    second_half(slots - GROUP, message)

    agg_b = agg_s[...].astype(BF16)
    node_pre = nn(moved, w_self[...]) + nn(agg_b, w_agg[...])
    act, slope = silu_parts(0.5 * node_pre)
    node_hid = act.astype(BF16)
    updated[0] = (moved.astype(F32) + nn(node_hid, w_out[...])).astype(BF16)
    cot = cotangent[0]
    d_node = (d_hid[...] * (0.5 * slope)).astype(BF16)
    half_d_agg = 0.5 * nt(d_node, w_agg[...])

    def message_slope(first):
        base = first // 2 * rows
        for pair in range(GROUP // 2):
            for block in blocks:
                at = slice(base + pair * rows + block.start, base + pair * rows + block.stop)
                for side in sides:
                    dpre2_s[at, side] = (half_d_agg[block] * ds2_s[at, side]).astype(BF16)
        return nn(dpre2_s[base : base + group_rows], wide[1])

    def edge_slope(first, d_hids):
        base = first // 2 * rows
        for block in blocks:
            total = jnp.zeros((BLOCK, width), F32) if first == 0 else dcen_s[block]
            for j in range(GROUP):
                pair, side = divmod(j, 2)
                at = slice(pair * rows + block.start, pair * rows + block.stop)
                part = d_hids[at, sides[side]] * ds1_s[base + at.start : base + at.stop, sides[side]]
                total = total + part
                part = part.astype(BF16)
                at = slice((first + j) * rows + block.start, (first + j) * rows + block.stop)
                part_up = part * upper[at]
                dpre_s[at, sides[0]] = part - part_up
                dpre_s[at, sides[1]] = part_up
            dcen_s[block] = total

    def message_gradient(first, last):
        pairs = slice(first // 2 * rows, last // 2 * rows)
        return tn(hid_s[pairs], dpre2_s[pairs])

    def scatter(first, last):
        at = slice(first * rows, last * rows)
        return nn(hot_t[:, at], dpre_s[at])

    middle = slots // (2 * GROUP) * GROUP
    ready = message_slope(0)
    for first in firsts:
        after = first + GROUP
        held, ready = ready, None if after == slots else message_slope(after)
        if after == middle:
            gmsg = message_gradient(0, middle)
        elif after == slots:
            gmsg = gmsg + message_gradient(middle, slots)
        edge_slope(first, held)
        if after == middle:
            scattered = scatter(0, middle)
    d_neigh = (scattered + scatter(middle, slots)).astype(BF16)

    d_centre = dcen_s[...].astype(BF16)
    d_neigh = jnp.concatenate([d_neigh[:, :width], d_neigh[:, width:]], axis=0)
    d_borrowed = nt(d_neigh[rows:], w_recv[...]).astype(BF16)
    back_off[...] = jnp.where(odd, d_borrowed[border:], d_borrowed[:border])
    back_on[...] = jnp.where(odd, d_borrowed[:border], d_borrowed[border:])
    d_node_o[...] = d_node
    d_centre_o[...] = d_centre
    d_neigh_o[...] = d_neigh[:rows]
    parts = (
        tn(moved, d_centre),
        tn(table, d_neigh),
        gmsg[:width, :width] + gmsg[width:, width:],
        tn(moved, d_node),
        tn(agg_b, d_node),
        tn(node_hid, cot),
    )
    for m, part in enumerate(parts):
        grads[m * width : (m + 1) * width] = part.astype(BF16)
    used = len(parts) * width
    if grads.shape[0] > used:
        grads[used:] = jnp.zeros_like(grads[used:])


def finish_kernel(
    cotangent, d_node, d_centre, d_neigh, w_self, w_send, w_recv, sends, got_off, got_on, out
):
    rows = d_node.shape[0]
    odd, _ = parities()
    from_low = jnp.where(odd, got_on[...], got_off[...])
    from_high = jnp.where(odd, got_off[...], got_on[...])
    returned = jnp.concatenate([from_low, from_high], axis=0)
    out[0] = (
        cotangent[0].astype(F32)
        + nt(d_node[...], w_self[...])
        + nt(d_centre[...], w_send[...])
        + nt(d_neigh[...], w_recv[...])
        + nn(hot_columns(sends[...], rows), returned)
    ).astype(BF16)


def sum_kernel(parts, out):
    total = jnp.sum(parts[...].astype(F32), axis=0).astype(BF16)
    out[...] = jnp.broadcast_to(total[None], out.shape)


def norm_kernel(total, steps):
    count, width = steps.shape[0], steps.shape[1]
    for m in range(count):
        part = total[m * width : (m + 1) * width].astype(F32)
        mean = jnp.sum(jnp.sum(part * part, axis=0, keepdims=True), axis=1, keepdims=True)
        mean = mean / (part.shape[0] * part.shape[1])
        steps[m] = part / jnp.sqrt(mean + 1e-06)


def call(kernel, outs, scratch=()):
    return pl.pallas_call(
        kernel,
        out_shape=[jax.ShapeDtypeStruct(shape, kind) for shape, kind in outs],
        scratch_shapes=scratch,
        compiler_params=pltpu.CompilerParams(vmem_limit_bytes=40 * 1024 * 1024),
        cost_estimate=pl.CostEstimate(flops=2 * 10**9, bytes_accessed=1024, transcendentals=0),
    )


def shards(
    nodes,
    leave_list,
    arrive_list,
    send_list,
    neighbours,
    valid,
    w_send,
    w_recv,
    w_msg,
    w_self,
    w_agg,
    w_out,
    cotangent,
):
    rows, width = nodes.shape[1:]
    slots = neighbours.shape[2]
    migr = leave_list.shape[1] // 2
    border = send_list.shape[1] // 2
    table_rows = rows + 2 * border
    size = lax.axis_size("slab")
    devices = size * lax.axis_size("grp")
    axes = ("grp", "slab")

    def swap(array, by):
        step = abs(by)
        pairs = [
            (i, (i + by if i // step % 2 == 0 else i - by) % size) for i in range(size)
        ]
        return lax.ppermute(array, "slab", pairs)

    message = (border + migr + CODE_ROWS, width)
    (token,) = call(first_kernel, [((8, LANES), F32)])()
    near_off, near_on, far_off, far_on = call(
        pack_kernel,
        [(message, BF16)] * 2 + [((migr, width), BF16)] * 2,
    )(token, nodes, leave_list, arrive_list, send_list)
    got_on = swap(near_on, 1)
    got_off = swap(near_off, -1)
    got_far_on = swap(far_on, 2)
    got_far_off = swap(far_off, -2)

    matrices = 6
    pair_rows = rows * slots // 2
    half_rows = table_rows // 2
    hot_rows = -(-(half_rows + 1) // LANES) * LANES
    share = -(-matrices * width // (8 * devices)) * 8
    edges = rows * slots
    hot, hot_t, upper, wide, ids, d_hid = call(
        prep_kernel,
        [
            ((edges, hot_rows), BF16),
            ((half_rows, edges), BF16),
            ((edges, width), BF16),
            ((2, 2 * width, 2 * width), BF16),
            ((rows, LANES), jnp.int32),
            ((rows, width), F32),
        ],
    )(jnp.swapaxes(neighbours, 1, 2), jnp.swapaxes(valid, 1, 2), w_msg, w_out, cotangent)
    sources = (
        nodes,
        arrive_list,
        far_off,
        far_on,
        got_off,
        got_on,
        got_far_off,
        got_far_on,
        hot,
        hot_t,
        upper,
        wide,
        ids,
        d_hid,
        w_send,
        w_recv,
        w_self,
        w_agg,
        w_out,
        cotangent,
    )
    updated, back_off, back_on, grads, d_node, d_centre, d_neigh = call(
        layer_kernel,
        [
            ((1, rows, width), BF16),
            ((border, width), BF16),
            ((border, width), BF16),
            ((devices * share, width), BF16),
            ((rows, width), BF16),
            ((rows, width), BF16),
            ((rows, width), BF16),
        ],
        [
            pltpu.VMEM((hot_rows, 2 * width), BF16),
            pltpu.VMEM((pair_rows, 2 * width), BF16),
            pltpu.VMEM((pair_rows, 2 * width), F32),
            pltpu.VMEM((pair_rows, 2 * width), F32),
            pltpu.VMEM((rows, width), F32),
            pltpu.VMEM((rows, width), F32),
            pltpu.VMEM((pair_rows, 2 * width), BF16),
            pltpu.VMEM((edges, 2 * width), BF16),
        ],
    )(*sources)
    got_on = swap(back_on, 1)
    got_off = swap(back_off, -1)
    parts = lax.all_to_all(
        grads.reshape(devices, share, width), axes, split_axis=0, concat_axis=0, tiled=True
    )
    sources = (
        cotangent,
        d_node,
        d_centre,
        d_neigh,
        w_self,
        w_send,
        w_recv,
        send_list,
        got_off,
        got_on,
    )
    (grad_nodes,) = call(
        finish_kernel,
        [((1, rows, width), BF16)],
    )(*sources)
    (shared,) = call(sum_kernel, [((devices, share, width), BF16)])(parts)
    total = lax.all_to_all(shared, axes, split_axis=0, concat_axis=0, tiled=True)
    total = total.reshape(devices * share, width)[: matrices * width]
    (weight_steps,) = call(norm_kernel, [((matrices, width, width), F32)])(total)
    return (updated, grad_nodes, weight_steps)


def solution(mesh):
    rows = P("grp", "slab", None)
    lists = P("grp", "slab")
    in_specs = (rows, lists, lists, lists, rows, rows, P(), P(), P(), P(), P(), P(), rows)
    out_specs = (rows, rows, P())
    return jax.shard_map(shards, mesh=mesh, in_specs=in_specs, out_specs=out_specs, check_vma=False)
```

```python
import functools

import jax
import jax.numpy as jnp
from jax import lax
from jax.experimental import pallas as pl
from jax.experimental.pallas import tpu as pltpu
from jax.sharding import PartitionSpec as P

F32 = jnp.float32
BF16 = jnp.bfloat16
CODE_ROWS = 16
LANES = 128
FAR = -1e30
GROUP = 16
BLOCK = 128


def nn(left, right):
    return lax.dot_general(left, right, (((1,), (0,)), ((), ())), preferred_element_type=F32)


def nt(left, right):
    return lax.dot_general(left, right, (((1,), (1,)), ((), ())), preferred_element_type=F32)


def tn(left, right):
    return lax.dot_general(left, right, (((0,), (0,)), ((), ())), preferred_element_type=F32)


def hot_columns(row, count):
    sub = lax.broadcasted_iota(jnp.int32, (count, row.shape[1]), 0)
    return jnp.where(sub == row, 1.0, 0.0).astype(BF16)


def silu_parts(half):
    tan = jnp.tanh(half)
    twice = 1.0 + tan
    act = half * twice
    return act, twice + act * (1.0 - tan)


def first_kernel(out):
    out[...] = jnp.zeros_like(out)


def parities():
    slab = lax.axis_index("slab")
    return lax.rem(slab, 2) == 1, lax.rem(slab // 2, 2) == 1


def pack_kernel(_, nodes, leave, arrive, sends, near_off, near_on, far_off, far_on):
    odd, odd_pair = parities()
    rows = nodes.shape[1]
    migr = leave.shape[1] // 2
    border = sends.shape[1] // 2
    own = nodes[0]
    leaving = tn(hot_columns(leave[...], rows), own).astype(BF16)
    sub = lax.broadcasted_iota(jnp.int32, (rows, 2 * border), 0)
    column = jnp.transpose(
        jnp.broadcast_to(arrive[...].astype(F32), (2 * border, rows)), (1, 0)
    )
    source = jnp.sum(jnp.where(sub == sends[...], column, 0.0), axis=0, keepdims=True)
    source = source.astype(jnp.int32)
    rest = tn(hot_columns(source, rows), own).astype(BF16)
    code = jnp.where(source >= rows, source - rows, -1).astype(F32)
    messages = []
    for part in range(2):
        shifted = code if part == 0 else pltpu.roll(code, border, 1)
        messages.append(
            jnp.concatenate(
                [
                    rest[part * border : (part + 1) * border],
                    leaving[part * migr : (part + 1) * migr],
                    jnp.broadcast_to(shifted, (CODE_ROWS, 2 * border)).astype(BF16),
                ],
                axis=0,
            )
        )
    down, up = messages
    near_off[...] = jnp.where(odd, up, down)
    near_on[...] = jnp.where(odd, down, up)
    down, up = leaving[:migr], leaving[migr:]
    far_off[...] = jnp.where(odd_pair, up, down)
    far_on[...] = jnp.where(odd_pair, down, up)


def prep_kernel(nbr, valid, w_msg, w_out, cotangent, hot_o, hot_t_o, up_o, wide_o, ids_o, d_hid_o):
    slots, rows = nbr.shape[1:]
    width = w_msg.shape[0]
    half_rows, hot_rows = hot_t_o.shape[0], hot_o.shape[1]
    chunk = 4
    half_msg = 0.5 * w_msg[...].astype(F32)
    none = jnp.zeros((width, width), F32)
    for part, block in enumerate((half_msg, jnp.transpose(half_msg, (1, 0)))):
        wide_o[part] = jnp.concatenate(
            [
                jnp.concatenate([block, none], axis=1),
                jnp.concatenate([none, block], axis=1),
            ],
            axis=0,
        ).astype(BF16)
    d_hid_o[...] = nt(cotangent[0], w_out[...])
    upper = nbr[0] >= half_rows
    low_row = jnp.where(upper, nbr[0] - half_rows, nbr[0])
    index = jnp.where(valid[0] == 1, low_row, half_rows) + jnp.where(upper, hot_rows, 0)
    fill = jnp.zeros((LANES - slots, rows), jnp.int32)
    ids_o[...] = jnp.transpose(jnp.concatenate([index, fill], axis=0), (1, 0))

    lane = lax.broadcasted_iota(jnp.int32, (rows, hot_rows), 1).astype(jnp.int16)
    one = jnp.ones((rows, hot_rows), BF16)
    zero = jnp.zeros((rows, hot_rows), BF16)
    sub = lax.broadcasted_iota(jnp.int32, (half_rows, rows), 0).astype(jnp.int16)
    one_t = jnp.ones((half_rows, rows), BF16)
    zero_t = jnp.zeros((half_rows, rows), BF16)

    border_id = jnp.full((rows, LANES), hot_rows, jnp.int16)

    @pl.loop(0, slots // chunk)
    def build(step):
        for j, short in enumerate(slot_ids(ids_o, step, chunk)):
            slot = step * chunk + j
            at_up = short.astype(jnp.int16) >= border_id
            up_o[pl.ds(slot * rows, rows)] = jnp.where(at_up, one[:, :LANES], zero[:, :LANES])
            short = (short & (hot_rows - 1)).astype(jnp.int16)
            short = jnp.concatenate([short] * (hot_rows // LANES), axis=1)
            hot_o[pl.ds(slot * rows, rows)] = jnp.where(short == lane, one, zero)
            row = nbr[0, pl.ds(slot, 1)]
            row = jnp.where(row >= half_rows, row - half_rows, row)
            short = jnp.broadcast_to(row, (16, rows)).astype(jnp.int16)
            short = jnp.concatenate([short] * (half_rows // 16), axis=0)
            hot_t_o[:, pl.ds(pl.multiple_of(slot * rows, LANES), rows)] = jnp.where(
                short == sub, one_t, zero_t
            )


def slot_ids(ids, step, chunk):
    near = pltpu.roll(ids[...], lax.rem(LANES - step * chunk, LANES), 1)
    shape = (ids.shape[0], LANES)
    return [jnp.broadcast_to(near[:, j : j + 1], shape) for j in range(chunk)]


def layer_kernel(
    nodes,
    arrive,
    my_far_off,
    my_far_on,
    got_off,
    got_on,
    got_far_off,
    got_far_on,
    hot,
    hot_t,
    upper,
    wide,
    nbr_ids,
    d_hid,
    w_send,
    w_recv,
    w_self,
    w_agg,
    w_out,
    cotangent,
    updated,
    back_off,
    back_on,
    grads,
    d_node_o,
    d_centre_o,
    d_neigh_o,
    neigh_s,
    hid_s,
    ds1_s,
    ds2_s,
    agg_s,
    dcen_s,
    dpre2_s,
    dpre_s,
):
    rows, width = nodes.shape[1:]
    slots = hot.shape[0] // rows
    border, migr = back_off.shape[0], got_far_off.shape[0]
    odd, odd_pair = parities()
    low = jnp.where(odd, got_on[...], got_off[...])
    high = jnp.where(odd, got_off[...], got_on[...])
    low_far = jnp.where(odd_pair, got_far_on[...], got_far_off[...])
    high_far = jnp.where(odd_pair, got_far_off[...], got_far_on[...])
    my_up = jnp.where(odd_pair, my_far_off[...], my_far_on[...])
    my_down = jnp.where(odd_pair, my_far_on[...], my_far_off[...])
    table_rows = rows + 2 * border

    pool = jnp.concatenate(
        [nodes[0], low[border : border + migr], high[border : border + migr]], axis=0
    )
    moved = tn(hot_columns(arrive[...], pool.shape[0]), pool).astype(BF16)

    def halo(message, first, second):
        code = message[border + migr : border + migr + 8].astype(F32)[:1]
        code = code.astype(jnp.int32)
        source = jnp.concatenate([first, second], axis=0)
        extra = tn(hot_columns(code, 2 * migr), source)
        return (message[:border].astype(F32) + extra[:border]).astype(BF16)

    below = halo(low, low_far, my_down)
    above = halo(high, my_up, high_far)
    table = jnp.concatenate([moved, below, above], axis=0)

    half_rows, hot_rows = hot_t.shape[0], hot.shape[1]
    half_centre = 0.5 * nn(moved, w_send[...])
    half_neigh = (0.5 * nn(table, w_recv[...]).astype(BF16).astype(F32)).astype(BF16)
    neigh_s[:half_rows] = jnp.concatenate([half_neigh[:half_rows], half_neigh[half_rows:]], axis=1)
    neigh_s[half_rows:] = jnp.full((hot_rows - half_rows, 2 * width), FAR, BF16)
    ids = slot_ids(nbr_ids, 0, slots)
    blocks = [slice(start, start + BLOCK) for start in range(0, rows, BLOCK)]
    sides = (slice(0, width), slice(width, 2 * width))

    firsts = range(0, slots, GROUP)
    group_rows = GROUP // 2 * rows

    def first_half(first, gathered):
        for j in range(GROUP):
            pair, side = divmod(first + j, 2)
            for block in blocks:
                pick = gathered[j * rows + block.start : j * rows + block.stop]
                pick = jnp.where(
                    ids[first + j][block] >= hot_rows, pick[:, sides[1]], pick[:, sides[0]]
                )
                act, slope = silu_parts(half_centre[block] + pick)
                at = slice(pair * rows + block.start, pair * rows + block.stop)
                ds1_s[at, sides[side]] = slope
                hid_s[at, sides[side]] = act.astype(BF16)

    def second_half(first, halves):
        base = first // 2 * rows
        for block in blocks:
            total = jnp.zeros((BLOCK, width), F32) if first == 0 else agg_s[block]
            for j in range(GROUP):
                pair, side = divmod(j, 2)
                at = slice(pair * rows + block.start, pair * rows + block.stop)
                act, slope = silu_parts(halves[at, sides[side]])
                total = total + act
                ds2_s[base + at.start : base + at.stop, sides[side]] = slope
            agg_s[block] = total

    def staggered(matmul, arithmetic):
        ready = matmul(firsts[0])
        for first, after in zip(firsts, [*firsts[1:], None]):
            held, ready = ready, None if after is None else matmul(after)
            arithmetic(first, held)

    staggered(lambda first: nn(hot[first * rows : (first + GROUP) * rows], neigh_s[...]), first_half)
    staggered(
        lambda first: nn(hid_s[first // 2 * rows : first // 2 * rows + group_rows], wide[0]),
        second_half,
    )

    agg_b = agg_s[...].astype(BF16)
    node_pre = nn(moved, w_self[...]) + nn(agg_b, w_agg[...])
    act, slope = silu_parts(0.5 * node_pre)
    node_hid = act.astype(BF16)
    updated[0] = (moved.astype(F32) + nn(node_hid, w_out[...])).astype(BF16)
    cot = cotangent[0]
    d_node = (d_hid[...] * (0.5 * slope)).astype(BF16)
    half_d_agg = 0.5 * nt(d_node, w_agg[...])

    def message_slope(first):
        base = first // 2 * rows
        for pair in range(GROUP // 2):
            for block in blocks:
                at = slice(base + pair * rows + block.start, base + pair * rows + block.stop)
                for side in sides:
                    dpre2_s[at, side] = (half_d_agg[block] * ds2_s[at, side]).astype(BF16)
        return nn(dpre2_s[base : base + group_rows], wide[1])

    def edge_slope(first, d_hids):
        base = first // 2 * rows
        for block in blocks:
            total = jnp.zeros((BLOCK, width), F32) if first == 0 else dcen_s[block]
            for j in range(GROUP):
                pair, side = divmod(j, 2)
                at = slice(pair * rows + block.start, pair * rows + block.stop)
                part = d_hids[at, sides[side]] * ds1_s[base + at.start : base + at.stop, sides[side]]
                total = total + part
                part = part.astype(BF16)
                at = slice((first + j) * rows + block.start, (first + j) * rows + block.stop)
                part_up = part * upper[at]
                dpre_s[at, sides[0]] = part - part_up
                dpre_s[at, sides[1]] = part_up
            dcen_s[block] = total

    staggered(message_slope, edge_slope)
    gmsg = tn(hid_s[...], dpre2_s[...])
    d_neigh = nn(hot_t[...], dpre_s[...]).astype(BF16)

    d_centre = dcen_s[...].astype(BF16)
    d_neigh = jnp.concatenate([d_neigh[:, :width], d_neigh[:, width:]], axis=0)
    d_borrowed = nt(d_neigh[rows:], w_recv[...]).astype(BF16)
    back_off[...] = jnp.where(odd, d_borrowed[border:], d_borrowed[:border])
    back_on[...] = jnp.where(odd, d_borrowed[:border], d_borrowed[border:])
    d_node_o[...] = d_node
    d_centre_o[...] = d_centre
    d_neigh_o[...] = d_neigh[:rows]
    parts = (
        tn(moved, d_centre),
        tn(table, d_neigh),
        gmsg[:width, :width] + gmsg[width:, width:],
        tn(moved, d_node),
        tn(agg_b, d_node),
        tn(node_hid, cot),
    )
    for m, part in enumerate(parts):
        grads[m * width : (m + 1) * width] = part.astype(BF16)
    used = len(parts) * width
    if grads.shape[0] > used:
        grads[used:] = jnp.zeros_like(grads[used:])


def finish_kernel(
    cotangent, d_node, d_centre, d_neigh, w_self, w_send, w_recv, sends, got_off, got_on, out
):
    rows = d_node.shape[0]
    odd, _ = parities()
    from_low = jnp.where(odd, got_on[...], got_off[...])
    from_high = jnp.where(odd, got_off[...], got_on[...])
    returned = jnp.concatenate([from_low, from_high], axis=0)
    out[0] = (
        cotangent[0].astype(F32)
        + nt(d_node[...], w_self[...])
        + nt(d_centre[...], w_send[...])
        + nt(d_neigh[...], w_recv[...])
        + nn(hot_columns(sends[...], rows), returned)
    ).astype(BF16)


def sum_kernel(parts, out):
    total = jnp.sum(parts[...].astype(F32), axis=0).astype(BF16)
    out[...] = jnp.broadcast_to(total[None], out.shape)


def norm_kernel(total, steps):
    count, width = steps.shape[0], steps.shape[1]
    for m in range(count):
        part = total[m * width : (m + 1) * width].astype(F32)
        mean = jnp.sum(jnp.sum(part * part, axis=0, keepdims=True), axis=1, keepdims=True)
        mean = mean / (part.shape[0] * part.shape[1])
        steps[m] = part * (1.0 / jnp.sqrt(mean + 1e-06))


def call(kernel, outs, scratch=()):
    return pl.pallas_call(
        kernel,
        out_shape=[jax.ShapeDtypeStruct(shape, kind) for shape, kind in outs],
        scratch_shapes=scratch,
        compiler_params=pltpu.CompilerParams(vmem_limit_bytes=40 * 1024 * 1024),
        cost_estimate=pl.CostEstimate(flops=2 * 10**9, bytes_accessed=1024, transcendentals=0),
    )


def shards(
    nodes,
    leave_list,
    arrive_list,
    send_list,
    neighbours,
    valid,
    w_send,
    w_recv,
    w_msg,
    w_self,
    w_agg,
    w_out,
    cotangent,
):
    rows, width = nodes.shape[1:]
    slots = neighbours.shape[2]
    migr = leave_list.shape[1] // 2
    border = send_list.shape[1] // 2
    table_rows = rows + 2 * border
    size = lax.axis_size("slab")
    devices = size * lax.axis_size("grp")
    axes = ("grp", "slab")

    def swap(array, by):
        step = abs(by)
        pairs = [
            (i, (i + by if i // step % 2 == 0 else i - by) % size) for i in range(size)
        ]
        return lax.ppermute(array, "slab", pairs)

    message = (border + migr + CODE_ROWS, width)
    (token,) = call(first_kernel, [((8, LANES), F32)])()
    near_off, near_on, far_off, far_on = call(
        pack_kernel,
        [(message, BF16)] * 2 + [((migr, width), BF16)] * 2,
    )(token, nodes, leave_list, arrive_list, send_list)
    got_on = swap(near_on, 1)
    got_off = swap(near_off, -1)
    got_far_on = swap(far_on, 2)
    got_far_off = swap(far_off, -2)

    matrices = 6
    pair_rows = rows * slots // 2
    half_rows = table_rows // 2
    hot_rows = -(-(half_rows + 1) // LANES) * LANES
    share = -(-matrices * width // (8 * devices)) * 8
    edges = rows * slots
    hot, hot_t, upper, wide, ids, d_hid = call(
        prep_kernel,
        [
            ((edges, hot_rows), BF16),
            ((half_rows, edges), BF16),
            ((edges, width), BF16),
            ((2, 2 * width, 2 * width), BF16),
            ((rows, LANES), jnp.int32),
            ((rows, width), F32),
        ],
    )(jnp.swapaxes(neighbours, 1, 2), jnp.swapaxes(valid, 1, 2), w_msg, w_out, cotangent)
    sources = (
        nodes,
        arrive_list,
        far_off,
        far_on,
        got_off,
        got_on,
        got_far_off,
        got_far_on,
        hot,
        hot_t,
        upper,
        wide,
        ids,
        d_hid,
        w_send,
        w_recv,
        w_self,
        w_agg,
        w_out,
        cotangent,
    )
    updated, back_off, back_on, grads, d_node, d_centre, d_neigh = call(
        layer_kernel,
        [
            ((1, rows, width), BF16),
            ((border, width), BF16),
            ((border, width), BF16),
            ((devices * share, width), BF16),
            ((rows, width), BF16),
            ((rows, width), BF16),
            ((rows, width), BF16),
        ],
        [
            pltpu.VMEM((hot_rows, 2 * width), BF16),
            pltpu.VMEM((pair_rows, 2 * width), BF16),
            pltpu.VMEM((pair_rows, 2 * width), F32),
            pltpu.VMEM((pair_rows, 2 * width), F32),
            pltpu.VMEM((rows, width), F32),
            pltpu.VMEM((rows, width), F32),
            pltpu.VMEM((pair_rows, 2 * width), BF16),
            pltpu.VMEM((edges, 2 * width), BF16),
        ],
    )(*sources)
    got_on = swap(back_on, 1)
    got_off = swap(back_off, -1)
    parts = lax.all_to_all(
        grads.reshape(devices, share, width), axes, split_axis=0, concat_axis=0, tiled=True
    )
    sources = (
        cotangent,
        d_node,
        d_centre,
        d_neigh,
        w_self,
        w_send,
        w_recv,
        send_list,
        got_off,
        got_on,
    )
    (grad_nodes,) = call(
        finish_kernel,
        [((1, rows, width), BF16)],
    )(*sources)
    (shared,) = call(sum_kernel, [((devices, share, width), BF16)])(parts)
    total = lax.all_to_all(shared, axes, split_axis=0, concat_axis=0, tiled=True)
    total = total.reshape(devices * share, width)[: matrices * width]
    (weight_steps,) = call(norm_kernel, [((matrices, width, width), F32)])(total)
    return (updated, grad_nodes, weight_steps)


def solution(mesh):
    rows = P("grp", "slab", None)
    lists = P("grp", "slab")
    in_specs = (rows, lists, lists, lists, rows, rows, P(), P(), P(), P(), P(), P(), rows)
    out_specs = (rows, rows, P())
    return jax.shard_map(shards, mesh=mesh, in_specs=in_specs, out_specs=out_specs, check_vma=False)
```
